256 devices in a mesh: ty: 16 (over z_hi, y, core), tx: 16 (over x, z_lo).
Axes of the slice: x: 4, y: 4, z: 8 (z_hi: 2, z_lo: 4; z = z_hi * 4 + z_lo), core: 2. Of those that a mesh axis runs over, the one named last changes fastest.
Arguments:
- object_field: float32 [2, 8192, 8192], P(None, 'ty', 'tx'), may hold values from -5 to 5
- probe: float32 [2, 256, 256], replicated, may hold values from -5 to 5
- intensity: float32 [16, 16, 8, 256, 256], P('ty', 'tx'), may hold values from 0.05 to 4
- positions: int32 [2, 16, 16, 8], P(None, 'ty', 'tx'), may hold values from -128 to 384
- counts: int32 [16, 16], P('ty', 'tx'), may hold values from 1 to 8, as said below
Outputs:
- object_new: float32 [2, 8192, 8192], P(None, 'ty', 'tx')
- probe_new: float32 [2, 256, 256], replicated
The draws below stay inside these ranges and needn't reach their ends.
Inputs may be any that keep to these rules, and one draw needn't show every extreme that they name: counts are skewed over tiles; some tile has 8.
All inputs are finite; a program needn't handle non-finite values.
Results may differ from the reference program's by a relative error of at most 0.00013.
Values sent between devices are 32-bit elements; how exact they have to be, the bound alone decides.
No kernel may reach another device: no remote copies, remote signals or barrier semaphores. Data moves between devices by JAX's collectives and lax.ppermute only.
A program may use at most 128 MiB of HBM per device.

```python
import math
import jax
import jax.numpy as jnp
from jax import lax

TILE = 512
PATCH = 256
HALF = 128
CAP = 8
NY = 8192
NX = 8192
N_TY = 16
N_TX = 16


def draw_counts(key, part):
    key = jax.random.fold_in(key, 11)
    first, second, third = jax.random.split(key, 3)
    lower = jax.random.randint(first, (N_TY, N_TX), 1, CAP + 1)
    upper = jax.random.randint(second, (N_TY, N_TX), 1, CAP + 1)
    spot = jax.random.randint(third, (), 0, N_TY * N_TX)
    merged = jnp.minimum(lower, upper).reshape(-1)
    merged = jnp.where(jnp.arange(N_TY * N_TX) == spot, CAP, merged)
    return merged.reshape(N_TY, N_TX).astype(jnp.int32)


def place_ends(entries, key, smallest, largest):
    dims = entries.shape
    spot = [jax.random.randint(jax.random.fold_in(key, axis), (), 0, dims[axis]) for axis in range(len(dims))]
    entries = entries.at[tuple(spot)].set(smallest)
    longest = dims.index(max(dims))
    spot[longest] = (spot[longest] + 1) % dims[longest]
    return entries.at[tuple(spot)].set(largest)


def steps_of(key, dims, shards, low, largest):
    level, own = 1.0, jax.random.fold_in(key, 6)
    for position, shards_of in shards:
        steps = jnp.exp(jax.random.uniform(jax.random.fold_in(own, position), (shards_of,), jnp.float32, low / len(shards), largest / len(shards)))
        level = level * jnp.repeat(steps, dims[position] // shards_of).reshape([-1 if axis == position else 1 for axis in range(len(dims))])
    return level


def bell_draw(key, extent, deviation, reach, cuts=(), held_as=jnp.bfloat16):
    loudness = steps_of(key, extent, cuts, -0.22, 0.18) if cuts else 1.0
    drawn = jax.random.normal(key, extent, jnp.float32) * deviation * loudness
    return jnp.minimum(jnp.maximum(drawn, -reach), reach).astype(held_as)


def setup_inputs(seed: int = 0) -> dict:
    seeds = jax.random.split(jax.random.key(seed), 6)
    object_field = bell_draw(seeds[0], (2, NY, NX), 0.7, 5.0, ((1, 16), (2, 16)), jnp.float32)
    probe = bell_draw(seeds[1], (2, PATCH, PATCH), 1.0, 5.0, (), jnp.float32)
    intensity = jnp.clip(jnp.exp(math.log(4.0) - 4.3820266 * jax.random.uniform(seeds[2], (N_TY, N_TX, CAP, PATCH, PATCH), jnp.float32) ** steps_of(seeds[2], (N_TY, N_TX, CAP, PATCH, PATCH), ((0, 16), (1, 16)), -0.2, 0.2)), 0.05, 4.0)
    positions = place_ends(jax.random.randint(seeds[3], (2, N_TY, N_TX, CAP), -HALF, TILE - HALF + 1), jax.random.fold_in(seeds[3], 1), -HALF, TILE - HALF).astype(jnp.int32)
    counts = draw_counts(jax.random.fold_in(seeds[5], 71), 0)
    return {"object_field": object_field, "probe": probe, "intensity": intensity, "positions": positions, "counts": counts}


def dft_tables(size):
    index = jnp.arange(size, dtype=jnp.int32)
    product = index[:, None] * index[None, :] % size
    angle = product.astype(jnp.float32) * (2.0 * jnp.pi / size)
    scale = 1.0 / jnp.sqrt(jnp.float32(size))
    return (jnp.cos(angle) * scale, -jnp.sin(angle) * scale)

def matmul(left, right):
    return jnp.dot(left, right, precision=lax.Precision.HIGHEST, preferred_element_type=jnp.float32)

def transform(real, imag, table_re, table_im):
    first_re = matmul(table_re, real) - matmul(table_im, imag)
    first_im = matmul(table_re, imag) + matmul(table_im, real)
    out_re = matmul(first_re, table_re) - matmul(first_im, table_im)
    out_im = matmul(first_re, table_im) + matmul(first_im, table_re)
    return (out_re, out_im)

def slot_terms(patch_re, patch_im, probe_re, probe_im, measured, table_re, table_im):
    exit_re = probe_re * patch_re - probe_im * patch_im
    exit_im = probe_re * patch_im + probe_im * patch_re
    wave_re, wave_im = transform(exit_re, exit_im, table_re, table_im)
    excess = wave_re * wave_re + wave_im * wave_im - measured
    chi_re, chi_im = transform(excess * wave_re, excess * wave_im, table_re, -table_im)
    obj_re = probe_re * chi_re + probe_im * chi_im
    obj_im = probe_re * chi_im - probe_im * chi_re
    obj_wt = probe_re * probe_re + probe_im * probe_im
    prb_re = patch_re * chi_re + patch_im * chi_im
    prb_im = patch_re * chi_im - patch_im * chi_re
    prb_wt = patch_re * patch_re + patch_im * patch_im
    return (jnp.stack([obj_re, obj_im, obj_wt]), jnp.stack([prb_re, prb_im, prb_wt]))

def reference(object_field, probe, intensity, positions, counts):
    table_re, table_im = dft_tables(PATCH)
    padded = jnp.pad(object_field, ((0, 0), (HALF, HALF), (HALF, HALF)))
    tile_rows = jnp.arange(N_TY, dtype=jnp.int32)[:, None, None] * TILE
    tile_cols = jnp.arange(N_TX, dtype=jnp.int32)[None, :, None] * TILE
    row_at = (tile_rows + positions[0] + HALF).reshape(-1).astype(jnp.int32)
    col_at = (tile_cols + positions[1] + HALF).reshape(-1).astype(jnp.int32)
    slot_ids = jnp.arange(CAP, dtype=jnp.int32)[None, None, :]
    live = (slot_ids < counts[:, :, None]).astype(jnp.float32).reshape(-1)
    measured_all = intensity.reshape(N_TY * N_TX * CAP, PATCH, PATCH)
    canvas = jnp.zeros((3, NY + PATCH, NX + PATCH), jnp.float32)
    probe_acc = jnp.zeros((3, PATCH, PATCH), jnp.float32)

    def step(carry, item):
        grid, acc = carry
        row_pos, col_pos, weight, measured = item
        zero = jnp.zeros((), jnp.int32)
        patch = lax.dynamic_slice(padded, (zero, row_pos, col_pos), (2, PATCH, PATCH))
        obj_terms, prb_terms = slot_terms(patch[0], patch[1], probe[0], probe[1], measured, table_re, table_im)
        old = lax.dynamic_slice(grid, (zero, row_pos, col_pos), (3, PATCH, PATCH))
        grid = lax.dynamic_update_slice(grid, old + weight * obj_terms, (zero, row_pos, col_pos))
        return ((grid, acc + weight * prb_terms), None)
    (canvas, probe_acc), _ = lax.scan(step, (canvas, probe_acc), (row_at, col_at, live, measured_all))
    inner = canvas[:, HALF:HALF + NY, HALF:HALF + NX]
    object_new = object_field - inner[:2] / (inner[2] + 1.0)
    probe_new = probe - probe_acc[:2] / jnp.sqrt(probe_acc[2] + 1.0)
    return (object_new, probe_new)
```

```python
import numpy as np
import ml_dtypes
import jax
import jax.numpy as jnp
from jax import lax
from jax.experimental import pallas as pl
from jax.experimental.pallas import tpu as pltpu
from jax.sharding import PartitionSpec as P

BF16 = jnp.bfloat16
F32 = jnp.float32
LANES = 128
VMEM = pl.BlockSpec(memory_space=pltpu.VMEM)
SMEM = pl.BlockSpec(memory_space=pltpu.SMEM)
ANY = pl.BlockSpec(memory_space=pl.ANY)
AROUND = ((-1, 0), (1, 0), (0, -1), (0, 1), (-1, -1), (-1, 1), (1, -1), (1, 1))


def split_host(table):
    high = table.astype(ml_dtypes.bfloat16)
    low = (table - high.astype(np.float64)).astype(ml_dtypes.bfloat16)
    return high, low


def half_tables(size):
    half = size // 2
    left, right = [], []
    for parity in range(2):
        product = (2 * np.arange(half)[:, None] + parity) * np.arange(half)[None, :] % size
        angle = 2.0 * np.pi * product / size
        cos, sin = np.cos(angle) / np.sqrt(size), np.sin(angle) / np.sqrt(size)
        base = np.block([[cos, sin], [-sin, cos]])
        for table in (base, base.T):
            high, low = split_host(table)
            left.append(np.concatenate([high, high, low], axis=1))
            right.append(np.concatenate([high, high, low], axis=0))
    return np.stack(left), np.stack(right)


def parity_tables(size):
    order = np.concatenate([np.arange(0, size, 2), np.arange(1, size, 2)])
    gather = np.eye(size)[order].astype(ml_dtypes.bfloat16)
    return np.concatenate([gather] * 3, axis=1), np.concatenate([gather.T] * 3, axis=0)


def matmul(left, right):
    return jnp.dot(left, right, preferred_element_type=F32)


def split(value):
    high = value.astype(BF16)
    return high, (value - high.astype(F32)).astype(BF16)


def put_rows(ref, start, columns, value):
    rows = value.shape[0]
    high, low = split(value)
    third = ref.shape[0] // 3
    ref[start : start + rows, columns] = high
    ref[third + start : third + start + rows, columns] = low
    ref[2 * third + start : 2 * third + start + rows, columns] = high


def put_columns(ref, rows, start, value):
    width = value.shape[1]
    high, low = split(value)
    third = ref.shape[1] // 3
    ref[rows, start : start + width] = high
    ref[rows, third + start : third + start + width] = low
    ref[rows, 2 * third + start : 2 * third + start + width] = high


def place(position, slot, half):
    row = position[0, slot] + half
    col = position[1, slot] + half
    tile = jnp.minimum(lax.shift_right_logical(col, 7), 3)
    return row, tile, col - tile * LANES


def add_window(accumulate, row, tile, offset, first, second):
    rows = first.shape[0]
    turn = jnp.bitwise_and(offset, LANES - 1)
    kept = lax.broadcasted_iota(jnp.int32, first.shape, 1) >= offset
    first = pltpu.roll(first, turn, 1)
    second = pltpu.roll(second, turn, 1)
    where = pl.ds(row, rows)
    accumulate[tile, where, :] += jnp.where(kept, first, 0.0)
    accumulate[tile + 1, where, :] += jnp.where(kept, second, first)
    accumulate[tile + 2, where, :] += jnp.where(kept, 0.0, second)


def early_kernel(position, count, probe, measured, gather_left, gather_right, folded, weight, parts):
    size = probe.shape[1]
    half = size // 2
    weight[...] = jnp.zeros_like(weight)

    def step(slot, carry):
        row, tile, offset = place(position, slot, half)
        pieces = []
        for start in (0, LANES):
            columns = slice(start, start + LANES)
            pieces.append(probe[0, :, columns] * probe[0, :, columns] + probe[1, :, columns] * probe[1, :, columns])
        add_window(weight, row, tile, offset, *pieces)

        def three(value):
            high = value.astype(BF16)
            rest = value - high.astype(F32)
            middle = rest.astype(BF16)
            return high, middle, (rest - middle.astype(F32)).astype(BF16)

        for index, part in enumerate(three(measured[slot])):
            parts[:, index * size : (index + 1) * size] = part
        value = matmul(parts[...], gather_right[...])
        value = jnp.concatenate(three(value), axis=0)
        folded[slot] = matmul(gather_left[...], value)
        return carry

    lax.fori_loop(0, count[0], step, 0)


def slot_kernel(
    position, count, probe, folded, left, right, tile_ref, top, bottom, low, high, top_low, top_high, bottom_low,
    bottom_high, grad, probe_sum, canvas, patch, rhs, lhs, sems,
):
    size = probe.shape[1]
    half = size // 2
    side = tile_ref.shape[1]
    tiles = side // LANES
    inner = slice(half, half + side)
    copies = []

    def fetch(source, target):
        copy = pltpu.make_async_copy(source, target, sems.at[len(copies)])
        copy.start()
        copies.append(copy)

    for index in range(tiles):
        columns = slice(index * LANES, (index + 1) * LANES)
        fetch(tile_ref.at[:, :, columns], canvas.at[:, 1 + index, inner, :])
        fetch(top.at[:, :, columns], canvas.at[:, 1 + index, :half, :])
        fetch(bottom.at[:, :, columns], canvas.at[:, 1 + index, half + side :, :])
    fetch(low, canvas.at[:, 0, inner, :])
    fetch(high, canvas.at[:, 1 + tiles, inner, :])
    fetch(top_low, canvas.at[:, 0, :half, :])
    fetch(top_high, canvas.at[:, 1 + tiles, :half, :])
    fetch(bottom_low, canvas.at[:, 0, half + side :, :])
    fetch(bottom_high, canvas.at[:, 1 + tiles, half + side :, :])
    grad[...] = jnp.zeros_like(grad)
    probe_sum[...] = jnp.zeros_like(probe_sum)
    for copy in copies:
        copy.wait()
    near, far = slice(0, half), slice(half, size)

    def step(slot, carry):
        row, tile, offset = place(position, slot, half)
        turn = jnp.bitwise_and(LANES - offset, LANES - 1)
        kept = lax.broadcasted_iota(jnp.int32, (size, LANES), 1) < LANES - offset
        for plane in range(2):
            raw = [pltpu.roll(canvas[plane, tile + index, pl.ds(row, size), :], turn, 1) for index in range(3)]
            patch[plane, :, near] = jnp.where(kept, raw[0], raw[1])
            patch[plane, :, far] = jnp.where(kept, raw[1], raw[2])
        for columns in (near, far):
            probe_re, probe_im = probe[0, :, columns], probe[1, :, columns]
            patch_re, patch_im = patch[0, :, columns], patch[1, :, columns]
            exit_re = probe_re * patch_re - probe_im * patch_im
            exit_im = probe_re * patch_im + probe_im * patch_re
            probe_sum[2, :, columns] += patch_re * patch_re + patch_im * patch_im
            put_rows(rhs.at[0], 0, columns, exit_re[:half] + exit_re[half:])
            put_rows(rhs.at[0], half, columns, exit_im[:half] + exit_im[half:])
            put_rows(rhs.at[1], 0, columns, exit_re[:half] - exit_re[half:])
            put_rows(rhs.at[1], half, columns, exit_im[:half] - exit_im[half:])
        for parity in range(2):
            value = matmul(left[2 * parity], rhs[parity])
            rows = slice(parity * half, (parity + 1) * half)
            put_columns(lhs.at[0], rows, 0, value[:half, near] + value[:half, far])
            put_columns(lhs.at[0], rows, half, value[half:, near] + value[half:, far])
            put_columns(lhs.at[1], rows, 0, value[:half, near] - value[:half, far])
            put_columns(lhs.at[1], rows, half, value[half:, near] - value[half:, far])
        everything = slice(0, size)
        back = []
        for parity in range(2):
            value = matmul(lhs[parity], right[2 * parity + 1])
            wave_re, wave_im = value[:, near], value[:, far]
            columns = slice(parity * half, (parity + 1) * half)
            excess = wave_re * wave_re + wave_im * wave_im - folded[slot, :, columns]
            put_columns(lhs.at[parity], everything, 0, excess * wave_re)
            put_columns(lhs.at[parity], everything, half, excess * wave_im)
            back.append(matmul(lhs[parity], right[2 * parity]))
        for parity in range(2):
            rows = slice(parity * half, (parity + 1) * half)
            put_rows(rhs.at[parity], 0, near, back[0][rows, near] + back[1][rows, near])
            put_rows(rhs.at[parity], half, near, back[0][rows, far] + back[1][rows, far])
            put_rows(rhs.at[parity], 0, far, back[0][rows, near] - back[1][rows, near])
            put_rows(rhs.at[parity], half, far, back[0][rows, far] - back[1][rows, far])
        even = matmul(left[1], rhs[0])
        odd = matmul(left[3], rhs[1])
        pieces = []
        for columns in (near, far):
            chi_re = jnp.concatenate([even[:half, columns] + odd[:half, columns], even[:half, columns] - odd[:half, columns]], axis=0)
            chi_im = jnp.concatenate([even[half:, columns] + odd[half:, columns], even[half:, columns] - odd[half:, columns]], axis=0)
            probe_re, probe_im = probe[0, :, columns], probe[1, :, columns]
            patch_re, patch_im = patch[0, :, columns], patch[1, :, columns]
            probe_sum[0, :, columns] += patch_re * chi_re + patch_im * chi_im
            probe_sum[1, :, columns] += patch_re * chi_im - patch_im * chi_re
            pieces.append((probe_re * chi_re + probe_im * chi_im, probe_re * chi_im - probe_im * chi_re))
        for plane in range(2):
            add_window(grad.at[plane], row, tile, offset, pieces[0][plane], pieces[1][plane])
        return carry

    lax.fori_loop(0, count[0], step, 0)


def final_kernel(tile_ref, grad, weight, *refs):
    grads, weights, out = refs[:8], refs[8:16], refs[16]
    half = LANES
    tiles = tile_ref.shape[2] // LANES
    side = tile_ref.shape[1]
    for index in range(tiles):
        columns = slice(index * LANES, (index + 1) * LANES)
        for start in range(0, side, half):
            rows = slice(start, start + half)
            inner = slice(half + start, 2 * half + start)

            def total(planes, pieces, own):
                value = own
                side_rows = rows
                if start == 0:
                    value = value + pieces[0][planes, index]
                if start + half == side:
                    value = value + pieces[1][planes, index]
                if index == 0:
                    value = value + pieces[2][planes, side_rows, :]
                if index == tiles - 1:
                    value = value + pieces[3][planes, side_rows, :]
                for corner, (first_row, first_col) in enumerate(((True, True), (True, False), (False, True), (False, False))):
                    if start == (0 if first_row else side - half) and index == (0 if first_col else tiles - 1):
                        value = value + pieces[4 + corner][planes]
                return value

            scale = 1.0 / (total(0, weights, weight[0, index + 1, inner, :]) + 1.0)
            for plane in range(2):
                value = total(plane, grads, grad[plane, index + 1, inner, :])
                out[plane, rows, columns] = tile_ref[plane, rows, columns] - value * scale


def to_neighbour(value, step, shape):
    rows, cols = shape
    down, across = step
    pairs = [
        (row * cols + col, (row + down) * cols + col + across)
        for row in range(rows)
        for col in range(cols)
        if 0 <= row + down < rows and 0 <= col + across < cols
    ]
    return lax.ppermute(value, ("ty", "tx"), pairs)


def edges_of_tile(value, half):
    pick = {-1: slice(0, half), 0: slice(None), 1: slice(-half, None)}
    return [value[:, pick[down], pick[across]] for down, across in AROUND]


def margins_of_grid(grid, half):
    side = grid.shape[2] - 2 * half
    rows = {-1: slice(0, half), 0: slice(half, half + side), 1: slice(half + side, None)}
    out = []
    for down, across in AROUND:
        if across == 0:
            out.append(grid[:, 1:-1, rows[down], :])
        else:
            out.append(grid[:, 0 if across < 0 else -1, rows[down], :])
    return out


def exchange(pieces, shape):
    arrived = [to_neighbour(piece, step, shape) for piece, step in zip(pieces, AROUND)]
    order = [AROUND.index((-down, -across)) for down, across in AROUND]
    return [arrived[index] for index in order]


def solution(mesh):
    shape = (mesh.shape["ty"], mesh.shape["tx"])

    def per_device(object_field, probe, intensity, positions, counts):
        side = object_field.shape[1]
        size = probe.shape[1]
        half = size // 2
        slots = intensity.shape[2]
        tiles = side // LANES
        position = positions[:, 0, 0, :]
        count = counts[0]
        left, right = half_tables(size)
        gather_left, gather_right = parity_tables(size)
        halo = exchange(edges_of_tile(object_field, half), shape)
        folded, weight = pl.pallas_call(
            early_kernel,
            out_shape=(
                jax.ShapeDtypeStruct((slots, size, size), F32),
                jax.ShapeDtypeStruct((tiles + 2, side + size, LANES), F32),
            ),
            in_specs=[SMEM, SMEM, VMEM, VMEM, VMEM, VMEM],
            out_specs=(VMEM, VMEM),
            scratch_shapes=[pltpu.VMEM((size, 3 * size), BF16)],
            compiler_params=pltpu.CompilerParams(vmem_limit_bytes=24 * 2**20),
            name="early",
        )(position, count, probe, intensity[0, 0], jnp.asarray(gather_left), jnp.asarray(gather_right))
        weight = weight[None]
        weights = exchange(margins_of_grid(weight, half), shape)
        grad, probe_sum = pl.pallas_call(
            slot_kernel,
            out_shape=(
                jax.ShapeDtypeStruct((2, tiles + 2, side + size, LANES), F32),
                jax.ShapeDtypeStruct((3, size, size), F32),
            ),
            in_specs=[SMEM, SMEM, VMEM, VMEM, VMEM, VMEM] + [ANY] * 9,
            out_specs=(VMEM, VMEM),
            scratch_shapes=[
                pltpu.VMEM((2, tiles + 2, side + size, LANES), F32),
                pltpu.VMEM((2, size, size), F32),
                pltpu.VMEM((2, 3 * size, size), BF16),
                pltpu.VMEM((2, size, 3 * size), BF16),
                pltpu.SemaphoreType.DMA((3 * tiles + 6,)),
            ],
            compiler_params=pltpu.CompilerParams(vmem_limit_bytes=48 * 2**20),
            name="slots",
        )(position, count, probe, folded, jnp.asarray(left), jnp.asarray(right), object_field, *halo)
        totals = lax.psum(probe_sum, ("ty", "tx"))
        grads = exchange(margins_of_grid(grad, half), shape)
        object_new = pl.pallas_call(
            final_kernel,
            out_shape=jax.ShapeDtypeStruct(object_field.shape, F32),
            in_specs=[VMEM] * 19,
            out_specs=VMEM,
            compiler_params=pltpu.CompilerParams(vmem_limit_bytes=48 * 2**20),
            name="final",
        )(object_field, grad, weight, *grads, *weights)
        probe_new = probe - totals[:2] / jnp.sqrt(totals[2] + 1.0)
        return (object_new, probe_new)

    in_specs = (
        P(None, "ty", "tx"),
        P(),
        P("ty", "tx", None, None, None),
        P(None, "ty", "tx", None),
        P("ty", "tx"),
    )
    out_specs = (P(None, "ty", "tx"), P())
    return jax.shard_map(per_device, mesh=mesh, in_specs=in_specs, out_specs=out_specs, check_vma=False)
```

```python
import numpy as np
import ml_dtypes
import jax
import jax.numpy as jnp
from jax import lax
from jax.experimental import pallas as pl
from jax.experimental.pallas import tpu as pltpu
from jax.sharding import PartitionSpec as P

BF16 = jnp.bfloat16
F32 = jnp.float32
LANES = 128
VMEM = pl.BlockSpec(memory_space=pltpu.VMEM)
SMEM = pl.BlockSpec(memory_space=pltpu.SMEM)
ANY = pl.BlockSpec(memory_space=pl.ANY)
def split_host(table):
    high = table.astype(ml_dtypes.bfloat16)
    low = (table - high.astype(np.float64)).astype(ml_dtypes.bfloat16)
    return high, low


def half_tables(size):
    half = size // 2
    left, right = [], []
    for parity in range(2):
        product = (2 * np.arange(half)[:, None] + parity) * np.arange(half)[None, :] % size
        angle = 2.0 * np.pi * product / size
        cos, sin = np.cos(angle) / np.sqrt(size), np.sin(angle) / np.sqrt(size)
        base = np.block([[cos, sin], [-sin, cos]])
        for table in (base, base.T):
            high, low = split_host(table)
            left.append(np.concatenate([high, high, low], axis=1))
            right.append(np.concatenate([high, high, low], axis=0))
    return np.stack(left), np.stack(right)


def parity_tables(size):
    order = np.concatenate([np.arange(0, size, 2), np.arange(1, size, 2)])
    gather = np.eye(size)[order].astype(ml_dtypes.bfloat16)
    return np.concatenate([gather] * 3, axis=1), np.concatenate([gather.T] * 3, axis=0)


def matmul(left, right):
    return jnp.dot(left, right, preferred_element_type=F32)


def split(value):
    high = value.astype(BF16)
    return high, (value - high.astype(F32)).astype(BF16)


def put_rows(ref, start, columns, value):
    rows = value.shape[0]
    high, low = split(value)
    third = ref.shape[0] // 3
    ref[start : start + rows, columns] = high
    ref[third + start : third + start + rows, columns] = low
    ref[2 * third + start : 2 * third + start + rows, columns] = high


def put_columns(ref, rows, start, value):
    width = value.shape[1]
    high, low = split(value)
    third = ref.shape[1] // 3
    ref[rows, start : start + width] = high
    ref[rows, third + start : third + start + width] = low
    ref[rows, 2 * third + start : 2 * third + start + width] = high


def place(row, col, last):
    tile = jnp.minimum(lax.shift_right_logical(col, 7), last)
    return row, tile, col - tile * LANES


def add_window(accumulate, row, tile, offset, first, second):
    rows = first.shape[0]
    turn = jnp.bitwise_and(offset, LANES - 1)
    kept = lax.broadcasted_iota(jnp.int32, first.shape, 1) >= offset
    first = pltpu.roll(first, turn, 1)
    second = pltpu.roll(second, turn, 1)
    where = pl.ds(row, rows)
    accumulate[tile, where, :] += jnp.where(kept, first, 0.0)
    accumulate[tile + 1, where, :] += jnp.where(kept, second, first)
    accumulate[tile + 2, where, :] += jnp.where(kept, 0.0, second)


def fold_kernel(count, measured, gather_left, gather_right, folded, parts):
    size = measured.shape[1]

    def three(value):
        high = value.astype(BF16)
        rest = value - high.astype(F32)
        middle = rest.astype(BF16)
        return high, middle, (rest - middle.astype(F32)).astype(BF16)

    def step(slot, carry):
        for index, part in enumerate(three(measured[slot])):
            parts[:, index * size : (index + 1) * size] = part
        value = matmul(parts[...], gather_right[...])
        folded[slot] = matmul(gather_left[...], jnp.concatenate(three(value), axis=0))
        return carry

    lax.fori_loop(0, count[0], step, 0)


def ends_kernel(tile_ref, low, high, notes, top, bottom):
    half = LANES
    side = tile_ref.shape[1]
    tiles = side // LANES
    for out, start in ((top, 0), (bottom, side - half)):
        rows = slice(start, start + half)
        for index in range(tiles):
            out[:, 1 + index, :half, :] = tile_ref[:, rows, index * LANES : (index + 1) * LANES]
        for index, strip in ((0, low), (1 + tiles, high)):
            out[:, index, :half, :] = strip[:, rows, :]
            out[:, index, half:, :] = strip[:, side:, :]
        out[:, 1, half:, :] = notes[...]
        out[:, 2 : 1 + tiles, half:, :] = jnp.zeros((2, tiles - 1, 8, LANES), F32)


def slot_kernel(
    position, count, probe, folded, left, right, tile_ref, low, high, top, bottom,
    margin_top, margin_bottom, side_low, side_high, middle, sums, canvas, grad, probe_sum, patch, rhs, lhs,
):
    size = probe.shape[1]
    half = size // 2
    side = tile_ref.shape[1]
    tiles = side // LANES
    inner = slice(half, half + side)
    for index in range(tiles):
        canvas[:, 1 + index, inner, :] = tile_ref[:, :, index * LANES : (index + 1) * LANES]
    canvas[:, 0, inner, :] = low[:, :side, :]
    canvas[:, 1 + tiles, inner, :] = high[:, :side, :]
    canvas[:, :, :half, :] = top[:, :, :half, :]
    canvas[:, :, half + side :, :] = bottom[:, :, :half, :]
    grad[...] = jnp.zeros_like(grad)
    probe_sum[...] = jnp.zeros_like(probe_sum)
    near, far = slice(0, half), slice(half, size)

    def step(slot, carry):
        row, tile, offset = place(position[0, slot] + half, position[1, slot] + half, tiles - 1)
        turn = jnp.bitwise_and(LANES - offset, LANES - 1)
        kept = lax.broadcasted_iota(jnp.int32, (size, LANES), 1) < LANES - offset
        for plane in range(2):
            raw = [pltpu.roll(canvas[plane, tile + index, pl.ds(row, size), :], turn, 1) for index in range(3)]
            patch[plane, 0] = jnp.where(kept, raw[0], raw[1])
            patch[plane, 1] = jnp.where(kept, raw[1], raw[2])
        for index, columns in enumerate((near, far)):
            probe_re, probe_im = probe[0, :, columns], probe[1, :, columns]
            patch_re, patch_im = patch[0, index], patch[1, index]
            exit_re = probe_re * patch_re - probe_im * patch_im
            exit_im = probe_re * patch_im + probe_im * patch_re
            probe_sum[2, index] += patch_re * patch_re + patch_im * patch_im
            put_rows(rhs.at[0], 0, columns, exit_re[:half] + exit_re[half:])
            put_rows(rhs.at[0], half, columns, exit_im[:half] + exit_im[half:])
            put_rows(rhs.at[1], 0, columns, exit_re[:half] - exit_re[half:])
            put_rows(rhs.at[1], half, columns, exit_im[:half] - exit_im[half:])
        for parity_ in range(2):
            value = matmul(left[2 * parity_], rhs[parity_])
            rows = slice(parity_ * half, (parity_ + 1) * half)
            put_columns(lhs.at[0], rows, 0, value[:half, near] + value[:half, far])
            put_columns(lhs.at[0], rows, half, value[half:, near] + value[half:, far])
            put_columns(lhs.at[1], rows, 0, value[:half, near] - value[:half, far])
            put_columns(lhs.at[1], rows, half, value[half:, near] - value[half:, far])
        everything = slice(0, size)
        back = []
        for parity_ in range(2):
            value = matmul(lhs[parity_], right[2 * parity_ + 1])
            wave_re, wave_im = value[:, near], value[:, far]
            columns = slice(parity_ * half, (parity_ + 1) * half)
            excess = wave_re * wave_re + wave_im * wave_im - folded[slot, :, columns]
            put_columns(lhs.at[parity_], everything, 0, excess * wave_re)
            put_columns(lhs.at[parity_], everything, half, excess * wave_im)
            back.append(matmul(lhs[parity_], right[2 * parity_]))
        for parity_ in range(2):
            rows = slice(parity_ * half, (parity_ + 1) * half)
            put_rows(rhs.at[parity_], 0, near, back[0][rows, near] + back[1][rows, near])
            put_rows(rhs.at[parity_], half, near, back[0][rows, far] + back[1][rows, far])
            put_rows(rhs.at[parity_], 0, far, back[0][rows, near] - back[1][rows, near])
            put_rows(rhs.at[parity_], half, far, back[0][rows, far] - back[1][rows, far])
        even = matmul(left[1], rhs[0])
        odd = matmul(left[3], rhs[1])
        pieces = []
        for index, columns in enumerate((near, far)):
            chi_re, chi_im = (
                jnp.concatenate([even[rows, columns] + odd[rows, columns], even[rows, columns] - odd[rows, columns]], axis=0)
                for rows in (near, far)
            )
            probe_re, probe_im = probe[0, :, columns], probe[1, :, columns]
            patch_re, patch_im = patch[0, index], patch[1, index]
            probe_sum[0, index] += patch_re * chi_re + patch_im * chi_im
            probe_sum[1, index] += patch_re * chi_im - patch_im * chi_re
            pieces.append((probe_re * chi_re + probe_im * chi_im, probe_re * chi_im - probe_im * chi_re))
        for plane in range(2):
            add_window(grad.at[plane], row, tile, offset, pieces[0][plane], pieces[1][plane])
        return carry

    lax.fori_loop(0, count[0], step, 0)
    margin_top[...] = grad[:, :, :half, :]
    margin_bottom[...] = grad[:, :, half + side :, :]
    side_low[...] = grad[:, 0, inner, :]
    side_high[...] = grad[:, 1 + tiles, inner, :]
    middle[...] = grad[:, 1 : 1 + tiles, inner, :]
    for plane in range(3):
        for index in range(2):
            sums[:, 2 * plane + index] = probe_sum[plane, index].reshape(size // 8, 8, LANES)


def sides_kernel(first, last, above_first, above_last, below_first, below_last, low, high):
    half = LANES
    side = first.shape[1]
    for out, own, above, below in ((low, first, above_first, below_first), (high, last, above_last, below_last)):
        out[...] = own[...]
        out[:, :half, :] += above[:, 0]
        out[:, side - half :, :] += below[:, 0]


def weight_kernel(probe, notes, low, high, top, bottom, scale, power, weight, numbers, sems):
    half = LANES
    side = scale.shape[1]
    tiles = side // LANES
    sources = (
        top.at[0, 0, half:, :], top.at[0, 1, half:, :], top.at[0, 1 + tiles, half:, :],
        low.at[0, side:, :], notes.at[0], high.at[0, side:, :],
        bottom.at[0, 0, half:, :], bottom.at[0, 1, half:, :], bottom.at[0, 1 + tiles, half:, :],
    )
    copies = [pltpu.make_async_copy(source, numbers.at[index], sems.at[index]) for index, source in enumerate(sources)]
    for copy in copies:
        copy.start()
    weight[...] = jnp.zeros_like(weight)
    for index in range(2):
        columns = slice(index * LANES, (index + 1) * LANES)
        power[index] = probe[0, :, columns] * probe[0, :, columns] + probe[1, :, columns] * probe[1, :, columns]
    for copy in copies:
        copy.wait()
    for index in range(9):
        down, across = index // 3 - 1, index % 3 - 1

        def step(slot, carry):
            row = numbers[index, 0, slot].astype(jnp.int32) + (2 * half + down * side)
            col = numbers[index, 1, slot].astype(jnp.int32) + (2 * half + across * side)
            reach = side + 2 * half

            @pl.when((row > 0) & (row < reach) & (col > 0) & (col < reach))
            def add():
                at, tile, offset = place(row, col, tiles + 1)
                add_window(weight, at, tile, offset, power[0], power[1])

            return carry

        lax.fori_loop(0, numbers[index, 2, 0].astype(jnp.int32), step, 0)
    for index in range(tiles):
        scale[index] = 1.0 / (weight[2 + index, 2 * half : 2 * half + side, :] + 1.0)


def final_kernel(tile_ref, middle, above, below, low, high, scale, out):
    half = LANES
    side = tile_ref.shape[1]
    index = pl.program_id(0)
    is_first = (index == 0).astype(F32)
    is_last = (index == pl.num_programs(0) - 1).astype(F32)
    for plane in range(2):
        for start in range(0, side, half):
            rows = slice(start, start + half)
            value = middle[plane, 0, rows, :]
            if start == 0:
                value = value + above[plane, 0]
            if start + half == side:
                value = value + below[plane, 0]
            value = value + low[plane, rows, :] * is_first + high[plane, rows, :] * is_last
            out[plane, rows, :] = tile_ref[plane, rows, :] - value * scale[0, rows, :]


def plane_kernel(parts, out):
    out[...] = jnp.broadcast_to(jnp.sum(parts[...], axis=0)[None], out.shape)


def probe_kernel(index, parts, probe, out):
    total = jnp.sum(parts[...], axis=0)
    rows = pl.ds(pl.multiple_of(index[0] * 8, 8), 8)
    for tile in range(2):
        root = jnp.sqrt(total[4 + tile] + 1.0)
        for plane in range(2):
            new = probe[plane, rows, tile * LANES : (tile + 1) * LANES] - total[2 * plane + tile] / root
            out[:, 2 * plane + tile] = jnp.broadcast_to(new[None], (out.shape[0], 8, LANES))


def join_kernel(pieces, out):
    for plane in range(2):
        for tile in range(2):
            value = pieces[:, 2 * plane + tile]
            out[plane, :, tile * LANES : (tile + 1) * LANES] = value.reshape(out.shape[1], LANES)


def both_ways(low, high, axis):
    count = lax.axis_size(axis)
    up = [(index, index + 1) for index in range(count - 1)]
    down = [(index + 1, index) for index in range(count - 1)]
    return lax.ppermute(high, axis, up), lax.ppermute(low, axis, down)


def block(shape, *where):
    return pl.BlockSpec(shape, lambda *_: where)


def params(mib):
    return pltpu.CompilerParams(vmem_limit_bytes=mib * 2**20)


def solution(mesh):
    rows, cols = mesh.shape["ty"], mesh.shape["tx"]
    near_y, near_z = 8, 4
    planes = [
        [(8 * high + row) * cols + near_z * x + low for row in range(near_y) for x in range(cols // near_z)]
        for high in range(rows // near_y)
        for low in range(near_z)
    ]
    lines = [list(line) for line in zip(*planes)]

    def trade(pieces, groups):
        return lax.all_to_all(pieces, ("ty", "tx"), 0, 0, axis_index_groups=groups, tiled=True)

    def per_device(object_field, probe, intensity, positions, counts):
        side = object_field.shape[1]
        size = probe.shape[1]
        half = size // 2
        slots = intensity.shape[2]
        tiles = side // LANES
        position = positions[:, 0, 0, :]
        count = counts[0]
        row, col = lax.axis_index("ty"), lax.axis_index("tx")
        piece = jnp.bitwise_and(row, near_y - 1) * (cols // near_z) + lax.shift_right_logical(col, 2)
        piece = piece.reshape(1).astype(jnp.int32)
        left, right = (jnp.asarray(table) for table in half_tables(size))
        gather_left, gather_right = (jnp.asarray(table) for table in parity_tables(size))

        notes = jnp.zeros((8, LANES), F32).at[:2, :slots].set(position.astype(F32))
        notes = notes.at[2, 0].set(counts[0, 0].astype(F32))
        notes = jnp.stack([notes, jnp.zeros_like(notes)])
        low, high = both_ways(
            jnp.concatenate([object_field[:, :, :half], notes], axis=1),
            jnp.concatenate([object_field[:, :, side - half :], notes], axis=1),
            "tx",
        )
        folded = pl.pallas_call(
            fold_kernel,
            out_shape=jax.ShapeDtypeStruct((slots, size, size), F32),
            in_specs=[SMEM, VMEM, VMEM, VMEM],
            out_specs=VMEM,
            scratch_shapes=[pltpu.VMEM((size, 3 * size), BF16)],
            compiler_params=params(16),
            name="fold",
        )(count, intensity[0, 0], gather_left, gather_right)
        end = jax.ShapeDtypeStruct((2, tiles + 2, half + 8, LANES), F32)
        first_rows, last_rows = pl.pallas_call(
            ends_kernel,
            out_shape=(end, end),
            in_specs=[VMEM] * 4,
            out_specs=(VMEM, VMEM),
            compiler_params=params(16),
            name="ends",
        )(object_field, low, high, notes)
        top, bottom = both_ways(first_rows, last_rows, "ty")

        margin = jax.ShapeDtypeStruct((2, tiles + 2, half, LANES), F32)
        strip = jax.ShapeDtypeStruct((2, side, LANES), F32)
        members = len(planes[0])
        margin_top, margin_bottom, side_low, side_high, middle, sums = pl.pallas_call(
            slot_kernel,
            out_shape=(
                margin, margin, strip, strip,
                jax.ShapeDtypeStruct((2, tiles, side, LANES), F32),
                jax.ShapeDtypeStruct((members, 6, 8, LANES), F32),
            ),
            in_specs=[SMEM] * 2 + [VMEM] * 9,
            out_specs=(VMEM,) * 6,
            scratch_shapes=[
                pltpu.VMEM((2, tiles + 2, side + size, LANES), F32),
                pltpu.VMEM((2, tiles + 2, side + size, LANES), F32),
                pltpu.VMEM((3, 2, size, LANES), F32),
                pltpu.VMEM((2, 2, size, LANES), F32),
                pltpu.VMEM((2, 3 * size, size), BF16),
                pltpu.VMEM((2, size, 3 * size), BF16),
            ],
            compiler_params=params(48),
            name="slots",
        )(position, count, probe, folded, left, right, object_field, low, high, top, bottom)

        above, below = both_ways(margin_top, margin_bottom, "ty")
        parts = trade(sums, planes)
        tall = (2, 1, side, LANES)
        flat = (2, 1, half, LANES)
        whole = block((2, side, LANES), 0, 0, 0)
        margin_low, margin_high = pl.pallas_call(
            sides_kernel,
            out_shape=(strip, strip),
            grid=(1,),
            in_specs=[
                whole, whole,
                block(flat, 0, 0, 0, 0), block(flat, 0, tiles + 1, 0, 0),
                block(flat, 0, 0, 0, 0), block(flat, 0, tiles + 1, 0, 0),
            ],
            out_specs=(whole, whole),
            name="sides",
        )(side_low, side_high, above, above, below, below)
        from_low, from_high = both_ways(margin_low, margin_high, "tx")

        parts = pl.pallas_call(
            plane_kernel,
            out_shape=jax.ShapeDtypeStruct((len(lines[0]), 6, 8, LANES), F32),
            in_specs=[VMEM],
            out_specs=VMEM,
            name="plane_sum",
        )(parts)
        parts = trade(parts, lines)
        pieces = pl.pallas_call(
            probe_kernel,
            out_shape=jax.ShapeDtypeStruct((members, 4, 8, LANES), F32),
            in_specs=[SMEM, VMEM, VMEM],
            out_specs=VMEM,
            name="probe_rows",
        )(piece, parts, probe)
        probe_new = pl.pallas_call(
            join_kernel,
            out_shape=jax.ShapeDtypeStruct(probe.shape, F32),
            in_specs=[VMEM],
            out_specs=VMEM,
            name="join",
        )(trade(pieces, planes))

        scale = pl.pallas_call(
            weight_kernel,
            out_shape=jax.ShapeDtypeStruct((tiles, side, LANES), F32),
            in_specs=[VMEM] + [ANY] * 5,
            out_specs=VMEM,
            scratch_shapes=[
                pltpu.VMEM((2, size, LANES), F32),
                pltpu.VMEM((tiles + 4, side + 2 * size, LANES), F32),
                pltpu.SMEM((9, 8, LANES), F32),
                pltpu.SemaphoreType.DMA((9,)),
            ],
            compiler_params=params(16),
            name="weights",
        )(probe, notes, low, high, top, bottom)
        object_new = pl.pallas_call(
            final_kernel,
            out_shape=jax.ShapeDtypeStruct(object_field.shape, F32),
            grid=(tiles,),
            in_specs=[
                pl.BlockSpec((2, side, LANES), lambda index: (0, 0, index)),
                pl.BlockSpec(tall, lambda index: (0, index, 0, 0)),
                pl.BlockSpec(flat, lambda index: (0, index + 1, 0, 0)),
                pl.BlockSpec(flat, lambda index: (0, index + 1, 0, 0)),
                block((2, side, LANES), 0, 0, 0),
                block((2, side, LANES), 0, 0, 0),
                pl.BlockSpec((1, side, LANES), lambda index: (index, 0, 0)),
            ],
            out_specs=pl.BlockSpec((2, side, LANES), lambda index: (0, 0, index)),
            compiler_params=params(24),
            name="final",
        )(object_field, middle, above, below, from_low, from_high, scale)
        return (object_new, probe_new)

    in_specs = (
        P(None, "ty", "tx"),
        P(),
        P("ty", "tx", None, None, None),
        P(None, "ty", "tx", None),
        P("ty", "tx"),
    )
    out_specs = (P(None, "ty", "tx"), P())
    return jax.shard_map(per_device, mesh=mesh, in_specs=in_specs, out_specs=out_specs, check_vma=False)
```

```python
import numpy as np
import ml_dtypes
import jax
import jax.numpy as jnp
from jax import lax
from jax.experimental import pallas as pl
from jax.experimental.pallas import tpu as pltpu
from jax.sharding import PartitionSpec as P

BF16 = jnp.bfloat16
F32 = jnp.float32
LANES = 128
VMEM = pl.BlockSpec(memory_space=pltpu.VMEM)
SMEM = pl.BlockSpec(memory_space=pltpu.SMEM)
HBM = pl.BlockSpec(memory_space=pltpu.HBM)
def split_host(table):
    high = table.astype(ml_dtypes.bfloat16)
    low = (table - high.astype(np.float64)).astype(ml_dtypes.bfloat16)
    return high, low


def half_tables(size):
    half = size // 2
    left, right = [], []
    for parity in range(2):
        product = (2 * np.arange(half)[:, None] + parity) * np.arange(half)[None, :] % size
        angle = 2.0 * np.pi * product / size
        cos, sin = np.cos(angle) / np.sqrt(size), np.sin(angle) / np.sqrt(size)
        base = np.block([[cos, sin], [-sin, cos]])
        for table in (base, base.T):
            high, low = split_host(table)
            left.append(np.concatenate([high, high, low], axis=1))
            right.append(np.concatenate([high, high, low], axis=0))
    return np.stack(left), np.stack(right)


def parity_tables(size):
    order = np.concatenate([np.arange(0, size, 2), np.arange(1, size, 2)])
    gather = np.eye(size)[order].astype(ml_dtypes.bfloat16)
    return np.concatenate([gather] * 3, axis=1), np.concatenate([gather.T] * 3, axis=0)


def matmul(left, right):
    return jnp.dot(left, right, preferred_element_type=F32)


def split(value):
    high = value.astype(BF16)
    return high, (value - high.astype(F32)).astype(BF16)


def put_rows(ref, start, columns, value):
    rows = value.shape[0]
    high, low = split(value)
    third = ref.shape[0] // 3
    ref[start : start + rows, columns] = high
    ref[third + start : third + start + rows, columns] = low
    ref[2 * third + start : 2 * third + start + rows, columns] = high


def put_columns(ref, rows, start, value):
    width = value.shape[1]
    high, low = split(value)
    third = ref.shape[1] // 3
    ref[rows, start : start + width] = high
    ref[rows, third + start : third + start + width] = low
    ref[rows, 2 * third + start : 2 * third + start + width] = high


def place(row, col, last):
    tile = jnp.minimum(lax.shift_right_logical(col, 7), last)
    return row, tile, col - tile * LANES


def add_window(accumulate, row, tile, offset, first, second):
    rows = first.shape[0]
    turn = jnp.bitwise_and(offset, LANES - 1)
    kept = lax.broadcasted_iota(jnp.int32, first.shape, 1) >= offset
    first = pltpu.roll(first, turn, 1)
    second = pltpu.roll(second, turn, 1)
    where = pl.ds(row, rows)
    accumulate[tile, where, :] += jnp.where(kept, first, 0.0)
    accumulate[tile + 1, where, :] += jnp.where(kept, second, first)
    accumulate[tile + 2, where, :] += jnp.where(kept, 0.0, second)


def fold_kernel(count, measured, gather_left, gather_right, folded, parts):
    size = measured.shape[1]

    def three(value):
        high = value.astype(BF16)
        rest = value - high.astype(F32)
        middle = rest.astype(BF16)
        return high, middle, (rest - middle.astype(F32)).astype(BF16)

    def step(slot, carry):
        for index, part in enumerate(three(measured[slot])):
            parts[:, index * size : (index + 1) * size] = part
        value = matmul(parts[...], gather_right[...])
        folded[slot] = matmul(gather_left[...], jnp.concatenate(three(value), axis=0))
        return carry

    lax.fori_loop(0, count[0], step, 0)


def ends_kernel(tile_ref, low, high, notes, top, bottom):
    half = LANES
    side = tile_ref.shape[1]
    tiles = side // LANES
    for out, start in ((top, 0), (bottom, side - half)):
        rows = slice(start, start + half)
        for index in range(tiles):
            out[:, 1 + index, :half, :] = tile_ref[:, rows, index * LANES : (index + 1) * LANES]
        for index, strip in ((0, low), (1 + tiles, high)):
            out[:, index, :half, :] = strip[:, rows, :]
            out[:, index, half:, :] = strip[:, side:, :]
        out[:, 1, half:, :] = notes[...]
        out[:, 2 : 1 + tiles, half:, :] = jnp.zeros((2, tiles - 1, 8, LANES), F32)


def slot_stages(row, tile, offset, live, probe, measured, left, right, canvas, grad, probe_sum, patch, rhs, lhs):
    size = probe.shape[1]
    half = size // 2
    near, far = slice(0, half), slice(half, size)
    turn = jnp.bitwise_and(LANES - offset, LANES - 1)
    kept = lax.broadcasted_iota(jnp.int32, (size, LANES), 1) < LANES - offset
    for plane in range(2):
        raw = [pltpu.roll(canvas[plane, tile + index, pl.ds(row, size), :], turn, 1) for index in range(3)]
        patch[plane, 0] = jnp.where(kept, raw[0], raw[1])
        patch[plane, 1] = jnp.where(kept, raw[1], raw[2])
    for index, columns in enumerate((near, far)):
        probe_re, probe_im = probe[0, :, columns], probe[1, :, columns]
        patch_re, patch_im = patch[0, index], patch[1, index]
        exit_re = probe_re * patch_re - probe_im * patch_im
        exit_im = probe_re * patch_im + probe_im * patch_re
        probe_sum[2, index] += (patch_re * patch_re + patch_im * patch_im) * live
        put_rows(rhs.at[0], 0, columns, exit_re[:half] + exit_re[half:])
        put_rows(rhs.at[0], half, columns, exit_im[:half] + exit_im[half:])
        put_rows(rhs.at[1], 0, columns, exit_re[:half] - exit_re[half:])
        put_rows(rhs.at[1], half, columns, exit_im[:half] - exit_im[half:])
    yield
    for parity in range(2):
        value = matmul(left[2 * parity], rhs[parity])
        rows = slice(parity * half, (parity + 1) * half)
        put_columns(lhs.at[0], rows, 0, value[:half, near] + value[:half, far])
        put_columns(lhs.at[0], rows, half, value[half:, near] + value[half:, far])
        put_columns(lhs.at[1], rows, 0, value[:half, near] - value[:half, far])
        put_columns(lhs.at[1], rows, half, value[half:, near] - value[half:, far])
        yield
    everything = slice(0, size)
    for parity in range(2):
        value = matmul(lhs[parity], right[2 * parity + 1])
        wave_re, wave_im = value[:, near], value[:, far]
        columns = slice(parity * half, (parity + 1) * half)
        excess = (wave_re * wave_re + wave_im * wave_im - measured[:, columns]) * live
        put_columns(lhs.at[parity], everything, 0, excess * wave_re)
        put_columns(lhs.at[parity], everything, half, excess * wave_im)
        yield
    back = []
    for parity in range(2):
        back.append(matmul(lhs[parity], right[2 * parity]))
    for parity in range(2):
        rows = slice(parity * half, (parity + 1) * half)
        put_rows(rhs.at[parity], 0, near, back[0][rows, near] + back[1][rows, near])
        put_rows(rhs.at[parity], half, near, back[0][rows, far] + back[1][rows, far])
        put_rows(rhs.at[parity], 0, far, back[0][rows, near] - back[1][rows, near])
        put_rows(rhs.at[parity], half, far, back[0][rows, far] - back[1][rows, far])
    yield
    even = matmul(left[1], rhs[0])
    odd = matmul(left[3], rhs[1])
    pieces = []
    for index, columns in enumerate((near, far)):
        chi_re, chi_im = (
            jnp.concatenate([even[rows, columns] + odd[rows, columns], even[rows, columns] - odd[rows, columns]], axis=0)
            for rows in (near, far)
        )
        probe_re, probe_im = probe[0, :, columns], probe[1, :, columns]
        patch_re, patch_im = patch[0, index], patch[1, index]
        probe_sum[0, index] += patch_re * chi_re + patch_im * chi_im
        probe_sum[1, index] += patch_re * chi_im - patch_im * chi_re
        pieces.append((probe_re * chi_re + probe_im * chi_im, probe_re * chi_im - probe_im * chi_re))
    for plane in range(2):
        add_window(grad.at[plane], row, tile, offset, pieces[0][plane], pieces[1][plane])
    yield


def run_slots(wanted, base, position, count, probe, folded, left, right, canvas, grad, probe_sum, order, patch, rhs, lhs):
    size = probe.shape[1]
    half = size // 2
    tiles = canvas.shape[1] - 2
    reach = tiles * LANES - size

    def pick(slot, found):
        row = position[0, slot]
        inside = (row >= 0) & (row <= reach)
        take = inside if wanted else jnp.logical_not(inside)

        @pl.when(take)
        def keep():
            order[found] = slot

        return found + jnp.where(take, 1, 0)

    total = lax.fori_loop(0, count[0], pick, 0)
    lanes = patch.shape[0]

    def step(group, carry):
        stages = []
        for lane in range(lanes):
            index = lanes * group + lane
            live = jnp.where(index < total, 1.0, 0.0)
            slot = order[jnp.minimum(index, total - 1)]
            row, tile, offset = place(position[0, slot] + base, position[1, slot] + half, tiles - 1)
            stages.append(slot_stages(
                row, tile, offset, live, probe, folded.at[slot], left, right, canvas, grad, probe_sum,
                patch.at[lane], rhs.at[lane], lhs.at[lane],
            ))
        for _ in zip(*stages):
            pass
        return carry

    lax.fori_loop(0, lax.div(total + (lanes - 1), lanes), step, 0)


def inner_kernel(position, count, probe, folded, left, right, tile_ref, low, high, grad, probe_sum, canvas, *scratch):
    side = tile_ref.shape[1]
    tiles = side // LANES
    for index in range(tiles):
        canvas[:, 1 + index] = tile_ref[:, :, index * LANES : (index + 1) * LANES]
    canvas[:, 0] = low[:, :side, :]
    canvas[:, 1 + tiles] = high[:, :side, :]
    grad[...] = jnp.zeros_like(grad)
    probe_sum[...] = jnp.zeros_like(probe_sum)
    run_slots(True, 0, position, count, probe, folded, left, right, canvas, grad, probe_sum, *scratch)


def outer_kernel(
    position, count, probe, folded, left, right, tile_ref, low, high, top, bottom, own_notes, grad_in, probe_sum_in,
    margin_top, margin_bottom, side_low, side_high, middle, sums, places, canvas, grad, probe_sum, sems, *scratch,
):
    size = probe.shape[1]
    half = size // 2
    side = tile_ref.shape[1]
    tiles = side // LANES
    inner = slice(half, half + side)
    for index in range(tiles):
        canvas[:, 1 + index, inner, :] = tile_ref[:, :, index * LANES : (index + 1) * LANES]
    canvas[:, 0, inner, :] = low[:, :side, :]
    canvas[:, 1 + tiles, inner, :] = high[:, :side, :]
    canvas[:, :, :half, :] = top[:, :, :half, :]
    canvas[:, :, half + side :, :] = bottom[:, :, :half, :]
    grad[:, :, :half, :] = jnp.zeros(margin_top.shape, F32)
    grad[:, :, half + side :, :] = jnp.zeros(margin_bottom.shape, F32)
    grad[:, :, inner, :] = grad_in[...]
    probe_sum[...] = probe_sum_in[...]
    run_slots(False, half, position, count, probe, folded, left, right, canvas, grad, probe_sum, *scratch)
    ends = slice(half, half + 8)
    notes = (
        top[0, 0, ends], top[0, 1, ends], top[0, 1 + tiles, ends],
        low[0, side:], own_notes[0], high[0, side:],
        bottom[0, 0, ends], bottom[0, 1, ends], bottom[0, 1 + tiles, ends],
    )
    for index, value in enumerate(notes):
        places[index] = value
    copies = [
        pltpu.make_async_copy(source, target, sems.at[index])
        for index, (source, target) in enumerate((
            (grad.at[:, :, :half, :], margin_top),
            (grad.at[:, :, half + side :, :], margin_bottom),
            (grad.at[:, 0, inner, :], side_low),
            (grad.at[:, 1 + tiles, inner, :], side_high),
            (grad.at[:, 1 : 1 + tiles, inner, :], middle),
        ))
    ]
    for copy in copies:
        copy.start()
    for plane in range(3):
        for index in range(2):
            sums[:, 2 * plane + index] = probe_sum[plane, index].reshape(size // 8, 8, LANES)
    for copy in copies:
        copy.wait()


def sides_kernel(first, last, above_first, above_last, below_first, below_last, low, high):
    half = LANES
    side = first.shape[1]
    for out, own, above, below in ((low, first, above_first, below_first), (high, last, above_last, below_last)):
        out[...] = own[...]
        out[:, :half, :] += above[:, 0]
        out[:, side - half :, :] += below[:, 0]


def weight_kernel(numbers, probe, scale, power, weight):
    half = LANES
    side = scale.shape[1]
    tiles = side // LANES
    weight[...] = jnp.zeros_like(weight)
    for index in range(2):
        columns = slice(index * LANES, (index + 1) * LANES)
        power[index] = probe[0, :, columns] * probe[0, :, columns] + probe[1, :, columns] * probe[1, :, columns]
    for index in range(9):
        down, across = index // 3 - 1, index % 3 - 1

        def step(slot, carry):
            row = numbers[index, 0, slot].astype(jnp.int32) + (2 * half + down * side)
            col = numbers[index, 1, slot].astype(jnp.int32) + (2 * half + across * side)
            reach = side + 2 * half

            @pl.when((row > 0) & (row < reach) & (col > 0) & (col < reach))
            def add():
                at, tile, offset = place(row, col, tiles + 1)
                add_window(weight, at, tile, offset, power[0], power[1])

            return carry

        lax.fori_loop(0, numbers[index, 2, 0].astype(jnp.int32), step, 0)
    for index in range(tiles):
        scale[index] = 1.0 / (weight[2 + index, 2 * half : 2 * half + side, :] + 1.0)


def update_kernel(tile_ref, grad, above, below, scale, out):
    half = LANES
    side = tile_ref.shape[1]
    for plane in range(2):
        for start in range(0, side, half):
            rows = slice(start, start + half)
            value = grad[plane, 0, rows, :]
            if start == 0:
                value = value + above[plane, 0]
            if start + half == side:
                value = value + below[plane, 0]
            out[plane, rows, :] = tile_ref[plane, rows, :] - value * scale[0, rows, :]


def edge_kernel(before, low, high, scale, out):
    is_low = (pl.program_id(0) == 0).astype(F32)
    is_high = 1.0 - is_low
    for plane in range(2):
        out[plane] = before[plane] - (low[plane] * is_low + high[plane] * is_high) * scale[0]


def plane_kernel(parts, out):
    out[...] = jnp.broadcast_to(jnp.sum(parts[...], axis=0)[None], out.shape)


def probe_kernel(index, parts, probe, out):
    total = jnp.sum(parts[...], axis=0)
    rows = pl.ds(pl.multiple_of(index[0] * 8, 8), 8)
    for tile in range(2):
        root = jnp.sqrt(total[4 + tile] + 1.0)
        for plane in range(2):
            new = probe[plane, rows, tile * LANES : (tile + 1) * LANES] - total[2 * plane + tile] / root
            out[:, 2 * plane + tile] = jnp.broadcast_to(new[None], (out.shape[0], 8, LANES))


def join_kernel(pieces, out):
    for plane in range(2):
        for tile in range(2):
            value = pieces[:, 2 * plane + tile]
            out[plane, :, tile * LANES : (tile + 1) * LANES] = value.reshape(out.shape[1], LANES)


def both_ways(low, high, axis):
    count = lax.axis_size(axis)
    up = [(index, index + 1) for index in range(count - 1)]
    down = [(index + 1, index) for index in range(count - 1)]
    return lax.ppermute(high, axis, up), lax.ppermute(low, axis, down)


def block(shape, *where):
    return pl.BlockSpec(shape, lambda *_: where)


def params(mib):
    return pltpu.CompilerParams(vmem_limit_bytes=mib * 2**20)


def cost(mib):
    return pl.CostEstimate(flops=0, bytes_accessed=mib * 2**20, transcendentals=0)


def solution(mesh):
    rows, cols = mesh.shape["ty"], mesh.shape["tx"]
    near_y, near_z = 8, 4
    planes = [
        [(8 * high + row) * cols + near_z * x + low for row in range(near_y) for x in range(cols // near_z)]
        for high in range(rows // near_y)
        for low in range(near_z)
    ]
    lines = [list(line) for line in zip(*planes)]

    def trade(pieces, groups):
        return lax.all_to_all(pieces, ("ty", "tx"), 0, 0, axis_index_groups=groups, tiled=True)

    def per_device(object_field, probe, intensity, positions, counts):
        side = object_field.shape[1]
        size = probe.shape[1]
        half = size // 2
        slots = intensity.shape[2]
        tiles = side // LANES
        position = positions[:, 0, 0, :]
        count = counts[0]
        row, col = lax.axis_index("ty"), lax.axis_index("tx")
        piece = jnp.bitwise_and(row, near_y - 1) * (cols // near_z) + lax.shift_right_logical(col, 2)
        piece = piece.reshape(1).astype(jnp.int32)
        left, right = (jnp.asarray(table) for table in half_tables(size))
        gather_left, gather_right = (jnp.asarray(table) for table in parity_tables(size))

        notes = jnp.zeros((8, LANES), F32).at[:2, :slots].set(position.astype(F32))
        notes = notes.at[2, 0].set(counts[0, 0].astype(F32))
        notes = jnp.stack([notes, jnp.zeros_like(notes)])
        low, high = both_ways(
            jnp.concatenate([object_field[:, :, :half], notes], axis=1),
            jnp.concatenate([object_field[:, :, side - half :], notes], axis=1),
            "tx",
        )
        folded = pl.pallas_call(
            fold_kernel,
            out_shape=jax.ShapeDtypeStruct((slots, size, size), F32),
            in_specs=[SMEM, VMEM, VMEM, VMEM],
            out_specs=VMEM,
            scratch_shapes=[pltpu.VMEM((size, 3 * size), BF16)],
            compiler_params=params(8),
            cost_estimate=cost(6),
            name="fold",
        )(count, intensity[0, 0], gather_left, gather_right)
        end = jax.ShapeDtypeStruct((2, tiles + 2, half + 8, LANES), F32)
        first_rows, last_rows = pl.pallas_call(
            ends_kernel,
            out_shape=(end, end),
            in_specs=[VMEM] * 4,
            out_specs=(VMEM, VMEM),
            compiler_params=params(8),
            cost_estimate=cost(4),
            name="ends",
        )(object_field, low, high, notes)
        top, bottom = both_ways(first_rows, last_rows, "ty")

        margin = pltpu.HBM((2, tiles + 2, half, LANES), F32)
        strip = jax.ShapeDtypeStruct((2, side, LANES), F32)
        members = len(planes[0])
        lanes = 2
        scratch = [
            pltpu.SMEM((slots,), jnp.int32),
            pltpu.VMEM((lanes, 2, 2, size, LANES), F32),
            pltpu.VMEM((lanes, 2, 3 * size, size), BF16),
            pltpu.VMEM((lanes, 2, size, 3 * size), BF16),
        ]
        grad, probe_sum = pl.pallas_call(
            inner_kernel,
            out_shape=(
                jax.ShapeDtypeStruct((2, tiles + 2, side, LANES), F32),
                jax.ShapeDtypeStruct((3, 2, size, LANES), F32),
            ),
            in_specs=[SMEM] * 2 + [VMEM] * 7,
            out_specs=(VMEM,) * 2,
            scratch_shapes=[pltpu.VMEM((2, tiles + 2, side, LANES), F32)] + scratch,
            compiler_params=params(22),
            cost_estimate=cost(16),
            name="inner_slots",
        )(position, count, probe, folded, left, right, object_field, low, high)
        margin_top, margin_bottom, side_low, side_high, middle, sums, places = pl.pallas_call(
            outer_kernel,
            out_shape=(
                margin, margin,
                pltpu.HBM((2, side, LANES), F32),
                pltpu.HBM((2, side, LANES), F32),
                pltpu.HBM((2, tiles, side, LANES), F32),
                pltpu.HBM((members, 6, 8, LANES), F32),
                jax.ShapeDtypeStruct((9, 8, LANES), F32),
            ),
            in_specs=[SMEM] * 2 + [VMEM] * 12,
            out_specs=(HBM,) * 5 + (VMEM, VMEM),
            scratch_shapes=[
                pltpu.VMEM((2, tiles + 2, side + size, LANES), F32),
                pltpu.VMEM((2, tiles + 2, side + size, LANES), F32),
                pltpu.VMEM((3, 2, size, LANES), F32),
                pltpu.SemaphoreType.DMA((5,)),
            ] + scratch,
            compiler_params=params(30),
            cost_estimate=cost(16),
            name="outer_slots",
        )(position, count, probe, folded, left, right, object_field, low, high, top, bottom, notes, grad, probe_sum)

        above, below = both_ways(margin_top, margin_bottom, "ty")
        parts = trade(sums, planes)
        flat = (2, 1, half, LANES)
        whole = block((2, side, LANES), 0, 0, 0)

        margin_low, margin_high = pl.pallas_call(
            sides_kernel,
            out_shape=(strip, strip),
            grid=(1,),
            in_specs=[
                whole, whole,
                block(flat, 0, 0, 0, 0), block(flat, 0, tiles + 1, 0, 0),
                block(flat, 0, 0, 0, 0), block(flat, 0, tiles + 1, 0, 0),
            ],
            out_specs=(whole, whole),
            compiler_params=params(8),
            cost_estimate=cost(16),
            name="sides",
        )(side_low, side_high, above, above, below, below)
        from_low, from_high = both_ways(margin_low, margin_high, "tx")

        parts = pl.pallas_call(
            plane_kernel,
            out_shape=pltpu.HBM((len(lines[0]), 6, 8, LANES), F32),
            in_specs=[VMEM],
            out_specs=VMEM,
            compiler_params=params(6),
            cost_estimate=cost(2),
            name="plane_sum",
        )(parts)
        parts = trade(parts, lines)
        pieces = pl.pallas_call(
            probe_kernel,
            out_shape=pltpu.HBM((members, 4, 8, LANES), F32),
            in_specs=[SMEM, VMEM, VMEM],
            out_specs=VMEM,
            compiler_params=params(6),
            cost_estimate=cost(2),
            name="probe_rows",
        )(piece, parts, probe)
        probe_new = pl.pallas_call(
            join_kernel,
            out_shape=jax.ShapeDtypeStruct(probe.shape, F32),
            in_specs=[VMEM],
            out_specs=VMEM,
            compiler_params=params(6),
            cost_estimate=cost(2),
            name="join",
        )(trade(pieces, planes))

        scale = pl.pallas_call(
            weight_kernel,
            out_shape=jax.ShapeDtypeStruct((tiles, side, LANES), F32),
            in_specs=[SMEM, VMEM],
            out_specs=VMEM,
            scratch_shapes=[
                pltpu.VMEM((2, size, LANES), F32),
                pltpu.VMEM((tiles + 4, side + 2 * size, LANES), F32),
            ],
            compiler_params=params(8),
            cost_estimate=cost(8),
            name="weights",
        )(places, probe)
        column = pl.BlockSpec((2, side, LANES), lambda index: (0, 0, index))
        object_new = pl.pallas_call(
            update_kernel,
            out_shape=jax.ShapeDtypeStruct(object_field.shape, F32),
            grid=(tiles,),
            in_specs=[
                column,
                pl.BlockSpec((2, 1, side, LANES), lambda index: (0, index, 0, 0)),
                pl.BlockSpec(flat, lambda index: (0, index + 1, 0, 0)),
                pl.BlockSpec(flat, lambda index: (0, index + 1, 0, 0)),
                pl.BlockSpec((1, side, LANES), lambda index: (index, 0, 0)),
            ],
            out_specs=column,
            compiler_params=params(8),
            cost_estimate=cost(8),
            name="update",
        )(object_field, middle, above, below, scale)
        ends = pl.BlockSpec((2, side, LANES), lambda index: (0, 0, index * (tiles - 1)))
        object_new = pl.pallas_call(
            edge_kernel,
            out_shape=jax.ShapeDtypeStruct(object_field.shape, F32),
            grid=(2,),
            in_specs=[ends, whole, whole, pl.BlockSpec((1, side, LANES), lambda index: (index * (tiles - 1), 0, 0))],
            out_specs=ends,
            input_output_aliases={0: 0},
            compiler_params=params(8),
            name="edges",
        )(object_new, from_low, from_high, scale)
        return (object_new, probe_new)

    in_specs = (
        P(None, "ty", "tx"),
        P(),
        P("ty", "tx", None, None, None),
        P(None, "ty", "tx", None),
        P("ty", "tx"),
    )
    out_specs = (P(None, "ty", "tx"), P())
    return jax.shard_map(per_device, mesh=mesh, in_specs=in_specs, out_specs=out_specs, check_vma=False)
```

```python
import numpy as np
import ml_dtypes
import jax
import jax.numpy as jnp
from jax import lax
from jax.experimental import pallas as pl
from jax.experimental.pallas import tpu as pltpu
from jax.sharding import PartitionSpec as P

BF16 = jnp.bfloat16
F32 = jnp.float32
LANES = 128
VMEM = pl.BlockSpec(memory_space=pltpu.VMEM)
SMEM = pl.BlockSpec(memory_space=pltpu.SMEM)
HBM = pl.BlockSpec(memory_space=pltpu.HBM)
def split_host(table):
    high = table.astype(ml_dtypes.bfloat16)
    low = (table - high.astype(np.float64)).astype(ml_dtypes.bfloat16)
    return high, low


def half_tables(size):
    half = size // 2
    left, right = [], []
    for parity in range(2):
        product = (2 * np.arange(half)[:, None] + parity) * np.arange(half)[None, :] % size
        angle = 2.0 * np.pi * product / size
        cos, sin = np.cos(angle) / np.sqrt(size), np.sin(angle) / np.sqrt(size)
        base = np.block([[cos, sin], [-sin, cos]])
        for table in (base, base.T):
            high, low = split_host(table)
            left.append(np.concatenate([high, high, low], axis=1))
            right.append(np.concatenate([high, high, low], axis=0))
    return np.stack(left), np.stack(right)


def parity_tables(size):
    order = np.concatenate([np.arange(0, size, 2), np.arange(1, size, 2)])
    gather = np.eye(size)[order].astype(ml_dtypes.bfloat16)
    return np.concatenate([gather] * 3, axis=1), np.concatenate([gather.T] * 3, axis=0)


def matmul(left, right):
    return jnp.dot(left, right, preferred_element_type=F32)


def split(value):
    high = value.astype(BF16)
    return high, (value - high.astype(F32)).astype(BF16)


def put_rows(ref, start, columns, value):
    rows = value.shape[0]
    high, low = split(value)
    third = ref.shape[0] // 3
    ref[start : start + rows, columns] = high
    ref[third + start : third + start + rows, columns] = low
    ref[2 * third + start : 2 * third + start + rows, columns] = high


def put_columns(ref, rows, start, value):
    width = value.shape[1]
    high, low = split(value)
    third = ref.shape[1] // 3
    ref[rows, start : start + width] = high
    ref[rows, third + start : third + start + width] = low
    ref[rows, 2 * third + start : 2 * third + start + width] = high


def place(row, col, last):
    tile = jnp.minimum(lax.shift_right_logical(col, 7), last)
    return row, tile, col - tile * LANES


def add_window(accumulate, row, tile, offset, first, second):
    rows = first.shape[0]
    turn = jnp.bitwise_and(offset, LANES - 1)
    kept = lax.broadcasted_iota(jnp.int32, first.shape, 1) >= offset
    first = pltpu.roll(first, turn, 1)
    second = pltpu.roll(second, turn, 1)
    where = pl.ds(row, rows)
    accumulate[tile, where, :] += jnp.where(kept, first, 0.0)
    accumulate[tile + 1, where, :] += jnp.where(kept, second, first)
    accumulate[tile + 2, where, :] += jnp.where(kept, 0.0, second)


def fold_kernel(count, measured, gather_left, gather_right, folded, parts):
    size = measured.shape[1]

    def three(value):
        high = value.astype(BF16)
        rest = value - high.astype(F32)
        middle = rest.astype(BF16)
        return high, middle, (rest - middle.astype(F32)).astype(BF16)

    def step(slot, carry):
        for index, part in enumerate(three(measured[slot])):
            parts[:, index * size : (index + 1) * size] = part
        value = matmul(parts[...], gather_right[...])
        folded[slot] = matmul(gather_left[...], jnp.concatenate(three(value), axis=0))
        return carry

    lax.fori_loop(0, count[0], step, 0)


def own_notes(position, count):
    row = lax.broadcasted_iota(jnp.int32, (8, LANES), 0)
    lane = lax.broadcasted_iota(jnp.int32, (8, LANES), 1)
    notes = jnp.where(row == 2, count[0], 0)
    for slot in range(position.shape[1]):
        for axis in range(2):
            notes = jnp.where((row == axis) & (lane == slot), position[axis, slot], notes)
    return notes.astype(F32)


def edge_kernel(odd, position, count, tile_ref, x_first, x_second, y_first, y_second):
    half = LANES
    side = tile_ref.shape[1]
    odd_y, odd_x = odd[0] == 1, odd[1] == 1
    notes = own_notes(position, count)
    low, high = tile_ref[:, :, :half], tile_ref[:, :, side - half :]
    x_first[:, :side, :] = jnp.where(odd_x, high, low)
    x_second[:, :side, :] = jnp.where(odd_x, low, high)
    for out in (x_first, x_second):
        for plane in range(2):
            out[plane, side:, :] = notes
    low, high = tile_ref[:, :half, :], tile_ref[:, side - half :, :]
    y_first[...] = jnp.where(odd_y, high, low)
    y_second[...] = jnp.where(odd_y, low, high)


def corner_kernel(odd, position, count, x_first, x_second, first, second):
    half = LANES
    side = x_first.shape[1] - 8
    far = side - half
    odd_x = odd[1] == 1
    notes = own_notes(position, count)
    for out, odd_start in ((first, far), (second, 0)):
        rows = pl.ds(pl.multiple_of(jnp.where(odd[0] == 1, odd_start, far - odd_start), LANES), half)
        for index, (even_ref, odd_ref) in enumerate(((x_first, x_second), (x_second, x_first))):
            out[:, index, :half, :] = jnp.where(odd_x, odd_ref[:, rows, :], even_ref[:, rows, :])
            out[:, index, half : half + 8, :] = jnp.where(odd_x, odd_ref[:, side:, :], even_ref[:, side:, :])
            for plane in range(2):
                out[plane, index, half + 8 :, :] = notes


def slot_stages(row, tile, offset, live, probe, measured, left, right, canvas, grad, probe_sum, patch, rhs, lhs):
    size = probe.shape[1]
    half = size // 2
    near, far = slice(0, half), slice(half, size)
    turn = jnp.bitwise_and(LANES - offset, LANES - 1)
    kept = lax.broadcasted_iota(jnp.int32, (size, LANES), 1) < LANES - offset
    for plane in range(2):
        raw = [pltpu.roll(canvas[plane, tile + index, pl.ds(row, size), :], turn, 1) for index in range(3)]
        patch[plane, 0] = jnp.where(kept, raw[0], raw[1])
        patch[plane, 1] = jnp.where(kept, raw[1], raw[2])
    for index, columns in enumerate((near, far)):
        probe_re, probe_im = probe[0, :, columns], probe[1, :, columns]
        patch_re, patch_im = patch[0, index], patch[1, index]
        exit_re = probe_re * patch_re - probe_im * patch_im
        exit_im = probe_re * patch_im + probe_im * patch_re
        probe_sum[2, index] += (patch_re * patch_re + patch_im * patch_im) * live
        put_rows(rhs.at[0], 0, columns, exit_re[:half] + exit_re[half:])
        put_rows(rhs.at[0], half, columns, exit_im[:half] + exit_im[half:])
        put_rows(rhs.at[1], 0, columns, exit_re[:half] - exit_re[half:])
        put_rows(rhs.at[1], half, columns, exit_im[:half] - exit_im[half:])
    yield
    for parity in range(2):
        value = matmul(left[2 * parity], rhs[parity])
        rows = slice(parity * half, (parity + 1) * half)
        put_columns(lhs.at[0], rows, 0, value[:half, near] + value[:half, far])
        put_columns(lhs.at[0], rows, half, value[half:, near] + value[half:, far])
        put_columns(lhs.at[1], rows, 0, value[:half, near] - value[:half, far])
        put_columns(lhs.at[1], rows, half, value[half:, near] - value[half:, far])
        yield
    everything = slice(0, size)
    for parity in range(2):
        value = matmul(lhs[parity], right[2 * parity + 1])
        wave_re, wave_im = value[:, near], value[:, far]
        columns = slice(parity * half, (parity + 1) * half)
        excess = (wave_re * wave_re + wave_im * wave_im - measured[:, columns]) * live
        put_columns(lhs.at[parity], everything, 0, excess * wave_re)
        put_columns(lhs.at[parity], everything, half, excess * wave_im)
        yield
    back = []
    for parity in range(2):
        back.append(matmul(lhs[parity], right[2 * parity]))
    for parity in range(2):
        rows = slice(parity * half, (parity + 1) * half)
        put_rows(rhs.at[parity], 0, near, back[0][rows, near] + back[1][rows, near])
        put_rows(rhs.at[parity], half, near, back[0][rows, far] + back[1][rows, far])
        put_rows(rhs.at[parity], 0, far, back[0][rows, near] - back[1][rows, near])
        put_rows(rhs.at[parity], half, far, back[0][rows, far] - back[1][rows, far])
    yield
    even = matmul(left[1], rhs[0])
    odd = matmul(left[3], rhs[1])
    pieces = []
    for index, columns in enumerate((near, far)):
        chi_re, chi_im = (
            jnp.concatenate([even[rows, columns] + odd[rows, columns], even[rows, columns] - odd[rows, columns]], axis=0)
            for rows in (near, far)
        )
        probe_re, probe_im = probe[0, :, columns], probe[1, :, columns]
        patch_re, patch_im = patch[0, index], patch[1, index]
        probe_sum[0, index] += patch_re * chi_re + patch_im * chi_im
        probe_sum[1, index] += patch_re * chi_im - patch_im * chi_re
        pieces.append((probe_re * chi_re + probe_im * chi_im, probe_re * chi_im - probe_im * chi_re))
    for plane in range(2):
        add_window(grad.at[plane], row, tile, offset, pieces[0][plane], pieces[1][plane])
    yield


def run_slots(wanted, base, position, count, probe, folded, left, right, canvas, grad, probe_sum, order, patch, rhs, lhs):
    size = probe.shape[1]
    half = size // 2
    tiles = canvas.shape[1] - 2
    reach = tiles * LANES - size

    def pick(slot, found):
        row = position[0, slot]
        inside = (row >= 0) & (row <= reach)
        take = inside if wanted else jnp.logical_not(inside)

        @pl.when(take)
        def keep():
            order[found] = slot

        return found + jnp.where(take, 1, 0)

    total = lax.fori_loop(0, count[0], pick, 0)
    lanes = patch.shape[0]

    def step(group, carry):
        stages = []
        for lane in range(lanes):
            index = lanes * group + lane
            live = jnp.where(index < total, 1.0, 0.0)
            slot = order[jnp.minimum(index, total - 1)]
            row, tile, offset = place(position[0, slot] + base, position[1, slot] + half, tiles - 1)
            stages.append(slot_stages(
                row, tile, offset, live, probe, folded.at[slot], left, right, canvas, grad, probe_sum,
                patch.at[lane], rhs.at[lane], lhs.at[lane],
            ))
        for _ in zip(*stages):
            pass
        return carry

    lax.fori_loop(0, lax.div(total + (lanes - 1), lanes), step, 0)


def inner_kernel(odd, position, count, probe, folded, left, right, tile_ref, x_first, x_second, grad, probe_sum, canvas, *scratch):
    side = tile_ref.shape[1]
    tiles = side // LANES
    odd_x = odd[1] == 1
    for index in range(tiles):
        canvas[:, 1 + index] = tile_ref[:, :, index * LANES : (index + 1) * LANES]
    canvas[:, 0] = jnp.where(odd_x, x_second[:, :side, :], x_first[:, :side, :])
    canvas[:, 1 + tiles] = jnp.where(odd_x, x_first[:, :side, :], x_second[:, :side, :])
    grad[...] = jnp.zeros_like(grad)
    probe_sum[...] = jnp.zeros_like(probe_sum)
    run_slots(True, 0, position, count, probe, folded, left, right, canvas, grad, probe_sum, *scratch)


def outer_kernel(
    odd, position, count, probe, folded, left, right, tile_ref, x_first, x_second, y_first, y_second,
    corner_first, corner_second, grad_in, probe_sum_in,
    margin_first, margin_second, side_low, side_high, middle, sums, places,
    canvas, grad, probe_sum, sems, *scratch,
):
    size = probe.shape[1]
    half = size // 2
    side = tile_ref.shape[1]
    tiles = side // LANES
    inner = slice(half, half + side)
    odd_y, odd_x = odd[0] == 1, odd[1] == 1
    for index in range(tiles):
        columns = slice(index * LANES, (index + 1) * LANES)
        canvas[:, 1 + index, inner, :] = tile_ref[:, :, columns]
        canvas[:, 1 + index, :half, :] = jnp.where(odd_y, y_second[:, :, columns], y_first[:, :, columns])
        canvas[:, 1 + index, half + side :, :] = jnp.where(odd_y, y_first[:, :, columns], y_second[:, :, columns])
    canvas[:, 0, inner, :] = jnp.where(odd_x, x_second[:, :side, :], x_first[:, :side, :])
    canvas[:, 1 + tiles, inner, :] = jnp.where(odd_x, x_first[:, :side, :], x_second[:, :side, :])
    for index, tile in enumerate((0, 1 + tiles)):
        above, below = corner_first[:, index, :half, :], corner_second[:, index, :half, :]
        canvas[:, tile, :half, :] = jnp.where(odd_y, below, above)
        canvas[:, tile, half + side :, :] = jnp.where(odd_y, above, below)
    grad[:, :, :half, :] = jnp.zeros((2, tiles + 2, half, LANES), F32)
    grad[:, :, half + side :, :] = jnp.zeros((2, tiles + 2, half, LANES), F32)
    grad[:, :, inner, :] = grad_in[...]
    probe_sum[...] = probe_sum_in[...]
    run_slots(False, half, position, count, probe, folded, left, right, canvas, grad, probe_sum, *scratch)
    copies = []

    def send(source, target):
        copy = pltpu.make_async_copy(source, target, sems.at[len(copies)])
        copy.start()
        copies.append(copy)

    for out, odd_start in ((margin_first, half + side), (margin_second, 0)):
        rows = pl.ds(pl.multiple_of(jnp.where(odd_y, odd_start, half + side - odd_start), LANES), half)
        send(grad.at[:, :, rows, :], out)
    send(grad.at[:, 0, inner, :], side_low)
    send(grad.at[:, 1 + tiles, inner, :], side_high)
    send(grad.at[:, 1 : 1 + tiles, inner, :], middle)
    for plane in range(3):
        for index in range(2):
            sums[:, 2 * plane + index] = probe_sum[plane, index].reshape(size // 8, 8, LANES)
    beside, own = slice(half, half + 8), slice(half + 8, half + 16)
    for start, (even_ref, odd_ref) in ((0, (corner_first, corner_second)), (6, (corner_second, corner_first))):
        for index, (tile, rows) in enumerate(((0, beside), (0, own), (1, beside))):
            places[start + index] = jnp.where(odd_y, odd_ref[0, tile, rows, :], even_ref[0, tile, rows, :])
    places[3] = jnp.where(odd_x, x_second[0, side:, :], x_first[0, side:, :])
    places[4] = own_notes(position, count)
    places[5] = jnp.where(odd_x, x_first[0, side:, :], x_second[0, side:, :])
    for copy in copies:
        copy.wait()


def sides_kernel(odd, own_low, own_high, low_first, low_second, high_first, high_second, first, second):
    half = LANES
    side = own_low.shape[1]
    odd_y, odd_x = odd[0] == 1, odd[1] == 1
    for start in range(0, side, half):
        rows = slice(start, start + half)
        values = []
        for own, y_first, y_second in ((own_low, low_first, low_second), (own_high, high_first, high_second)):
            value = own[:, rows, :]
            if start == 0:
                value = value + jnp.where(odd_y, y_second[:, 0], y_first[:, 0])
            if start + half == side:
                value = value + jnp.where(odd_y, y_first[:, 0], y_second[:, 0])
            values.append(value)
        first[:, rows, :] = jnp.where(odd_x, values[1], values[0])
        second[:, rows, :] = jnp.where(odd_x, values[0], values[1])


def weight_kernel(numbers, probe, scale, power, weight):
    half = LANES
    side = scale.shape[1]
    tiles = side // LANES
    weight[...] = jnp.zeros_like(weight)
    for index in range(2):
        columns = slice(index * LANES, (index + 1) * LANES)
        power[index] = probe[0, :, columns] * probe[0, :, columns] + probe[1, :, columns] * probe[1, :, columns]
    for index in range(9):
        down, across = index // 3 - 1, index % 3 - 1

        def step(slot, carry):
            row = numbers[index, 0, slot].astype(jnp.int32) + (2 * half + down * side)
            col = numbers[index, 1, slot].astype(jnp.int32) + (2 * half + across * side)
            reach = side + 2 * half

            @pl.when((row > 0) & (row < reach) & (col > 0) & (col < reach))
            def add():
                at, tile, offset = place(row, col, tiles + 1)
                add_window(weight, at, tile, offset, power[0], power[1])

            return carry

        lax.fori_loop(0, numbers[index, 2, 0].astype(jnp.int32), step, 0)
    for index in range(tiles):
        scale[index] = 1.0 / (weight[2 + index, 2 * half : 2 * half + side, :] + 1.0)


def update_kernel(odd, tile_ref, grad, y_first, y_second, scale, out):
    half = LANES
    side = tile_ref.shape[1]
    odd_y = odd[0] == 1
    for plane in range(2):
        for start in range(0, side, half):
            rows = slice(start, start + half)
            value = grad[plane, 0, rows, :]
            if start == 0:
                value = value + jnp.where(odd_y, y_second[plane, 0], y_first[plane, 0])
            if start + half == side:
                value = value + jnp.where(odd_y, y_first[plane, 0], y_second[plane, 0])
            out[plane, rows, :] = tile_ref[plane, rows, :] - value * scale[0, rows, :]


def column_kernel(odd, before, x_first, x_second, scale, out):
    use_first = odd[1] == pl.program_id(0)
    for plane in range(2):
        out[plane] = before[plane] - jnp.where(use_first, x_first[plane], x_second[plane]) * scale[0]


def plane_kernel(parts, after, out):
    out[...] = jnp.broadcast_to(jnp.sum(parts[...], axis=0)[None], out.shape)


def probe_kernel(index, parts, probe, out):
    total = jnp.sum(parts[...], axis=0)
    rows = pl.ds(pl.multiple_of(index[0] * 8, 8), 8)
    for tile in range(2):
        root = jnp.sqrt(total[4 + tile] + 1.0)
        for plane in range(2):
            new = probe[plane, rows, tile * LANES : (tile + 1) * LANES] - total[2 * plane + tile] / root
            out[:, 2 * plane + tile] = jnp.broadcast_to(new[None], (out.shape[0], 8, LANES))


def join_kernel(pieces, out):
    for plane in range(2):
        for tile in range(2):
            value = pieces[:, 2 * plane + tile]
            out[plane, :, tile * LANES : (tile + 1) * LANES] = value.reshape(out.shape[1], LANES)


def swap(first, second, axis):
    count = lax.axis_size(axis)
    across = [pair for low in range(1, count - 1, 2) for pair in ((low, low + 1), (low + 1, low))]
    return lax.ppermute(first, axis, across), lax.ppermute(second, axis, [(index, index ^ 1) for index in range(count)])


def params(mib):
    return pltpu.CompilerParams(vmem_limit_bytes=mib * 2**20)


def cost(mib):
    return pl.CostEstimate(flops=0, bytes_accessed=mib * 2**20, transcendentals=0)


def solution(mesh):
    rows, cols = mesh.shape["ty"], mesh.shape["tx"]
    near_y, near_z = 8, 4
    planes = [
        [(8 * high + row) * cols + near_z * x + low for row in range(near_y) for x in range(cols // near_z)]
        for high in range(rows // near_y)
        for low in range(near_z)
    ]
    lines = [list(line) for line in zip(*planes)]

    def trade(pieces, groups):
        return lax.all_to_all(pieces, ("ty", "tx"), 0, 0, axis_index_groups=groups, tiled=True)

    def per_device(object_field, probe, intensity, positions, counts):
        side = object_field.shape[1]
        size = probe.shape[1]
        half = size // 2
        slots = intensity.shape[2]
        tiles = side // LANES
        position = positions[:, 0, 0, :]
        count = counts[0]
        row, col = lax.axis_index("ty"), lax.axis_index("tx")
        piece = jnp.bitwise_and(row, near_y - 1) * (cols // near_z) + lax.shift_right_logical(col, 2)
        piece = piece.reshape(1).astype(jnp.int32)
        left, right = (jnp.asarray(table) for table in half_tables(size))
        gather_left, gather_right = (jnp.asarray(table) for table in parity_tables(size))

        odd = jnp.bitwise_and(jnp.stack([row, col]), 1).astype(jnp.int32)

        strip = jax.ShapeDtypeStruct((2, side + 8, LANES), F32)
        edge = jax.ShapeDtypeStruct((2, half, side), F32)
        x_first, x_second, y_first, y_second = pl.pallas_call(
            edge_kernel,
            out_shape=(strip, strip, edge, edge),
            in_specs=[SMEM] * 3 + [VMEM],
            out_specs=(VMEM,) * 4,
            compiler_params=params(6),
            cost_estimate=cost(4),
            name="edges",
        )(odd, position, count, object_field)
        x_first, x_second = swap(x_first, x_second, "tx")
        y_first, y_second = swap(y_first, y_second, "ty")
        folded = pl.pallas_call(
            fold_kernel,
            out_shape=jax.ShapeDtypeStruct((slots, size, size), F32),
            in_specs=[SMEM, VMEM, VMEM, VMEM],
            out_specs=VMEM,
            scratch_shapes=[pltpu.VMEM((size, 3 * size), BF16)],
            compiler_params=params(8),
            cost_estimate=cost(6),
            name="fold",
        )(count, intensity[0, 0], gather_left, gather_right)
        corner = jax.ShapeDtypeStruct((2, 2, half + 16, LANES), F32)
        corners = pl.pallas_call(
            corner_kernel,
            out_shape=(corner, corner),
            in_specs=[SMEM] * 3 + [VMEM] * 2,
            out_specs=(VMEM, VMEM),
            compiler_params=params(4),
            cost_estimate=cost(4),
            name="corners",
        )(odd, position, count, x_first, x_second)
        corners = swap(*corners, "ty")

        members = len(planes[0])
        lanes = 2
        scratch = [
            pltpu.SMEM((slots,), jnp.int32),
            pltpu.VMEM((lanes, 2, 2, size, LANES), F32),
            pltpu.VMEM((lanes, 2, 3 * size, size), BF16),
            pltpu.VMEM((lanes, 2, size, 3 * size), BF16),
        ]
        grad, probe_sum = pl.pallas_call(
            inner_kernel,
            out_shape=(
                jax.ShapeDtypeStruct((2, tiles + 2, side, LANES), F32),
                jax.ShapeDtypeStruct((3, 2, size, LANES), F32),
            ),
            in_specs=[SMEM] * 3 + [VMEM] * 7,
            out_specs=(VMEM,) * 2,
            scratch_shapes=[pltpu.VMEM((2, tiles + 2, side, LANES), F32)] + scratch,
            compiler_params=params(22),
            cost_estimate=cost(16),
            name="inner_slots",
        )(odd, position, count, probe, folded, left, right, object_field, x_first, x_second)
        margin = pltpu.HBM((2, tiles + 2, half, LANES), F32)
        column = pltpu.HBM((2, side, LANES), F32)
        margin_first, margin_second, side_low, side_high, middle, sums, places = pl.pallas_call(
            outer_kernel,
            out_shape=(
                margin, margin, column, column,
                pltpu.HBM((2, tiles, side, LANES), F32),
                pltpu.HBM((members, 6, 8, LANES), F32),
                jax.ShapeDtypeStruct((9, 8, LANES), F32),
            ),
            in_specs=[SMEM] * 3 + [VMEM] * 13,
            out_specs=(HBM,) * 5 + (VMEM, VMEM),
            scratch_shapes=[
                pltpu.VMEM((2, tiles + 2, side + size, LANES), F32),
                pltpu.VMEM((2, tiles + 2, side + size, LANES), F32),
                pltpu.VMEM((3, 2, size, LANES), F32),
                pltpu.SemaphoreType.DMA((5,)),
            ] + scratch,
            compiler_params=params(30),
            cost_estimate=cost(16),
            name="outer_slots",
        )(
            odd, position, count, probe, folded, left, right, object_field, x_first, x_second, y_first, y_second,
            *corners, grad, probe_sum,
        )

        margin_first, margin_second = swap(margin_first, margin_second, "ty")
        scale = pl.pallas_call(
            weight_kernel,
            out_shape=jax.ShapeDtypeStruct((tiles, side, LANES), F32),
            in_specs=[SMEM, VMEM],
            out_specs=VMEM,
            scratch_shapes=[
                pltpu.VMEM((2, size, LANES), F32),
                pltpu.VMEM((tiles + 4, side + 2 * size, LANES), F32),
            ],
            compiler_params=params(8),
            cost_estimate=cost(8),
            name="weights",
        )(places, probe)
        parts = trade(sums, planes)
        strip = jax.ShapeDtypeStruct((2, side, LANES), F32)
        whole = pl.BlockSpec((2, side, LANES), lambda index: (0, 0, 0))
        first_tile = pl.BlockSpec((2, 1, half, LANES), lambda index: (0, 0, 0, 0))
        last_tile = pl.BlockSpec((2, 1, half, LANES), lambda index: (0, tiles + 1, 0, 0))
        x_first, x_second = pl.pallas_call(
            sides_kernel,
            out_shape=(strip, strip),
            grid=(1,),
            in_specs=[SMEM, whole, whole, first_tile, first_tile, last_tile, last_tile],
            out_specs=(whole, whole),
            compiler_params=params(8),
            cost_estimate=cost(16),
            name="sides",
        )(odd, side_low, side_high, margin_first, margin_second, margin_first, margin_second)
        x_first, x_second = swap(x_first, x_second, "tx")

        parts = pl.pallas_call(
            plane_kernel,
            out_shape=pltpu.HBM((len(lines[0]), 6, 8, LANES), F32),
            in_specs=[VMEM, HBM],
            out_specs=VMEM,
            compiler_params=params(6),
            cost_estimate=cost(2),
            name="plane_sum",
        )(parts, scale)
        parts = trade(parts, lines)
        pieces = pl.pallas_call(
            probe_kernel,
            out_shape=pltpu.HBM((members, 4, 8, LANES), F32),
            in_specs=[SMEM, VMEM, VMEM],
            out_specs=VMEM,
            compiler_params=params(6),
            cost_estimate=cost(2),
            name="probe_rows",
        )(piece, parts, probe)
        probe_new = pl.pallas_call(
            join_kernel,
            out_shape=jax.ShapeDtypeStruct(probe.shape, F32),
            in_specs=[VMEM],
            out_specs=VMEM,
            compiler_params=params(6),
            cost_estimate=cost(2),
            name="join",
        )(trade(pieces, planes))

        column = pl.BlockSpec((2, side, LANES), lambda index: (0, 0, index))
        flat = pl.BlockSpec((2, 1, half, LANES), lambda index: (0, index + 1, 0, 0))
        object_new = pl.pallas_call(
            update_kernel,
            out_shape=jax.ShapeDtypeStruct(object_field.shape, F32),
            grid=(tiles,),
            in_specs=[
                SMEM, column, pl.BlockSpec((2, 1, side, LANES), lambda index: (0, index, 0, 0)), flat, flat,
                pl.BlockSpec((1, side, LANES), lambda index: (index, 0, 0)),
            ],
            out_specs=column,
            compiler_params=params(8),
            cost_estimate=cost(8),
            name="update",
        )(odd, object_field, middle, margin_first, margin_second, scale)
        ends = pl.BlockSpec((2, side, LANES), lambda index: (0, 0, index * (tiles - 1)))
        object_new = pl.pallas_call(
            column_kernel,
            out_shape=jax.ShapeDtypeStruct(object_field.shape, F32),
            grid=(2,),
            in_specs=[SMEM, ends, whole, whole, pl.BlockSpec((1, side, LANES), lambda index: (index * (tiles - 1), 0, 0))],
            out_specs=ends,
            input_output_aliases={1: 0},
            compiler_params=params(8),
            name="columns",
        )(odd, object_new, x_first, x_second, scale)
        return (object_new, probe_new)

    in_specs = (
        P(None, "ty", "tx"),
        P(),
        P("ty", "tx", None, None, None),
        P(None, "ty", "tx", None),
        P("ty", "tx"),
    )
    out_specs = (P(None, "ty", "tx"), P())
    return jax.shard_map(per_device, mesh=mesh, in_specs=in_specs, out_specs=out_specs, check_vma=False)
```

```python
import numpy as np
import ml_dtypes
import jax
import jax.numpy as jnp
from jax import lax
from jax.experimental import pallas as pl
from jax.experimental.pallas import tpu as pltpu
from jax.sharding import PartitionSpec as P

BF16 = jnp.bfloat16
F32 = jnp.float32
LANES = 128
VMEM = pl.BlockSpec(memory_space=pltpu.VMEM)
SMEM = pl.BlockSpec(memory_space=pltpu.SMEM)
HBM = pl.BlockSpec(memory_space=pltpu.HBM)
def split_host(table):
    high = table.astype(ml_dtypes.bfloat16)
    low = (table - high.astype(np.float64)).astype(ml_dtypes.bfloat16)
    return high, low


def half_tables(size):
    half = size // 2
    left, right = [], []
    for parity in range(2):
        product = (2 * np.arange(half)[:, None] + parity) * np.arange(half)[None, :] % size
        angle = 2.0 * np.pi * product / size
        cos, sin = np.cos(angle) / np.sqrt(size), np.sin(angle) / np.sqrt(size)
        base = np.block([[cos, sin], [-sin, cos]])
        for table in (base, base.T):
            high, low = split_host(table)
            left.append(np.concatenate([high, high, low], axis=1))
            right.append(np.concatenate([high, high, low], axis=0))
    return np.stack(left), np.stack(right)


def parity_tables(size):
    order = np.concatenate([np.arange(0, size, 2), np.arange(1, size, 2)])
    gather = np.eye(size)[order].astype(ml_dtypes.bfloat16)
    return np.concatenate([gather] * 3, axis=1), np.concatenate([gather.T] * 3, axis=0)


def matmul(left, right):
    return jnp.dot(left, right, preferred_element_type=F32)


def split(value):
    high = value.astype(BF16)
    return high, (value - high.astype(F32)).astype(BF16)


def put_rows(ref, start, columns, value):
    rows = value.shape[0]
    high, low = split(value)
    third = ref.shape[0] // 3
    ref[start : start + rows, columns] = high
    ref[third + start : third + start + rows, columns] = low
    ref[2 * third + start : 2 * third + start + rows, columns] = high


def put_columns(ref, rows, start, value):
    width = value.shape[1]
    high, low = split(value)
    third = ref.shape[1] // 3
    ref[rows, start : start + width] = high
    ref[rows, third + start : third + start + width] = low
    ref[rows, 2 * third + start : 2 * third + start + width] = high


def place(row, col, last):
    tile = jnp.minimum(lax.shift_right_logical(col, 7), last)
    return row, tile, col - tile * LANES


def add_window(accumulate, row, tile, offset, first, second):
    rows = first.shape[0]
    turn = jnp.bitwise_and(offset, LANES - 1)
    kept = lax.broadcasted_iota(jnp.int32, first.shape, 1) >= offset
    first = pltpu.roll(first, turn, 1)
    second = pltpu.roll(second, turn, 1)
    where = pl.ds(row, rows)
    accumulate[tile, where, :] += jnp.where(kept, first, 0.0)
    accumulate[tile + 1, where, :] += jnp.where(kept, second, first)
    accumulate[tile + 2, where, :] += jnp.where(kept, 0.0, second)


def fold_kernel(count, measured, gather_left, gather_right, folded, parts):
    size = measured.shape[1]

    def three(value):
        high = value.astype(BF16)
        rest = value - high.astype(F32)
        middle = rest.astype(BF16)
        return high, middle, (rest - middle.astype(F32)).astype(BF16)

    def step(slot, carry):
        for index, part in enumerate(three(measured[slot])):
            parts[:, index * size : (index + 1) * size] = part
        value = matmul(parts[...], gather_right[...])
        folded[slot] = matmul(gather_left[...], jnp.concatenate(three(value), axis=0))
        return carry

    lax.fori_loop(0, count[0], step, 0)


def own_notes(position, count):
    row = lax.broadcasted_iota(jnp.int32, (8, LANES), 0)
    lane = lax.broadcasted_iota(jnp.int32, (8, LANES), 1)
    notes = jnp.where(row == 2, count[0], 0)
    for slot in range(position.shape[1]):
        for axis in range(2):
            notes = jnp.where((row == axis) & (lane == slot), position[axis, slot], notes)
    return notes.astype(F32)


def edge_kernel(odd, position, count, tile_ref, x_first, x_second, y_first, y_second):
    half = LANES
    side = tile_ref.shape[1]
    odd_y, odd_x = odd[0] == 1, odd[1] == 1
    notes = own_notes(position, count)
    low, high = tile_ref[:, :, :half], tile_ref[:, :, side - half :]
    x_first[:, :side, :] = jnp.where(odd_x, high, low)
    x_second[:, :side, :] = jnp.where(odd_x, low, high)
    for out in (x_first, x_second):
        for plane in range(2):
            out[plane, side:, :] = notes
    low, high = tile_ref[:, :half, :], tile_ref[:, side - half :, :]
    y_first[...] = jnp.where(odd_y, high, low)
    y_second[...] = jnp.where(odd_y, low, high)


def corner_kernel(odd, position, count, x_first, x_second, after, first, second):
    half = LANES
    side = x_first.shape[1] - 8
    far = side - half
    odd_x = odd[1] == 1
    notes = own_notes(position, count)
    for out, odd_start in ((first, far), (second, 0)):
        rows = pl.ds(pl.multiple_of(jnp.where(odd[0] == 1, odd_start, far - odd_start), LANES), half)
        for index, (even_ref, odd_ref) in enumerate(((x_first, x_second), (x_second, x_first))):
            out[:, index, :half, :] = jnp.where(odd_x, odd_ref[:, rows, :], even_ref[:, rows, :])
            out[:, index, half : half + 8, :] = jnp.where(odd_x, odd_ref[:, side:, :], even_ref[:, side:, :])
            for plane in range(2):
                out[plane, index, half + 8 :, :] = notes


def slot_stages(row, tile, offset, live, probe, measured, left, right, canvas, grad, probe_sum, patch, rhs, lhs):
    size = probe.shape[1]
    half = size // 2
    near, far = slice(0, half), slice(half, size)
    turn = jnp.bitwise_and(LANES - offset, LANES - 1)
    kept = lax.broadcasted_iota(jnp.int32, (size, LANES), 1) < LANES - offset
    for plane in range(2):
        raw = [pltpu.roll(canvas[plane, tile + index, pl.ds(row, size), :], turn, 1) for index in range(3)]
        patch[plane, 0] = jnp.where(kept, raw[0], raw[1])
        patch[plane, 1] = jnp.where(kept, raw[1], raw[2])
    for index, columns in enumerate((near, far)):
        probe_re, probe_im = probe[0, :, columns], probe[1, :, columns]
        patch_re, patch_im = patch[0, index], patch[1, index]
        exit_re = probe_re * patch_re - probe_im * patch_im
        exit_im = probe_re * patch_im + probe_im * patch_re
        probe_sum[2, index] += (patch_re * patch_re + patch_im * patch_im) * live
        put_rows(rhs.at[0], 0, columns, exit_re[:half] + exit_re[half:])
        put_rows(rhs.at[0], half, columns, exit_im[:half] + exit_im[half:])
        put_rows(rhs.at[1], 0, columns, exit_re[:half] - exit_re[half:])
        put_rows(rhs.at[1], half, columns, exit_im[:half] - exit_im[half:])
    yield
    for parity in range(2):
        value = matmul(left[2 * parity], rhs[parity])
        rows = slice(parity * half, (parity + 1) * half)
        put_columns(lhs.at[0], rows, 0, value[:half, near] + value[:half, far])
        put_columns(lhs.at[0], rows, half, value[half:, near] + value[half:, far])
        put_columns(lhs.at[1], rows, 0, value[:half, near] - value[:half, far])
        put_columns(lhs.at[1], rows, half, value[half:, near] - value[half:, far])
        yield
    everything = slice(0, size)
    for parity in range(2):
        value = matmul(lhs[parity], right[2 * parity + 1])
        wave_re, wave_im = value[:, near], value[:, far]
        columns = slice(parity * half, (parity + 1) * half)
        excess = (wave_re * wave_re + wave_im * wave_im - measured[:, columns]) * live
        put_columns(lhs.at[parity], everything, 0, excess * wave_re)
        put_columns(lhs.at[parity], everything, half, excess * wave_im)
        yield
    back = []
    for parity in range(2):
        back.append(matmul(lhs[parity], right[2 * parity]))
    for parity in range(2):
        rows = slice(parity * half, (parity + 1) * half)
        put_rows(rhs.at[parity], 0, near, back[0][rows, near] + back[1][rows, near])
        put_rows(rhs.at[parity], half, near, back[0][rows, far] + back[1][rows, far])
        put_rows(rhs.at[parity], 0, far, back[0][rows, near] - back[1][rows, near])
        put_rows(rhs.at[parity], half, far, back[0][rows, far] - back[1][rows, far])
    yield
    even = matmul(left[1], rhs[0])
    odd = matmul(left[3], rhs[1])
    pieces = []
    for index, columns in enumerate((near, far)):
        chi_re, chi_im = (
            jnp.concatenate([even[rows, columns] + odd[rows, columns], even[rows, columns] - odd[rows, columns]], axis=0)
            for rows in (near, far)
        )
        probe_re, probe_im = probe[0, :, columns], probe[1, :, columns]
        patch_re, patch_im = patch[0, index], patch[1, index]
        probe_sum[0, index] += patch_re * chi_re + patch_im * chi_im
        probe_sum[1, index] += patch_re * chi_im - patch_im * chi_re
        pieces.append((probe_re * chi_re + probe_im * chi_im, probe_re * chi_im - probe_im * chi_re))
    for plane in range(2):
        add_window(grad.at[plane], row, tile, offset, pieces[0][plane], pieces[1][plane])
    yield


def run_slots(wanted, base, position, count, probe, folded, left, right, canvas, grad, probe_sum, order, patch, rhs, lhs):
    size = probe.shape[1]
    half = size // 2
    tiles = canvas.shape[1] - 2
    reach = tiles * LANES - size

    def pick(slot, found):
        row = position[0, slot]
        inside = (row >= 0) & (row <= reach)
        take = inside if wanted else jnp.logical_not(inside)

        @pl.when(take)
        def keep():
            order[found] = slot

        return found + jnp.where(take, 1, 0)

    total = lax.fori_loop(0, count[0], pick, 0)
    lanes = patch.shape[0]

    def step(group, carry):
        stages = []
        for lane in range(lanes):
            index = lanes * group + lane
            live = jnp.where(index < total, 1.0, 0.0)
            slot = order[jnp.minimum(index, total - 1)]
            row, tile, offset = place(position[0, slot] + base, position[1, slot] + half, tiles - 1)
            stages.append(slot_stages(
                row, tile, offset, live, probe, folded.at[slot], left, right, canvas, grad, probe_sum,
                patch.at[lane], rhs.at[lane], lhs.at[lane],
            ))
        for _ in zip(*stages):
            pass
        return carry

    lax.fori_loop(0, lax.div(total + (lanes - 1), lanes), step, 0)


def inner_kernel(odd, position, count, probe, folded, left, right, tile_ref, x_first, x_second, grad, probe_sum, canvas, *scratch):
    side = tile_ref.shape[1]
    tiles = side // LANES
    odd_x = odd[1] == 1
    for index in range(tiles):
        canvas[:, 1 + index] = tile_ref[:, :, index * LANES : (index + 1) * LANES]
    canvas[:, 0] = jnp.where(odd_x, x_second[:, :side, :], x_first[:, :side, :])
    canvas[:, 1 + tiles] = jnp.where(odd_x, x_first[:, :side, :], x_second[:, :side, :])
    grad[...] = jnp.zeros_like(grad)
    probe_sum[...] = jnp.zeros_like(probe_sum)
    run_slots(True, 0, position, count, probe, folded, left, right, canvas, grad, probe_sum, *scratch)


def outer_kernel(
    odd, position, count, probe, folded, left, right, tile_ref, x_first, x_second, y_first, y_second,
    corner_first, corner_second, grad_in, probe_sum_in,
    margin_first, margin_second, side_low, side_high, middle, sums, places,
    canvas, grad, probe_sum, sems, *scratch,
):
    size = probe.shape[1]
    half = size // 2
    side = tile_ref.shape[1]
    tiles = side // LANES
    inner = slice(half, half + side)
    odd_y, odd_x = odd[0] == 1, odd[1] == 1
    for index in range(tiles):
        columns = slice(index * LANES, (index + 1) * LANES)
        canvas[:, 1 + index, inner, :] = tile_ref[:, :, columns]
        canvas[:, 1 + index, :half, :] = jnp.where(odd_y, y_second[:, :, columns], y_first[:, :, columns])
        canvas[:, 1 + index, half + side :, :] = jnp.where(odd_y, y_first[:, :, columns], y_second[:, :, columns])
    canvas[:, 0, inner, :] = jnp.where(odd_x, x_second[:, :side, :], x_first[:, :side, :])
    canvas[:, 1 + tiles, inner, :] = jnp.where(odd_x, x_first[:, :side, :], x_second[:, :side, :])
    for index, tile in enumerate((0, 1 + tiles)):
        above, below = corner_first[:, index, :half, :], corner_second[:, index, :half, :]
        canvas[:, tile, :half, :] = jnp.where(odd_y, below, above)
        canvas[:, tile, half + side :, :] = jnp.where(odd_y, above, below)
    grad[:, :, :half, :] = jnp.zeros((2, tiles + 2, half, LANES), F32)
    grad[:, :, half + side :, :] = jnp.zeros((2, tiles + 2, half, LANES), F32)
    grad[:, :, inner, :] = grad_in[...]
    probe_sum[...] = probe_sum_in[...]
    run_slots(False, half, position, count, probe, folded, left, right, canvas, grad, probe_sum, *scratch)
    copies = []

    def send(source, target):
        copy = pltpu.make_async_copy(source, target, sems.at[len(copies)])
        copy.start()
        copies.append(copy)

    for out, odd_start in ((margin_first, half + side), (margin_second, 0)):
        rows = pl.ds(pl.multiple_of(jnp.where(odd_y, odd_start, half + side - odd_start), LANES), half)
        send(grad.at[:, :, rows, :], out)
    send(grad.at[:, 0, inner, :], side_low)
    send(grad.at[:, 1 + tiles, inner, :], side_high)
    send(grad.at[:, 1 : 1 + tiles, inner, :], middle)
    for plane in range(3):
        for index in range(2):
            sums[:, 2 * plane + index] = probe_sum[plane, index].reshape(size // 8, 8, LANES)
    beside, own = slice(half, half + 8), slice(half + 8, half + 16)
    for start, (even_ref, odd_ref) in ((0, (corner_first, corner_second)), (6, (corner_second, corner_first))):
        for index, (tile, rows) in enumerate(((0, beside), (0, own), (1, beside))):
            places[start + index] = jnp.where(odd_y, odd_ref[0, tile, rows, :], even_ref[0, tile, rows, :])
    places[3] = jnp.where(odd_x, x_second[0, side:, :], x_first[0, side:, :])
    places[4] = own_notes(position, count)
    places[5] = jnp.where(odd_x, x_first[0, side:, :], x_second[0, side:, :])
    for copy in copies:
        copy.wait()


def sides_kernel(odd, own_low, own_high, low_first, low_second, high_first, high_second, first, second, token):
    half = LANES
    side = own_low.shape[1]
    odd_y, odd_x = odd[0] == 1, odd[1] == 1
    for start in range(0, side, half):
        rows = slice(start, start + half)
        values = []
        for own, y_first, y_second in ((own_low, low_first, low_second), (own_high, high_first, high_second)):
            value = own[:, rows, :]
            if start == 0:
                value = value + jnp.where(odd_y, y_second[:, 0], y_first[:, 0])
            if start + half == side:
                value = value + jnp.where(odd_y, y_first[:, 0], y_second[:, 0])
            values.append(value)
        first[:, rows, :] = jnp.where(odd_x, values[1], values[0])
        second[:, rows, :] = jnp.where(odd_x, values[0], values[1])
    token[...] = jnp.zeros_like(token)


def weight_kernel(numbers, probe, scale, power, weight):
    half = LANES
    side = scale.shape[1]
    tiles = side // LANES
    weight[...] = jnp.zeros_like(weight)
    for index in range(2):
        columns = slice(index * LANES, (index + 1) * LANES)
        power[index] = probe[0, :, columns] * probe[0, :, columns] + probe[1, :, columns] * probe[1, :, columns]
    for index in range(9):
        down, across = index // 3 - 1, index % 3 - 1

        def step(slot, carry):
            row = numbers[index, 0, slot].astype(jnp.int32) + (2 * half + down * side)
            col = numbers[index, 1, slot].astype(jnp.int32) + (2 * half + across * side)
            reach = side + 2 * half

            @pl.when((row > 0) & (row < reach) & (col > 0) & (col < reach))
            def add():
                at, tile, offset = place(row, col, tiles + 1)
                add_window(weight, at, tile, offset, power[0], power[1])

            return carry

        lax.fori_loop(0, numbers[index, 2, 0].astype(jnp.int32), step, 0)
    for index in range(tiles):
        scale[index] = 1.0 / (weight[2 + index, 2 * half : 2 * half + side, :] + 1.0)


def update_kernel(odd, tile_ref, grad, y_first, y_second, scale, out):
    half = LANES
    side = tile_ref.shape[1]
    odd_y = odd[0] == 1
    for plane in range(2):
        for start in range(0, side, half):
            rows = slice(start, start + half)
            value = grad[plane, 0, rows, :]
            if start == 0:
                value = value + jnp.where(odd_y, y_second[plane, 0], y_first[plane, 0])
            if start + half == side:
                value = value + jnp.where(odd_y, y_first[plane, 0], y_second[plane, 0])
            out[plane, rows, :] = tile_ref[plane, rows, :] - value * scale[0, rows, :]


def column_kernel(odd, before, x_first, x_second, scale, out):
    use_first = odd[1] == pl.program_id(0)
    for plane in range(2):
        out[plane] = before[plane] - jnp.where(use_first, x_first[plane], x_second[plane]) * scale[0]


def plane_kernel(parts, after, later, out):
    out[...] = jnp.broadcast_to(jnp.sum(parts[...], axis=0)[None], out.shape)


def probe_kernel(index, parts, probe, out):
    total = jnp.sum(parts[...], axis=0)
    rows = pl.ds(pl.multiple_of(index[0] * 8, 8), 8)
    for tile in range(2):
        root = jnp.sqrt(total[4 + tile] + 1.0)
        for plane in range(2):
            new = probe[plane, rows, tile * LANES : (tile + 1) * LANES] - total[2 * plane + tile] / root
            out[:, 2 * plane + tile] = jnp.broadcast_to(new[None], (out.shape[0], 8, LANES))


def join_kernel(pieces, out):
    for plane in range(2):
        for tile in range(2):
            value = pieces[:, 2 * plane + tile]
            out[plane, :, tile * LANES : (tile + 1) * LANES] = value.reshape(out.shape[1], LANES)


def swap(first, second, axis):
    count = lax.axis_size(axis)
    across = [pair for low in range(1, count - 1, 2) for pair in ((low, low + 1), (low + 1, low))]
    return lax.ppermute(first, axis, across), lax.ppermute(second, axis, [(index, index ^ 1) for index in range(count)])


def keep(value):
    return pltpu.with_memory_space_constraint(value, pltpu.HBM)


def params(mib):
    return pltpu.CompilerParams(vmem_limit_bytes=mib * 2**20)


def cost(mib):
    return pl.CostEstimate(flops=0, bytes_accessed=mib * 2**20, transcendentals=0)


def solution(mesh):
    rows, cols = mesh.shape["ty"], mesh.shape["tx"]
    near_y, near_z = 8, 4
    planes = [
        [(8 * high + row) * cols + near_z * x + low for row in range(near_y) for x in range(cols // near_z)]
        for high in range(rows // near_y)
        for low in range(near_z)
    ]
    lines = [list(line) for line in zip(*planes)]

    def trade(pieces, groups):
        return lax.all_to_all(pieces, ("ty", "tx"), 0, 0, axis_index_groups=groups, tiled=True)

    def per_device(object_field, probe, intensity, positions, counts):
        side = object_field.shape[1]
        size = probe.shape[1]
        half = size // 2
        slots = intensity.shape[2]
        tiles = side // LANES
        position = positions[:, 0, 0, :]
        count = counts[0]
        row, col = lax.axis_index("ty"), lax.axis_index("tx")
        piece = jnp.bitwise_and(row, near_y - 1) * (cols // near_z) + lax.shift_right_logical(col, 2)
        piece = piece.reshape(1).astype(jnp.int32)
        left, right = (jnp.asarray(table) for table in half_tables(size))
        gather_left, gather_right = (jnp.asarray(table) for table in parity_tables(size))

        odd = jnp.bitwise_and(jnp.stack([row, col]), 1).astype(jnp.int32)

        strip = jax.ShapeDtypeStruct((2, side + 8, LANES), F32)
        edge = jax.ShapeDtypeStruct((2, half, side), F32)
        x_first, x_second, y_first, y_second = pl.pallas_call(
            edge_kernel,
            out_shape=(strip, strip, edge, edge),
            in_specs=[SMEM] * 3 + [VMEM],
            out_specs=(VMEM,) * 4,
            compiler_params=params(6),
            cost_estimate=cost(4),
            name="edges",
        )(odd, position, count, object_field)
        x_first, x_second = swap(x_first, x_second, "tx")
        y_first, y_second = swap(y_first, y_second, "ty")
        folded = pl.pallas_call(
            fold_kernel,
            out_shape=jax.ShapeDtypeStruct((slots, size, size), F32),
            in_specs=[SMEM, VMEM, VMEM, VMEM],
            out_specs=VMEM,
            scratch_shapes=[pltpu.VMEM((size, 3 * size), BF16)],
            compiler_params=params(8),
            cost_estimate=cost(6),
            name="fold",
        )(count, intensity[0, 0], gather_left, gather_right)
        corner = jax.ShapeDtypeStruct((2, 2, half + 16, LANES), F32)
        corners = pl.pallas_call(
            corner_kernel,
            out_shape=(corner, corner),
            in_specs=[SMEM] * 3 + [VMEM] * 2 + [HBM],
            out_specs=(VMEM, VMEM),
            compiler_params=params(4),
            cost_estimate=cost(4),
            name="corners",
        )(odd, position, count, x_first, x_second, folded)
        corners = swap(*corners, "ty")

        members = len(planes[0])
        lanes = 2
        scratch = [
            pltpu.SMEM((slots,), jnp.int32),
            pltpu.VMEM((lanes, 2, 2, size, LANES), F32),
            pltpu.VMEM((lanes, 2, 3 * size, size), BF16),
            pltpu.VMEM((lanes, 2, size, 3 * size), BF16),
        ]
        grad, probe_sum = pl.pallas_call(
            inner_kernel,
            out_shape=(
                jax.ShapeDtypeStruct((2, tiles + 2, side, LANES), F32),
                jax.ShapeDtypeStruct((3, 2, size, LANES), F32),
            ),
            in_specs=[SMEM] * 3 + [VMEM] * 7,
            out_specs=(VMEM,) * 2,
            scratch_shapes=[pltpu.VMEM((2, tiles + 2, side, LANES), F32)] + scratch,
            compiler_params=params(22),
            cost_estimate=cost(16),
            name="inner_slots",
        )(odd, position, count, probe, folded, left, right, object_field, x_first, x_second)
        margin = pltpu.HBM((2, tiles + 2, half, LANES), F32)
        column = pltpu.HBM((2, side, LANES), F32)
        margin_first, margin_second, side_low, side_high, middle, sums, places = pl.pallas_call(
            outer_kernel,
            out_shape=(
                margin, margin, column, column,
                pltpu.HBM((2, tiles, side, LANES), F32),
                pltpu.HBM((members, 6, 8, LANES), F32),
                jax.ShapeDtypeStruct((9, 8, LANES), F32),
            ),
            in_specs=[SMEM] * 3 + [VMEM] * 13,
            out_specs=(HBM,) * 5 + (VMEM, VMEM),
            scratch_shapes=[
                pltpu.VMEM((2, tiles + 2, side + size, LANES), F32),
                pltpu.VMEM((2, tiles + 2, side + size, LANES), F32),
                pltpu.VMEM((3, 2, size, LANES), F32),
                pltpu.SemaphoreType.DMA((5,)),
            ] + scratch,
            compiler_params=params(30),
            cost_estimate=cost(16),
            name="outer_slots",
        )(
            odd, position, count, probe, folded, left, right, object_field, x_first, x_second, y_first, y_second,
            *corners, grad, probe_sum,
        )

        margin_first, margin_second = swap(margin_first, margin_second, "ty")
        scale = pl.pallas_call(
            weight_kernel,
            out_shape=jax.ShapeDtypeStruct((tiles, side, LANES), F32),
            in_specs=[SMEM, VMEM],
            out_specs=VMEM,
            scratch_shapes=[
                pltpu.VMEM((2, size, LANES), F32),
                pltpu.VMEM((tiles + 4, side + 2 * size, LANES), F32),
            ],
            compiler_params=params(8),
            cost_estimate=cost(8),
            name="weights",
        )(places, keep(probe))
        parts = trade(sums, planes)
        strip = pltpu.HBM((2, side, LANES), F32)
        whole = pl.BlockSpec((2, side, LANES), lambda index: (0, 0, 0))
        first_tile = pl.BlockSpec((2, 1, half, LANES), lambda index: (0, 0, 0, 0))
        last_tile = pl.BlockSpec((2, 1, half, LANES), lambda index: (0, tiles + 1, 0, 0))
        *margins, token = pl.pallas_call(
            sides_kernel,
            out_shape=(strip, strip, jax.ShapeDtypeStruct((8, LANES), F32)),
            grid=(1,),
            in_specs=[SMEM, whole, whole, first_tile, first_tile, last_tile, last_tile],
            out_specs=(whole, whole, pl.BlockSpec((8, LANES), lambda index: (0, 0))),
            compiler_params=params(8),
            cost_estimate=cost(16),
            name="sides",
        )(odd, keep(side_low), keep(side_high), margin_first, margin_second, margin_first, margin_second)
        x_first, x_second = swap(*margins, "tx")

        parts = pl.pallas_call(
            plane_kernel,
            out_shape=pltpu.HBM((len(lines[0]), 6, 8, LANES), F32),
            in_specs=[VMEM, HBM, HBM],
            out_specs=VMEM,
            compiler_params=params(6),
            cost_estimate=cost(2),
            name="plane_sum",
        )(parts, scale, token)
        parts = trade(parts, lines)
        pieces = pl.pallas_call(
            probe_kernel,
            out_shape=pltpu.HBM((members, 4, 8, LANES), F32),
            in_specs=[SMEM, VMEM, VMEM],
            out_specs=VMEM,
            compiler_params=params(6),
            cost_estimate=cost(2),
            name="probe_rows",
        )(piece, parts, keep(probe))
        probe_new = pl.pallas_call(
            join_kernel,
            out_shape=jax.ShapeDtypeStruct(probe.shape, F32),
            in_specs=[VMEM],
            out_specs=VMEM,
            compiler_params=params(6),
            cost_estimate=cost(2),
            name="join",
        )(trade(pieces, planes))

        column = pl.BlockSpec((2, side, LANES), lambda index: (0, 0, index))
        flat = pl.BlockSpec((2, 1, half, LANES), lambda index: (0, index + 1, 0, 0))
        object_new = pl.pallas_call(
            update_kernel,
            out_shape=jax.ShapeDtypeStruct(object_field.shape, F32),
            grid=(tiles,),
            in_specs=[
                SMEM, column, pl.BlockSpec((2, 1, side, LANES), lambda index: (0, index, 0, 0)), flat, flat,
                pl.BlockSpec((1, side, LANES), lambda index: (index, 0, 0)),
            ],
            out_specs=column,
            compiler_params=params(8),
            cost_estimate=cost(8),
            name="update",
        )(odd, keep(object_field), keep(middle), margin_first, margin_second, scale)
        ends = pl.BlockSpec((2, side, LANES), lambda index: (0, 0, index * (tiles - 1)))
        object_new = pl.pallas_call(
            column_kernel,
            out_shape=jax.ShapeDtypeStruct(object_field.shape, F32),
            grid=(2,),
            in_specs=[SMEM, ends, whole, whole, pl.BlockSpec((1, side, LANES), lambda index: (index * (tiles - 1), 0, 0))],
            out_specs=ends,
            input_output_aliases={1: 0},
            compiler_params=params(8),
            name="columns",
        )(odd, object_new, x_first, x_second, scale)
        return (object_new, probe_new)

    in_specs = (
        P(None, "ty", "tx"),
        P(),
        P("ty", "tx", None, None, None),
        P(None, "ty", "tx", None),
        P("ty", "tx"),
    )
    out_specs = (P(None, "ty", "tx"), P())
    return jax.shard_map(per_device, mesh=mesh, in_specs=in_specs, out_specs=out_specs, check_vma=False)
```

```python
import numpy as np
import ml_dtypes
import jax
import jax.numpy as jnp
from jax import lax
from jax.experimental import pallas as pl
from jax.experimental.pallas import tpu as pltpu
from jax.sharding import PartitionSpec as P

BF16 = jnp.bfloat16
F32 = jnp.float32
LANES = 128
VMEM = pl.BlockSpec(memory_space=pltpu.VMEM)
SMEM = pl.BlockSpec(memory_space=pltpu.SMEM)
HBM = pl.BlockSpec(memory_space=pltpu.HBM)
def split_host(table):
    high = table.astype(ml_dtypes.bfloat16)
    low = (table - high.astype(np.float64)).astype(ml_dtypes.bfloat16)
    return high, low


def half_tables(size):
    half = size // 2
    left, right = [], []
    for parity in range(2):
        product = (2 * np.arange(half)[:, None] + parity) * np.arange(half)[None, :] % size
        angle = 2.0 * np.pi * product / size
        cos, sin = np.cos(angle) / np.sqrt(size), np.sin(angle) / np.sqrt(size)
        base = np.block([[cos, sin], [-sin, cos]])
        for table in (base, base.T):
            high, low = split_host(table)
            left.append(np.concatenate([high, high, low], axis=1))
            right.append(np.concatenate([high, high, low], axis=0))
    return np.stack(left), np.stack(right)


def parity_tables(size):
    order = np.concatenate([np.arange(0, size, 2), np.arange(1, size, 2)])
    gather = np.eye(size)[order].astype(ml_dtypes.bfloat16)
    return np.concatenate([gather] * 3, axis=1), np.concatenate([gather.T] * 3, axis=0)


def matmul(left, right):
    return jnp.dot(left, right, preferred_element_type=F32)


def split(value):
    high = value.astype(BF16)
    return high, (value - high.astype(F32)).astype(BF16)


def put_rows(ref, start, columns, value):
    rows = value.shape[0]
    high, low = split(value)
    third = ref.shape[0] // 3
    ref[start : start + rows, columns] = high
    ref[third + start : third + start + rows, columns] = low
    ref[2 * third + start : 2 * third + start + rows, columns] = high


def put_columns(ref, rows, start, value):
    width = value.shape[1]
    high, low = split(value)
    third = ref.shape[1] // 3
    ref[rows, start : start + width] = high
    ref[rows, third + start : third + start + width] = low
    ref[rows, 2 * third + start : 2 * third + start + width] = high


def place(row, col, last):
    tile = jnp.minimum(lax.shift_right_logical(col, 7), last)
    return row, tile, col - tile * LANES


def add_window(accumulate, row, tile, offset, first, second):
    rows = first.shape[0]
    turn = jnp.bitwise_and(offset, LANES - 1)
    kept = lax.broadcasted_iota(jnp.int32, first.shape, 1) >= offset
    first = pltpu.roll(first, turn, 1)
    second = pltpu.roll(second, turn, 1)
    where = pl.ds(row, rows)
    accumulate[tile, where, :] += jnp.where(kept, first, 0.0)
    accumulate[tile + 1, where, :] += jnp.where(kept, second, first)
    accumulate[tile + 2, where, :] += jnp.where(kept, 0.0, second)


def fold_kernel(count, measured, gather_left, gather_right, folded, parts):
    size = measured.shape[1]

    def three(value):
        high = value.astype(BF16)
        rest = value - high.astype(F32)
        middle = rest.astype(BF16)
        return high, middle, (rest - middle.astype(F32)).astype(BF16)

    def step(slot, carry):
        for index, part in enumerate(three(measured[slot])):
            parts[:, index * size : (index + 1) * size] = part
        value = matmul(parts[...], gather_right[...])
        folded[slot] = matmul(gather_left[...], jnp.concatenate(three(value), axis=0))
        return carry

    lax.fori_loop(0, count[0], step, 0)


def own_notes(position, count):
    row = lax.broadcasted_iota(jnp.int32, (8, LANES), 0)
    lane = lax.broadcasted_iota(jnp.int32, (8, LANES), 1)
    notes = jnp.where(row == 2, count[0], 0)
    for slot in range(position.shape[1]):
        for axis in range(2):
            notes = jnp.where((row == axis) & (lane == slot), position[axis, slot], notes)
    return notes.astype(F32)


def edge_kernel(odd, position, count, tile_ref, x_first, x_second, y_first, y_second):
    half = LANES
    side = tile_ref.shape[1]
    odd_y, odd_x = odd[0] == 1, odd[1] == 1
    notes = own_notes(position, count)
    low, high = tile_ref[:, :, :half], tile_ref[:, :, side - half :]
    x_first[:, :side, :] = jnp.where(odd_x, high, low)
    x_second[:, :side, :] = jnp.where(odd_x, low, high)
    for out in (x_first, x_second):
        for plane in range(2):
            out[plane, side:, :] = notes
    low, high = tile_ref[:, :half, :], tile_ref[:, side - half :, :]
    y_first[...] = jnp.where(odd_y, high, low)
    y_second[...] = jnp.where(odd_y, low, high)


def corner_kernel(odd, position, count, x_first, x_second, after, first, second):
    half = LANES
    side = x_first.shape[1] - 8
    far = side - half
    odd_x = odd[1] == 1
    notes = own_notes(position, count)
    for out, odd_start in ((first, far), (second, 0)):
        rows = pl.ds(pl.multiple_of(jnp.where(odd[0] == 1, odd_start, far - odd_start), LANES), half)
        for index, (even_ref, odd_ref) in enumerate(((x_first, x_second), (x_second, x_first))):
            out[:, index, :half, :] = jnp.where(odd_x, odd_ref[:, rows, :], even_ref[:, rows, :])
            out[:, index, half : half + 8, :] = jnp.where(odd_x, odd_ref[:, side:, :], even_ref[:, side:, :])
            for plane in range(2):
                out[plane, index, half + 8 :, :] = notes


def slot_stages(row, tile, offset, live, probe, measured, left, right, canvas, grad, probe_sum, patch, rhs, lhs):
    size = probe.shape[1]
    half = size // 2
    near, far = slice(0, half), slice(half, size)
    turn = jnp.bitwise_and(LANES - offset, LANES - 1)
    kept = lax.broadcasted_iota(jnp.int32, (size, LANES), 1) < LANES - offset
    for plane in range(2):
        raw = [pltpu.roll(canvas[plane, tile + index, pl.ds(row, size), :], turn, 1) for index in range(3)]
        patch[plane, 0] = jnp.where(kept, raw[0], raw[1])
        patch[plane, 1] = jnp.where(kept, raw[1], raw[2])
    for index, columns in enumerate((near, far)):
        probe_re, probe_im = probe[0, :, columns], probe[1, :, columns]
        patch_re, patch_im = patch[0, index], patch[1, index]
        exit_re = probe_re * patch_re - probe_im * patch_im
        exit_im = probe_re * patch_im + probe_im * patch_re
        probe_sum[2, index] += (patch_re * patch_re + patch_im * patch_im) * live
        put_rows(rhs.at[0], 0, columns, exit_re[:half] + exit_re[half:])
        put_rows(rhs.at[0], half, columns, exit_im[:half] + exit_im[half:])
        put_rows(rhs.at[1], 0, columns, exit_re[:half] - exit_re[half:])
        put_rows(rhs.at[1], half, columns, exit_im[:half] - exit_im[half:])
    yield
    for parity in range(2):
        value = matmul(left[2 * parity], rhs[parity])
        rows = slice(parity * half, (parity + 1) * half)
        put_columns(lhs.at[0], rows, 0, value[:half, near] + value[:half, far])
        put_columns(lhs.at[0], rows, half, value[half:, near] + value[half:, far])
        put_columns(lhs.at[1], rows, 0, value[:half, near] - value[:half, far])
        put_columns(lhs.at[1], rows, half, value[half:, near] - value[half:, far])
        yield
    everything = slice(0, size)
    for parity in range(2):
        value = matmul(lhs[parity], right[2 * parity + 1])
        wave_re, wave_im = value[:, near], value[:, far]
        columns = slice(parity * half, (parity + 1) * half)
        excess = (wave_re * wave_re + wave_im * wave_im - measured[:, columns]) * live
        put_columns(lhs.at[parity], everything, 0, excess * wave_re)
        put_columns(lhs.at[parity], everything, half, excess * wave_im)
        yield
    back = []
    for parity in range(2):
        back.append(matmul(lhs[parity], right[2 * parity]))
    for parity in range(2):
        rows = slice(parity * half, (parity + 1) * half)
        put_rows(rhs.at[parity], 0, near, back[0][rows, near] + back[1][rows, near])
        put_rows(rhs.at[parity], half, near, back[0][rows, far] + back[1][rows, far])
        put_rows(rhs.at[parity], 0, far, back[0][rows, near] - back[1][rows, near])
        put_rows(rhs.at[parity], half, far, back[0][rows, far] - back[1][rows, far])
    yield
    even = matmul(left[1], rhs[0])
    odd = matmul(left[3], rhs[1])
    pieces = []
    for index, columns in enumerate((near, far)):
        chi_re, chi_im = (
            jnp.concatenate([even[rows, columns] + odd[rows, columns], even[rows, columns] - odd[rows, columns]], axis=0)
            for rows in (near, far)
        )
        probe_re, probe_im = probe[0, :, columns], probe[1, :, columns]
        patch_re, patch_im = patch[0, index], patch[1, index]
        probe_sum[0, index] += patch_re * chi_re + patch_im * chi_im
        probe_sum[1, index] += patch_re * chi_im - patch_im * chi_re
        pieces.append((probe_re * chi_re + probe_im * chi_im, probe_re * chi_im - probe_im * chi_re))
    for plane in range(2):
        add_window(grad.at[plane], row, tile, offset, pieces[0][plane], pieces[1][plane])
    yield


def run_slots(wanted, position, count, probe, folded, left, right, canvas, grad, probe_sum, order, patch, rhs, lhs):
    size = probe.shape[1]
    half = size // 2
    tiles = canvas.shape[1] - 2
    reach = tiles * LANES - size

    def pick(slot, found):
        row, col = position[0, slot], position[1, slot]
        take = wanted((row >= 0) & (row <= reach), (col >= 0) & (col <= reach))

        @pl.when(take)
        def keep():
            order[found] = slot

        return found + jnp.where(take, 1, 0)

    total = lax.fori_loop(0, count[0], pick, 0)
    lanes = patch.shape[0]

    def step(group, carry):
        stages = []
        for lane in range(lanes):
            index = lanes * group + lane
            live = jnp.where(index < total, 1.0, 0.0)
            slot = order[jnp.minimum(index, total - 1)]
            row, tile, offset = place(position[0, slot] + half, position[1, slot] + half, tiles - 1)
            stages.append(slot_stages(
                row, tile, offset, live, probe, folded.at[slot], left, right, canvas, grad, probe_sum,
                patch.at[lane], rhs.at[lane], lhs.at[lane],
            ))
        for _ in zip(*stages):
            pass
        return carry

    lax.fori_loop(0, lax.div(total + (lanes - 1), lanes), step, 0)


def inner_kernel(
    odd, position, count, probe, folded, left, right, tile_ref, x_first, x_second, canvas, grad, probe_sum, *scratch,
):
    side = tile_ref.shape[1]
    half = LANES
    tiles = side // LANES
    inner = slice(half, half + side)
    odd_x = odd[1] == 1
    for index in range(tiles):
        canvas[:, 1 + index, inner, :] = tile_ref[:, :, index * LANES : (index + 1) * LANES]
    canvas[:, 0, inner, :] = jnp.where(odd_x, x_second[:, :side, :], x_first[:, :side, :])
    canvas[:, 1 + tiles, inner, :] = jnp.where(odd_x, x_first[:, :side, :], x_second[:, :side, :])
    for rows in (slice(0, half), slice(half + side, 2 * half + side)):
        canvas[:, :, rows, :] = jnp.zeros((2, tiles + 2, half, LANES), F32)
    grad[...] = jnp.zeros_like(grad)
    probe_sum[...] = jnp.zeros_like(probe_sum)
    run_slots(lambda row, col: row, position, count, probe, folded, left, right, canvas, grad, probe_sum, *scratch)


def row_kernel(
    odd, position, count, probe, folded, left, right, y_first, y_second, canvas_in, grad_in, sum_in,
    canvas, grad, probe_sum, *scratch,
):
    half = LANES
    side = y_first.shape[2]
    odd_y = odd[0] == 1
    for index in range(side // LANES):
        columns = slice(index * LANES, (index + 1) * LANES)
        canvas[:, 1 + index, :half, :] = jnp.where(odd_y, y_second[:, :, columns], y_first[:, :, columns])
        canvas[:, 1 + index, half + side :, :] = jnp.where(odd_y, y_first[:, :, columns], y_second[:, :, columns])
    run_slots(
        lambda row, col: jnp.logical_not(row) & col,
        position, count, probe, folded, left, right, canvas, grad, probe_sum, *scratch,
    )


def outer_kernel(
    odd, position, count, probe, folded, left, right, x_first, x_second, corner_first, corner_second,
    canvas_in, grad_in, sum_in,
    margin_first, margin_second, side_low, side_high, middle, sums, places, canvas, grad, probe_sum, sems, *scratch,
):
    size = probe.shape[1]
    half = size // 2
    side = x_first.shape[1] - 8
    tiles = side // LANES
    inner = slice(half, half + side)
    odd_y, odd_x = odd[0] == 1, odd[1] == 1
    for index, tile in enumerate((0, 1 + tiles)):
        above, below = corner_first[:, index, :half, :], corner_second[:, index, :half, :]
        canvas[:, tile, :half, :] = jnp.where(odd_y, below, above)
        canvas[:, tile, half + side :, :] = jnp.where(odd_y, above, below)
    run_slots(
        lambda row, col: jnp.logical_not(row | col),
        position, count, probe, folded, left, right, canvas, grad, probe_sum, *scratch,
    )
    copies = []

    def send(source, target):
        copy = pltpu.make_async_copy(source, target, sems.at[len(copies)])
        copy.start()
        copies.append(copy)

    for out, odd_start in ((margin_first, half + side), (margin_second, 0)):
        rows = pl.ds(pl.multiple_of(jnp.where(odd_y, odd_start, half + side - odd_start), LANES), half)
        send(grad.at[:, :, rows, :], out)
    send(grad.at[:, 0, inner, :], side_low)
    send(grad.at[:, 1 + tiles, inner, :], side_high)
    send(grad.at[:, 1 : 1 + tiles, inner, :], middle)
    for plane in range(3):
        for index in range(2):
            sums[:, 2 * plane + index] = probe_sum[plane, index].reshape(size // 8, 8, LANES)
    beside, own = slice(half, half + 8), slice(half + 8, half + 16)
    for start, (even_ref, odd_ref) in ((0, (corner_first, corner_second)), (6, (corner_second, corner_first))):
        for index, (tile, rows) in enumerate(((0, beside), (0, own), (1, beside))):
            places[start + index] = jnp.where(odd_y, odd_ref[0, tile, rows, :], even_ref[0, tile, rows, :])
    places[3] = jnp.where(odd_x, x_second[0, side:, :], x_first[0, side:, :])
    places[4] = own_notes(position, count)
    places[5] = jnp.where(odd_x, x_first[0, side:, :], x_second[0, side:, :])
    for copy in copies:
        copy.wait()


def sides_kernel(odd, own_low, own_high, low_first, low_second, high_first, high_second, first, second):
    half = LANES
    side = own_low.shape[1]
    odd_y, odd_x = odd[0] == 1, odd[1] == 1
    for start in range(0, side, half):
        rows = slice(start, start + half)
        values = []
        for own, y_first, y_second in ((own_low, low_first, low_second), (own_high, high_first, high_second)):
            value = own[:, rows, :]
            if start == 0:
                value = value + jnp.where(odd_y, y_second[:, 0], y_first[:, 0])
            if start + half == side:
                value = value + jnp.where(odd_y, y_first[:, 0], y_second[:, 0])
            values.append(value)
        first[:, rows, :] = jnp.where(odd_x, values[1], values[0])
        second[:, rows, :] = jnp.where(odd_x, values[0], values[1])


def weight_kernel(numbers, probe, scale, power, weight):
    half = LANES
    side = scale.shape[1]
    tiles = side // LANES
    weight[...] = jnp.zeros_like(weight)
    for index in range(2):
        columns = slice(index * LANES, (index + 1) * LANES)
        power[index] = probe[0, :, columns] * probe[0, :, columns] + probe[1, :, columns] * probe[1, :, columns]
    for index in range(9):
        down, across = index // 3 - 1, index % 3 - 1

        def step(slot, carry):
            row = numbers[index, 0, slot].astype(jnp.int32) + (2 * half + down * side)
            col = numbers[index, 1, slot].astype(jnp.int32) + (2 * half + across * side)
            reach = side + 2 * half

            @pl.when((row > 0) & (row < reach) & (col > 0) & (col < reach))
            def add():
                at, tile, offset = place(row, col, tiles + 1)
                add_window(weight, at, tile, offset, power[0], power[1])

            return carry

        lax.fori_loop(0, numbers[index, 2, 0].astype(jnp.int32), step, 0)
    for index in range(tiles):
        scale[index] = 1.0 / (weight[2 + index, 2 * half : 2 * half + side, :] + 1.0)


def update_kernel(odd, tile_ref, grad, y_first, y_second, scale, out):
    half = LANES
    side = tile_ref.shape[1]
    odd_y = odd[0] == 1
    for plane in range(2):
        for start in range(0, side, half):
            rows = slice(start, start + half)
            value = grad[plane, 0, rows, :]
            if start == 0:
                value = value + jnp.where(odd_y, y_second[plane, 0], y_first[plane, 0])
            if start + half == side:
                value = value + jnp.where(odd_y, y_first[plane, 0], y_second[plane, 0])
            out[plane, rows, :] = tile_ref[plane, rows, :] - value * scale[0, rows, :]


def column_kernel(odd, before, x_first, x_second, scale, out):
    use_first = odd[1] == pl.program_id(0)
    for plane in range(2):
        out[plane] = before[plane] - jnp.where(use_first, x_first[plane], x_second[plane]) * scale[0]


def plane_kernel(parts, after, out):
    out[...] = jnp.broadcast_to(jnp.sum(parts[...], axis=0)[None], out.shape)


def probe_kernel(index, parts, probe, out):
    total = jnp.sum(parts[...], axis=0)
    rows = pl.ds(pl.multiple_of(index[0] * 8, 8), 8)
    for tile in range(2):
        root = jnp.sqrt(total[4 + tile] + 1.0)
        for plane in range(2):
            new = probe[plane, rows, tile * LANES : (tile + 1) * LANES] - total[2 * plane + tile] / root
            out[:, 2 * plane + tile] = jnp.broadcast_to(new[None], (out.shape[0], 8, LANES))


def join_kernel(pieces, out):
    for plane in range(2):
        for tile in range(2):
            value = pieces[:, 2 * plane + tile]
            out[plane, :, tile * LANES : (tile + 1) * LANES] = value.reshape(out.shape[1], LANES)


def swap(first, second, axis):
    count = lax.axis_size(axis)
    across = [pair for low in range(1, count - 1, 2) for pair in ((low, low + 1), (low + 1, low))]
    return lax.ppermute(first, axis, across), lax.ppermute(second, axis, [(index, index ^ 1) for index in range(count)])


def keep(value):
    return pltpu.with_memory_space_constraint(value, pltpu.HBM)


def params(mib):
    return pltpu.CompilerParams(vmem_limit_bytes=mib * 2**20)


def cost(mib):
    return pl.CostEstimate(flops=0, bytes_accessed=mib * 2**20, transcendentals=0)


def solution(mesh):
    rows, cols = mesh.shape["ty"], mesh.shape["tx"]
    near_y, near_z = 8, 4
    planes = [
        [(8 * high + row) * cols + near_z * x + low for row in range(near_y) for x in range(cols // near_z)]
        for high in range(rows // near_y)
        for low in range(near_z)
    ]
    lines = [list(line) for line in zip(*planes)]

    def trade(pieces, groups):
        return lax.all_to_all(pieces, ("ty", "tx"), 0, 0, axis_index_groups=groups, tiled=True)

    def per_device(object_field, probe, intensity, positions, counts):
        side = object_field.shape[1]
        size = probe.shape[1]
        half = size // 2
        slots = intensity.shape[2]
        tiles = side // LANES
        position = positions[:, 0, 0, :]
        count = counts[0]
        row, col = lax.axis_index("ty"), lax.axis_index("tx")
        piece = jnp.bitwise_and(row, near_y - 1) * (cols // near_z) + lax.shift_right_logical(col, 2)
        piece = piece.reshape(1).astype(jnp.int32)
        left, right = (jnp.asarray(table) for table in half_tables(size))
        gather_left, gather_right = (jnp.asarray(table) for table in parity_tables(size))

        odd = jnp.bitwise_and(jnp.stack([row, col]), 1).astype(jnp.int32)

        strip = jax.ShapeDtypeStruct((2, side + 8, LANES), F32)
        edge = jax.ShapeDtypeStruct((2, half, side), F32)
        x_first, x_second, y_first, y_second = pl.pallas_call(
            edge_kernel,
            out_shape=(strip, strip, edge, edge),
            in_specs=[SMEM] * 3 + [VMEM],
            out_specs=(VMEM,) * 4,
            compiler_params=params(6),
            cost_estimate=cost(4),
            name="edges",
        )(odd, position, count, object_field)
        x_first, x_second = swap(x_first, x_second, "tx")
        y_first, y_second = swap(y_first, y_second, "ty")
        folded = pl.pallas_call(
            fold_kernel,
            out_shape=jax.ShapeDtypeStruct((slots, size, size), F32),
            in_specs=[SMEM, VMEM, VMEM, VMEM],
            out_specs=VMEM,
            scratch_shapes=[pltpu.VMEM((size, 3 * size), BF16)],
            compiler_params=params(8),
            cost_estimate=cost(6),
            name="fold",
        )(count, intensity[0, 0], gather_left, gather_right)
        corner = jax.ShapeDtypeStruct((2, 2, half + 16, LANES), F32)
        corners = pl.pallas_call(
            corner_kernel,
            out_shape=(corner, corner),
            in_specs=[SMEM] * 3 + [VMEM] * 2 + [HBM],
            out_specs=(VMEM, VMEM),
            compiler_params=params(4),
            cost_estimate=cost(4),
            name="corners",
        )(odd, position, count, x_first, x_second, folded)
        corners = swap(*corners, "ty")

        members = len(planes[0])
        lanes = 2
        scratch = [
            pltpu.SMEM((slots,), jnp.int32),
            pltpu.VMEM((lanes, 2, 2, size, LANES), F32),
            pltpu.VMEM((lanes, 2, 3 * size, size), BF16),
            pltpu.VMEM((lanes, 2, size, 3 * size), BF16),
        ]
        state = (
            pltpu.VMEM((2, tiles + 2, side + size, LANES), F32),
            pltpu.VMEM((2, tiles + 2, side + size, LANES), F32),
            pltpu.VMEM((3, 2, size, LANES), F32),
        )
        given = (odd, position, count, probe, folded, left, right)
        canvas, grad, probe_sum = pl.pallas_call(
            inner_kernel,
            out_shape=state,
            in_specs=[SMEM] * 3 + [VMEM] * 7,
            out_specs=(VMEM,) * 3,
            scratch_shapes=scratch,
            compiler_params=params(26),
            cost_estimate=cost(16),
            name="inner_slots",
        )(*given, object_field, x_first, x_second)
        canvas, grad, probe_sum = pl.pallas_call(
            row_kernel,
            out_shape=state,
            in_specs=[SMEM] * 3 + [VMEM] * 9,
            out_specs=(VMEM,) * 3,
            scratch_shapes=scratch,
            input_output_aliases={9: 0, 10: 1, 11: 2},
            compiler_params=params(26),
            cost_estimate=cost(8),
            name="row_slots",
        )(*given, y_first, y_second, canvas, grad, probe_sum)
        margin = pltpu.HBM((2, tiles + 2, half, LANES), F32)
        column = pltpu.HBM((2, side, LANES), F32)
        margin_first, margin_second, side_low, side_high, middle, sums, places, *_ = pl.pallas_call(
            outer_kernel,
            out_shape=(
                margin, margin, column, column,
                pltpu.HBM((2, tiles, side, LANES), F32),
                pltpu.HBM((members, 6, 8, LANES), F32),
                jax.ShapeDtypeStruct((9, 8, LANES), F32),
            ) + state,
            in_specs=[SMEM] * 3 + [VMEM] * 11,
            out_specs=(HBM,) * 5 + (VMEM,) * 5,
            scratch_shapes=[pltpu.SemaphoreType.DMA((5,))] + scratch,
            input_output_aliases={11: 7, 12: 8, 13: 9},
            compiler_params=params(26),
            cost_estimate=cost(16),
            name="outer_slots",
        )(*given, x_first, x_second, *corners, canvas, grad, probe_sum)

        margin_first, margin_second = swap(margin_first, margin_second, "ty")
        scale = pl.pallas_call(
            weight_kernel,
            out_shape=jax.ShapeDtypeStruct((tiles, side, LANES), F32),
            in_specs=[SMEM, VMEM],
            out_specs=VMEM,
            scratch_shapes=[
                pltpu.VMEM((2, size, LANES), F32),
                pltpu.VMEM((tiles + 4, side + 2 * size, LANES), F32),
            ],
            compiler_params=params(8),
            cost_estimate=cost(8),
            name="weights",
        )(places, keep(probe))
        parts = trade(sums, planes)
        strip = pltpu.HBM((2, side, LANES), F32)
        whole = pl.BlockSpec((2, side, LANES), lambda index: (0, 0, 0))
        first_tile = pl.BlockSpec((2, 1, half, LANES), lambda index: (0, 0, 0, 0))
        last_tile = pl.BlockSpec((2, 1, half, LANES), lambda index: (0, tiles + 1, 0, 0))
        margins = pl.pallas_call(
            sides_kernel,
            out_shape=(strip, strip),
            grid=(1,),
            in_specs=[SMEM, whole, whole, first_tile, first_tile, last_tile, last_tile],
            out_specs=(whole, whole),
            compiler_params=params(8),
            cost_estimate=cost(16),
            name="sides",
        )(odd, keep(side_low), keep(side_high), margin_first, margin_second, margin_first, margin_second)
        x_first, x_second = swap(*margins, "tx")

        parts = pl.pallas_call(
            plane_kernel,
            out_shape=pltpu.HBM((len(lines[0]), 6, 8, LANES), F32),
            in_specs=[VMEM, HBM],
            out_specs=VMEM,
            compiler_params=params(6),
            cost_estimate=cost(2),
            name="plane_sum",
        )(parts, scale)
        parts = trade(parts, lines)
        pieces = pl.pallas_call(
            probe_kernel,
            out_shape=pltpu.HBM((members, 4, 8, LANES), F32),
            in_specs=[SMEM, VMEM, VMEM],
            out_specs=VMEM,
            compiler_params=params(6),
            cost_estimate=cost(2),
            name="probe_rows",
        )(piece, parts, keep(probe))
        probe_new = pl.pallas_call(
            join_kernel,
            out_shape=jax.ShapeDtypeStruct(probe.shape, F32),
            in_specs=[VMEM],
            out_specs=VMEM,
            compiler_params=params(6),
            cost_estimate=cost(2),
            name="join",
        )(trade(pieces, planes))

        column = pl.BlockSpec((2, side, LANES), lambda index: (0, 0, index))
        flat = pl.BlockSpec((2, 1, half, LANES), lambda index: (0, index + 1, 0, 0))
        object_new = pl.pallas_call(
            update_kernel,
            out_shape=jax.ShapeDtypeStruct(object_field.shape, F32),
            grid=(tiles,),
            in_specs=[
                SMEM, column, pl.BlockSpec((2, 1, side, LANES), lambda index: (0, index, 0, 0)), flat, flat,
                pl.BlockSpec((1, side, LANES), lambda index: (index, 0, 0)),
            ],
            out_specs=column,
            compiler_params=params(8),
            cost_estimate=cost(8),
            name="update",
        )(odd, keep(object_field), keep(middle), margin_first, margin_second, scale)
        ends = pl.BlockSpec((2, side, LANES), lambda index: (0, 0, index * (tiles - 1)))
        object_new = pl.pallas_call(
            column_kernel,
            out_shape=jax.ShapeDtypeStruct(object_field.shape, F32),
            grid=(2,),
            in_specs=[SMEM, ends, whole, whole, pl.BlockSpec((1, side, LANES), lambda index: (index * (tiles - 1), 0, 0))],
            out_specs=ends,
            input_output_aliases={1: 0},
            compiler_params=params(8),
            name="columns",
        )(odd, object_new, x_first, x_second, scale)
        return (object_new, probe_new)

    in_specs = (
        P(None, "ty", "tx"),
        P(),
        P("ty", "tx", None, None, None),
        P(None, "ty", "tx", None),
        P("ty", "tx"),
    )
    out_specs = (P(None, "ty", "tx"), P())
    return jax.shard_map(per_device, mesh=mesh, in_specs=in_specs, out_specs=out_specs, check_vma=False)
```

```python
import numpy as np
import ml_dtypes
import jax
import jax.numpy as jnp
from jax import lax
from jax.experimental import pallas as pl
from jax.experimental.pallas import tpu as pltpu
from jax.sharding import PartitionSpec as P

BF16 = jnp.bfloat16
F32 = jnp.float32
LANES = 128
VMEM = pl.BlockSpec(memory_space=pltpu.VMEM)
SMEM = pl.BlockSpec(memory_space=pltpu.SMEM)
HBM = pl.BlockSpec(memory_space=pltpu.HBM)
def split_host(table):
    high = table.astype(ml_dtypes.bfloat16)
    low = (table - high.astype(np.float64)).astype(ml_dtypes.bfloat16)
    return high, low


def half_tables(size):
    half = size // 2
    left, right = [], []
    for parity in range(2):
        product = (2 * np.arange(half)[:, None] + parity) * np.arange(half)[None, :] % size
        angle = 2.0 * np.pi * product / size
        cos, sin = np.cos(angle) / np.sqrt(size), np.sin(angle) / np.sqrt(size)
        base = np.block([[cos, sin], [-sin, cos]])
        for table in (base, base.T):
            high, low = split_host(table)
            left.append(np.concatenate([high, high, low], axis=1))
            right.append(np.concatenate([high, high, low], axis=0))
    return np.stack(left), np.stack(right)


def parity_tables(size):
    order = np.concatenate([np.arange(0, size, 2), np.arange(1, size, 2)])
    gather = np.eye(size)[order].astype(ml_dtypes.bfloat16)
    return np.concatenate([gather] * 3, axis=1), np.concatenate([gather.T] * 3, axis=0)


def matmul(left, right):
    return jnp.dot(left, right, preferred_element_type=F32)


def split(value):
    high = value.astype(BF16)
    return high, (value - high.astype(F32)).astype(BF16)


def put_rows(ref, start, columns, value):
    rows = value.shape[0]
    high, low = split(value)
    third = ref.shape[0] // 3
    ref[start : start + rows, columns] = high
    ref[third + start : third + start + rows, columns] = low
    ref[2 * third + start : 2 * third + start + rows, columns] = high


def put_columns(ref, rows, start, value):
    width = value.shape[1]
    high, low = split(value)
    third = ref.shape[1] // 3
    ref[rows, start : start + width] = high
    ref[rows, third + start : third + start + width] = low
    ref[rows, 2 * third + start : 2 * third + start + width] = high


def place(row, col, last):
    tile = jnp.minimum(lax.shift_right_logical(col, 7), last)
    return row, tile, col - tile * LANES


def add_window(accumulate, row, tile, offset, first, second):
    rows = first.shape[0]
    turn = jnp.bitwise_and(offset, LANES - 1)
    kept = lax.broadcasted_iota(jnp.int32, first.shape, 1) >= offset
    first = pltpu.roll(first, turn, 1)
    second = pltpu.roll(second, turn, 1)
    where = pl.ds(row, rows)
    accumulate[tile, where, :] += jnp.where(kept, first, 0.0)
    accumulate[tile + 1, where, :] += jnp.where(kept, second, first)
    accumulate[tile + 2, where, :] += jnp.where(kept, 0.0, second)


def fold_kernel(count, measured, gather_left, gather_right, folded, parts):
    size = measured.shape[1]

    def three(value):
        high = value.astype(BF16)
        rest = value - high.astype(F32)
        middle = rest.astype(BF16)
        return high, middle, (rest - middle.astype(F32)).astype(BF16)

    def step(slot, carry):
        for index, part in enumerate(three(measured[slot])):
            parts[:, index * size : (index + 1) * size] = part
        value = matmul(parts[...], gather_right[...])
        folded[slot] = matmul(gather_left[...], jnp.concatenate(three(value), axis=0))
        return carry

    lax.fori_loop(0, count[0], step, 0)


def own_notes(position, count):
    row = lax.broadcasted_iota(jnp.int32, (8, LANES), 0)
    lane = lax.broadcasted_iota(jnp.int32, (8, LANES), 1)
    notes = jnp.where(row == 2, count[0], 0)
    for slot in range(position.shape[1]):
        for axis in range(2):
            notes = jnp.where((row == axis) & (lane == slot), position[axis, slot], notes)
    return notes.astype(F32)


def edge_kernel(odd, position, count, low, high, upper, lower, x_first, x_second, y_first, y_second):
    side = low.shape[1]
    odd_y, odd_x = odd[0] == 1, odd[1] == 1
    notes = own_notes(position, count)
    x_first[:, :side, :] = jnp.where(odd_x, high[...], low[...])
    x_second[:, :side, :] = jnp.where(odd_x, low[...], high[...])
    for out in (x_first, x_second):
        for plane in range(2):
            out[plane, side:, :] = notes
    y_first[...] = jnp.where(odd_y, lower[...], upper[...])
    y_second[...] = jnp.where(odd_y, upper[...], lower[...])


def corner_kernel(odd, position, count, x_first, x_second, after, first, second):
    half = LANES
    side = x_first.shape[1] - 8
    far = side - half
    odd_x = odd[1] == 1
    notes = own_notes(position, count)
    for out, odd_start in ((first, far), (second, 0)):
        rows = pl.ds(pl.multiple_of(jnp.where(odd[0] == 1, odd_start, far - odd_start), LANES), half)
        for index, (even_ref, odd_ref) in enumerate(((x_first, x_second), (x_second, x_first))):
            out[:, index, :half, :] = jnp.where(odd_x, odd_ref[:, rows, :], even_ref[:, rows, :])
            out[:, index, half : half + 8, :] = jnp.where(odd_x, odd_ref[:, side:, :], even_ref[:, side:, :])
            for plane in range(2):
                out[plane, index, half + 8 :, :] = notes


def slot_stages(row, tile, offset, live, probe, measured, left, right, canvas, grad, probe_sum, patch, rhs, lhs):
    size = probe.shape[1]
    half = size // 2
    near, far = slice(0, half), slice(half, size)
    turn = jnp.bitwise_and(LANES - offset, LANES - 1)
    kept = lax.broadcasted_iota(jnp.int32, (size, LANES), 1) < LANES - offset
    for plane in range(2):
        raw = [pltpu.roll(canvas[plane, tile + index, pl.ds(row, size), :], turn, 1) for index in range(3)]
        patch[plane, 0] = jnp.where(kept, raw[0], raw[1])
        patch[plane, 1] = jnp.where(kept, raw[1], raw[2])
    for index, columns in enumerate((near, far)):
        probe_re, probe_im = probe[0, :, columns], probe[1, :, columns]
        patch_re, patch_im = patch[0, index], patch[1, index]
        exit_re = probe_re * patch_re - probe_im * patch_im
        exit_im = probe_re * patch_im + probe_im * patch_re
        probe_sum[2, index] += (patch_re * patch_re + patch_im * patch_im) * live
        put_rows(rhs.at[0], 0, columns, exit_re[:half] + exit_re[half:])
        put_rows(rhs.at[0], half, columns, exit_im[:half] + exit_im[half:])
        put_rows(rhs.at[1], 0, columns, exit_re[:half] - exit_re[half:])
        put_rows(rhs.at[1], half, columns, exit_im[:half] - exit_im[half:])
    yield
    for parity in range(2):
        value = matmul(left[2 * parity], rhs[parity])
        rows = slice(parity * half, (parity + 1) * half)
        put_columns(lhs.at[0], rows, 0, value[:half, near] + value[:half, far])
        put_columns(lhs.at[0], rows, half, value[half:, near] + value[half:, far])
        put_columns(lhs.at[1], rows, 0, value[:half, near] - value[:half, far])
        put_columns(lhs.at[1], rows, half, value[half:, near] - value[half:, far])
        yield
    everything = slice(0, size)
    for parity in range(2):
        value = matmul(lhs[parity], right[2 * parity + 1])
        wave_re, wave_im = value[:, near], value[:, far]
        columns = slice(parity * half, (parity + 1) * half)
        excess = (wave_re * wave_re + wave_im * wave_im - measured[:, columns]) * live
        put_columns(lhs.at[parity], everything, 0, excess * wave_re)
        put_columns(lhs.at[parity], everything, half, excess * wave_im)
        yield
    back = []
    for parity in range(2):
        back.append(matmul(lhs[parity], right[2 * parity]))
    for parity in range(2):
        rows = slice(parity * half, (parity + 1) * half)
        put_rows(rhs.at[parity], 0, near, back[0][rows, near] + back[1][rows, near])
        put_rows(rhs.at[parity], half, near, back[0][rows, far] + back[1][rows, far])
        put_rows(rhs.at[parity], 0, far, back[0][rows, near] - back[1][rows, near])
        put_rows(rhs.at[parity], half, far, back[0][rows, far] - back[1][rows, far])
    yield
    even = matmul(left[1], rhs[0])
    odd = matmul(left[3], rhs[1])
    pieces = []
    for index, columns in enumerate((near, far)):
        chi_re, chi_im = (
            jnp.concatenate([even[rows, columns] + odd[rows, columns], even[rows, columns] - odd[rows, columns]], axis=0)
            for rows in (near, far)
        )
        probe_re, probe_im = probe[0, :, columns], probe[1, :, columns]
        patch_re, patch_im = patch[0, index], patch[1, index]
        probe_sum[0, index] += patch_re * chi_re + patch_im * chi_im
        probe_sum[1, index] += patch_re * chi_im - patch_im * chi_re
        pieces.append((probe_re * chi_re + probe_im * chi_im, probe_re * chi_im - probe_im * chi_re))
    for plane in range(2):
        add_window(grad.at[plane], row, tile, offset, pieces[0][plane], pieces[1][plane])
    yield


def run_slots(wanted, position, count, probe, folded, left, right, canvas, grad, probe_sum, order, patch, rhs, lhs):
    size = probe.shape[1]
    half = size // 2
    tiles = canvas.shape[1] - 2
    reach = tiles * LANES - size

    def pick(slot, found):
        row, col = position[0, slot], position[1, slot]
        take = wanted((row >= 0) & (row <= reach), (col >= 0) & (col <= reach))

        @pl.when(take)
        def keep():
            order[found] = slot

        return found + jnp.where(take, 1, 0)

    total = lax.fori_loop(0, count[0], pick, 0)
    lanes = patch.shape[0]

    def step(group, carry):
        stages = []
        for lane in range(lanes):
            index = lanes * group + lane
            live = jnp.where(index < total, 1.0, 0.0)
            slot = order[jnp.minimum(index, total - 1)]
            row, tile, offset = place(position[0, slot] + half, position[1, slot] + half, tiles - 1)
            stages.append(slot_stages(
                row, tile, offset, live, probe, folded.at[slot], left, right, canvas, grad, probe_sum,
                patch.at[lane], rhs.at[lane], lhs.at[lane],
            ))
        for _ in zip(*stages):
            pass
        return carry

    lax.fori_loop(0, lax.div(total + (lanes - 1), lanes), step, 0)


def core_kernel(odd, position, count, probe, folded, left, right, tile_ref, canvas, grad, probe_sum, token, *scratch):
    side = tile_ref.shape[1]
    half = LANES
    tiles = side // LANES
    canvas[...] = jnp.zeros_like(canvas)
    for index in range(tiles):
        canvas[:, 1 + index, half : half + side, :] = tile_ref[:, :, index * LANES : (index + 1) * LANES]
    grad[...] = jnp.zeros_like(grad)
    probe_sum[...] = jnp.zeros_like(probe_sum)
    token[...] = jnp.zeros_like(token)
    run_slots(lambda row, col: row & col, position, count, probe, folded, left, right, canvas, grad, probe_sum, *scratch)


def column_slots_kernel(
    odd, position, count, probe, folded, left, right, x_first, x_second, canvas_in, grad_in, sum_in,
    canvas, grad, probe_sum, *scratch,
):
    side = x_first.shape[1] - 8
    half = LANES
    last = canvas.shape[1] - 1
    inner = slice(half, half + side)
    odd_x = odd[1] == 1
    canvas[:, 0, inner, :] = jnp.where(odd_x, x_second[:, :side, :], x_first[:, :side, :])
    canvas[:, last, inner, :] = jnp.where(odd_x, x_first[:, :side, :], x_second[:, :side, :])
    run_slots(
        lambda row, col: row & jnp.logical_not(col),
        position, count, probe, folded, left, right, canvas, grad, probe_sum, *scratch,
    )


def row_kernel(
    odd, position, count, probe, folded, left, right, y_first, y_second, canvas_in, grad_in, sum_in,
    canvas, grad, probe_sum, *scratch,
):
    half = LANES
    side = y_first.shape[2]
    odd_y = odd[0] == 1
    for index in range(side // LANES):
        columns = slice(index * LANES, (index + 1) * LANES)
        canvas[:, 1 + index, :half, :] = jnp.where(odd_y, y_second[:, :, columns], y_first[:, :, columns])
        canvas[:, 1 + index, half + side :, :] = jnp.where(odd_y, y_first[:, :, columns], y_second[:, :, columns])
    run_slots(
        lambda row, col: jnp.logical_not(row) & col,
        position, count, probe, folded, left, right, canvas, grad, probe_sum, *scratch,
    )


def outer_kernel(
    odd, position, count, probe, folded, left, right, x_first, x_second, corner_first, corner_second,
    canvas_in, grad_in, sum_in,
    margin_first, margin_second, side_low, side_high, middle, sums, places, canvas, grad, probe_sum, sems, *scratch,
):
    size = probe.shape[1]
    half = size // 2
    side = x_first.shape[1] - 8
    tiles = side // LANES
    inner = slice(half, half + side)
    odd_y, odd_x = odd[0] == 1, odd[1] == 1
    for index, tile in enumerate((0, 1 + tiles)):
        above, below = corner_first[:, index, :half, :], corner_second[:, index, :half, :]
        canvas[:, tile, :half, :] = jnp.where(odd_y, below, above)
        canvas[:, tile, half + side :, :] = jnp.where(odd_y, above, below)
    run_slots(
        lambda row, col: jnp.logical_not(row | col),
        position, count, probe, folded, left, right, canvas, grad, probe_sum, *scratch,
    )
    copies = []

    def send(source, target):
        copy = pltpu.make_async_copy(source, target, sems.at[len(copies)])
        copy.start()
        copies.append(copy)

    for out, odd_start in ((margin_first, half + side), (margin_second, 0)):
        rows = pl.ds(pl.multiple_of(jnp.where(odd_y, odd_start, half + side - odd_start), LANES), half)
        send(grad.at[:, :, rows, :], out)
    send(grad.at[:, 0, inner, :], side_low)
    send(grad.at[:, 1 + tiles, inner, :], side_high)
    send(grad.at[:, 1 : 1 + tiles, inner, :], middle)
    for plane in range(3):
        for index in range(2):
            sums[:, 2 * plane + index] = probe_sum[plane, index].reshape(size // 8, 8, LANES)
    beside, own = slice(half, half + 8), slice(half + 8, half + 16)
    for start, (even_ref, odd_ref) in ((0, (corner_first, corner_second)), (6, (corner_second, corner_first))):
        for index, (tile, rows) in enumerate(((0, beside), (0, own), (1, beside))):
            places[start + index] = jnp.where(odd_y, odd_ref[0, tile, rows, :], even_ref[0, tile, rows, :])
    places[3] = jnp.where(odd_x, x_second[0, side:, :], x_first[0, side:, :])
    places[4] = own_notes(position, count)
    places[5] = jnp.where(odd_x, x_first[0, side:, :], x_second[0, side:, :])
    for copy in copies:
        copy.wait()


def sides_kernel(odd, own_low, own_high, low_first, low_second, high_first, high_second, first, second):
    half = LANES
    side = own_low.shape[1]
    odd_y, odd_x = odd[0] == 1, odd[1] == 1
    for start in range(0, side, half):
        rows = slice(start, start + half)
        values = []
        for own, y_first, y_second in ((own_low, low_first, low_second), (own_high, high_first, high_second)):
            value = own[:, rows, :]
            if start == 0:
                value = value + jnp.where(odd_y, y_second[:, 0], y_first[:, 0])
            if start + half == side:
                value = value + jnp.where(odd_y, y_first[:, 0], y_second[:, 0])
            values.append(value)
        first[:, rows, :] = jnp.where(odd_x, values[1], values[0])
        second[:, rows, :] = jnp.where(odd_x, values[0], values[1])


def weight_kernel(numbers, probe, scale, power, weight):
    half = LANES
    side = scale.shape[1]
    tiles = side // LANES
    weight[...] = jnp.zeros_like(weight)
    for index in range(2):
        columns = slice(index * LANES, (index + 1) * LANES)
        power[index] = probe[0, :, columns] * probe[0, :, columns] + probe[1, :, columns] * probe[1, :, columns]
    for index in range(9):
        down, across = index // 3 - 1, index % 3 - 1

        def step(slot, carry):
            row = numbers[index, 0, slot].astype(jnp.int32) + (2 * half + down * side)
            col = numbers[index, 1, slot].astype(jnp.int32) + (2 * half + across * side)
            reach = side + 2 * half

            @pl.when((row > 0) & (row < reach) & (col > 0) & (col < reach))
            def add():
                at, tile, offset = place(row, col, tiles + 1)
                add_window(weight, at, tile, offset, power[0], power[1])

            return carry

        lax.fori_loop(0, numbers[index, 2, 0].astype(jnp.int32), step, 0)
    for index in range(tiles):
        scale[index] = 1.0 / (weight[2 + index, 2 * half : 2 * half + side, :] + 1.0)


def update_kernel(odd, tile_ref, grad, y_first, y_second, scale, out):
    half = LANES
    side = tile_ref.shape[1]
    odd_y = odd[0] == 1
    for plane in range(2):
        for start in range(0, side, half):
            rows = slice(start, start + half)
            value = grad[plane, 0, rows, :]
            if start == 0:
                value = value + jnp.where(odd_y, y_second[plane, 0], y_first[plane, 0])
            if start + half == side:
                value = value + jnp.where(odd_y, y_first[plane, 0], y_second[plane, 0])
            out[plane, rows, :] = tile_ref[plane, rows, :] - value * scale[0, rows, :]


def column_kernel(odd, before, x_first, x_second, scale, out):
    use_first = odd[1] == pl.program_id(0)
    for plane in range(2):
        out[plane] = before[plane] - jnp.where(use_first, x_first[plane], x_second[plane]) * scale[0]


def plane_kernel(parts, after, out):
    out[...] = jnp.broadcast_to(jnp.sum(parts[...], axis=0)[None], out.shape)


def probe_kernel(index, parts, probe, out):
    total = jnp.sum(parts[...], axis=0)
    rows = pl.ds(pl.multiple_of(index[0] * 8, 8), 8)
    for tile in range(2):
        root = jnp.sqrt(total[4 + tile] + 1.0)
        for plane in range(2):
            new = probe[plane, rows, tile * LANES : (tile + 1) * LANES] - total[2 * plane + tile] / root
            out[:, 2 * plane + tile] = jnp.broadcast_to(new[None], (out.shape[0], 8, LANES))


def join_kernel(pieces, out):
    for plane in range(2):
        for tile in range(2):
            value = pieces[:, 2 * plane + tile]
            out[plane, :, tile * LANES : (tile + 1) * LANES] = value.reshape(out.shape[1], LANES)


def swap(first, second, axis):
    count = lax.axis_size(axis)
    across = [pair for low in range(1, count - 1, 2) for pair in ((low, low + 1), (low + 1, low))]
    return lax.ppermute(first, axis, across), lax.ppermute(second, axis, [(index, index ^ 1) for index in range(count)])


def keep(value):
    return pltpu.with_memory_space_constraint(value, pltpu.HBM)


def params(mib):
    return pltpu.CompilerParams(vmem_limit_bytes=mib * 2**20)


def cost(mib):
    return pl.CostEstimate(flops=0, bytes_accessed=mib * 2**20, transcendentals=0)


def solution(mesh):
    rows, cols = mesh.shape["ty"], mesh.shape["tx"]
    near_y, near_z = 8, 4
    planes = [
        [(8 * high + row) * cols + near_z * x + low for row in range(near_y) for x in range(cols // near_z)]
        for high in range(rows // near_y)
        for low in range(near_z)
    ]
    lines = [list(line) for line in zip(*planes)]

    def trade(pieces, groups):
        return lax.all_to_all(pieces, ("ty", "tx"), 0, 0, axis_index_groups=groups, tiled=True)

    def per_device(object_field, probe, intensity, positions, counts):
        side = object_field.shape[1]
        size = probe.shape[1]
        half = size // 2
        slots = intensity.shape[2]
        tiles = side // LANES
        position = positions[:, 0, 0, :]
        count = counts[0]
        row, col = lax.axis_index("ty"), lax.axis_index("tx")
        piece = jnp.bitwise_and(row, near_y - 1) * (cols // near_z) + lax.shift_right_logical(col, 2)
        piece = piece.reshape(1).astype(jnp.int32)
        left, right = (jnp.asarray(table) for table in half_tables(size))
        gather_left, gather_right = (jnp.asarray(table) for table in parity_tables(size))

        odd = jnp.bitwise_and(jnp.stack([row, col]), 1).astype(jnp.int32)

        strip = jax.ShapeDtypeStruct((2, side + 8, LANES), F32)
        edge = jax.ShapeDtypeStruct((2, half, side), F32)
        x_first, x_second, y_first, y_second = pl.pallas_call(
            edge_kernel,
            out_shape=(strip, strip, edge, edge),
            grid=(1,),
            in_specs=[SMEM] * 3 + [
                pl.BlockSpec((2, side, half), lambda index: (0, 0, 0)),
                pl.BlockSpec((2, side, half), lambda index: (0, 0, tiles - 1)),
                pl.BlockSpec((2, half, side), lambda index: (0, 0, 0)),
                pl.BlockSpec((2, half, side), lambda index: (0, tiles - 1, 0)),
            ],
            out_specs=(
                pl.BlockSpec((2, side + 8, half), lambda index: (0, 0, 0)),
                pl.BlockSpec((2, side + 8, half), lambda index: (0, 0, 0)),
                pl.BlockSpec((2, half, side), lambda index: (0, 0, 0)),
                pl.BlockSpec((2, half, side), lambda index: (0, 0, 0)),
            ),
            compiler_params=params(10),
            cost_estimate=cost(4),
            name="edges",
        )(odd, position, count, *[keep(object_field)] * 4)
        x_first, x_second = swap(x_first, x_second, "tx")
        y_first, y_second = swap(y_first, y_second, "ty")
        folded = pl.pallas_call(
            fold_kernel,
            out_shape=jax.ShapeDtypeStruct((slots, size, size), F32),
            in_specs=[SMEM, VMEM, VMEM, VMEM],
            out_specs=VMEM,
            scratch_shapes=[pltpu.VMEM((size, 3 * size), BF16)],
            compiler_params=params(8),
            cost_estimate=cost(6),
            name="fold",
        )(count, intensity[0, 0], gather_left, gather_right)
        members = len(planes[0])
        lanes = 2
        scratch = [
            pltpu.SMEM((slots,), jnp.int32),
            pltpu.VMEM((lanes, 2, 2, size, LANES), F32),
            pltpu.VMEM((lanes, 2, 3 * size, size), BF16),
            pltpu.VMEM((lanes, 2, size, 3 * size), BF16),
        ]
        state = (
            pltpu.VMEM((2, tiles + 2, side + size, LANES), F32),
            pltpu.VMEM((2, tiles + 2, side + size, LANES), F32),
            pltpu.VMEM((3, 2, size, LANES), F32),
        )
        given = (odd, position, count, probe, folded, left, right)
        canvas, grad, probe_sum, token = pl.pallas_call(
            core_kernel,
            out_shape=state + (jax.ShapeDtypeStruct((8, LANES), F32),),
            in_specs=[SMEM] * 3 + [VMEM] * 5,
            out_specs=(VMEM,) * 4,
            scratch_shapes=scratch,
            compiler_params=params(26),
            cost_estimate=cost(16),
            name="core_slots",
        )(*given, object_field)
        corner = jax.ShapeDtypeStruct((2, 2, half + 16, LANES), F32)
        corners = pl.pallas_call(
            corner_kernel,
            out_shape=(corner, corner),
            in_specs=[SMEM] * 3 + [VMEM] * 2 + [HBM],
            out_specs=(VMEM, VMEM),
            compiler_params=params(4),
            cost_estimate=cost(4),
            name="corners",
        )(odd, position, count, x_first, x_second, token)
        corners = swap(*corners, "ty")

        canvas, grad, probe_sum = pl.pallas_call(
            column_slots_kernel,
            out_shape=state,
            in_specs=[SMEM] * 3 + [VMEM] * 9,
            out_specs=(VMEM,) * 3,
            scratch_shapes=scratch,
            input_output_aliases={9: 0, 10: 1, 11: 2},
            compiler_params=params(26),
            cost_estimate=cost(16),
            name="column_slots",
        )(*given, x_first, x_second, canvas, grad, probe_sum)
        canvas, grad, probe_sum = pl.pallas_call(
            row_kernel,
            out_shape=state,
            in_specs=[SMEM] * 3 + [VMEM] * 9,
            out_specs=(VMEM,) * 3,
            scratch_shapes=scratch,
            input_output_aliases={9: 0, 10: 1, 11: 2},
            compiler_params=params(26),
            cost_estimate=cost(8),
            name="row_slots",
        )(*given, y_first, y_second, canvas, grad, probe_sum)
        margin = pltpu.HBM((2, tiles + 2, half, LANES), F32)
        column = pltpu.HBM((2, side, LANES), F32)
        margin_first, margin_second, side_low, side_high, middle, sums, places, *_ = pl.pallas_call(
            outer_kernel,
            out_shape=(
                margin, margin, column, column,
                pltpu.HBM((2, tiles, side, LANES), F32),
                pltpu.HBM((members, 6, 8, LANES), F32),
                jax.ShapeDtypeStruct((9, 8, LANES), F32),
            ) + state,
            in_specs=[SMEM] * 3 + [VMEM] * 11,
            out_specs=(HBM,) * 5 + (VMEM,) * 5,
            scratch_shapes=[pltpu.SemaphoreType.DMA((5,))] + scratch,
            input_output_aliases={11: 7, 12: 8, 13: 9},
            compiler_params=params(26),
            cost_estimate=cost(16),
            name="outer_slots",
        )(*given, x_first, x_second, *corners, canvas, grad, probe_sum)

        margin_first, margin_second = swap(margin_first, margin_second, "ty")
        scale = pl.pallas_call(
            weight_kernel,
            out_shape=jax.ShapeDtypeStruct((tiles, side, LANES), F32),
            in_specs=[SMEM, VMEM],
            out_specs=VMEM,
            scratch_shapes=[
                pltpu.VMEM((2, size, LANES), F32),
                pltpu.VMEM((tiles + 4, side + 2 * size, LANES), F32),
            ],
            compiler_params=params(8),
            cost_estimate=cost(8),
            name="weights",
        )(places, keep(probe))
        parts = trade(sums, planes)
        strip = pltpu.HBM((2, side, LANES), F32)
        whole = pl.BlockSpec((2, side, LANES), lambda index: (0, 0, 0))
        first_tile = pl.BlockSpec((2, 1, half, LANES), lambda index: (0, 0, 0, 0))
        last_tile = pl.BlockSpec((2, 1, half, LANES), lambda index: (0, tiles + 1, 0, 0))
        margins = pl.pallas_call(
            sides_kernel,
            out_shape=(strip, strip),
            grid=(1,),
            in_specs=[SMEM, whole, whole, first_tile, first_tile, last_tile, last_tile],
            out_specs=(whole, whole),
            compiler_params=params(8),
            cost_estimate=cost(16),
            name="sides",
        )(odd, keep(side_low), keep(side_high), margin_first, margin_second, margin_first, margin_second)
        x_first, x_second = swap(*margins, "tx")

        parts = pl.pallas_call(
            plane_kernel,
            out_shape=pltpu.HBM((len(lines[0]), 6, 8, LANES), F32),
            in_specs=[VMEM, HBM],
            out_specs=VMEM,
            compiler_params=params(6),
            cost_estimate=cost(2),
            name="plane_sum",
        )(parts, scale)
        parts = trade(parts, lines)
        pieces = pl.pallas_call(
            probe_kernel,
            out_shape=pltpu.HBM((members, 4, 8, LANES), F32),
            in_specs=[SMEM, VMEM, VMEM],
            out_specs=VMEM,
            compiler_params=params(6),
            cost_estimate=cost(2),
            name="probe_rows",
        )(piece, parts, keep(probe))
        probe_new = pl.pallas_call(
            join_kernel,
            out_shape=jax.ShapeDtypeStruct(probe.shape, F32),
            in_specs=[VMEM],
            out_specs=VMEM,
            compiler_params=params(6),
            cost_estimate=cost(2),
            name="join",
        )(trade(pieces, planes))

        column = pl.BlockSpec((2, side, LANES), lambda index: (0, 0, index))
        flat = pl.BlockSpec((2, 1, half, LANES), lambda index: (0, index + 1, 0, 0))
        object_new = pl.pallas_call(
            update_kernel,
            out_shape=jax.ShapeDtypeStruct(object_field.shape, F32),
            grid=(tiles,),
            in_specs=[
                SMEM, column, pl.BlockSpec((2, 1, side, LANES), lambda index: (0, index, 0, 0)), flat, flat,
                pl.BlockSpec((1, side, LANES), lambda index: (index, 0, 0)),
            ],
            out_specs=column,
            compiler_params=params(8),
            cost_estimate=cost(8),
            name="update",
        )(odd, keep(object_field), keep(middle), margin_first, margin_second, scale)
        ends = pl.BlockSpec((2, side, LANES), lambda index: (0, 0, index * (tiles - 1)))
        object_new = pl.pallas_call(
            column_kernel,
            out_shape=jax.ShapeDtypeStruct(object_field.shape, F32),
            grid=(2,),
            in_specs=[SMEM, ends, whole, whole, pl.BlockSpec((1, side, LANES), lambda index: (index * (tiles - 1), 0, 0))],
            out_specs=ends,
            input_output_aliases={1: 0},
            compiler_params=params(8),
            name="columns",
        )(odd, object_new, x_first, x_second, scale)
        return (object_new, probe_new)

    in_specs = (
        P(None, "ty", "tx"),
        P(),
        P("ty", "tx", None, None, None),
        P(None, "ty", "tx", None),
        P("ty", "tx"),
    )
    out_specs = (P(None, "ty", "tx"), P())
    return jax.shard_map(per_device, mesh=mesh, in_specs=in_specs, out_specs=out_specs, check_vma=False)
```

```python
import numpy as np
import ml_dtypes
import jax
import jax.numpy as jnp
from jax import lax
from jax.experimental import pallas as pl
from jax.experimental.pallas import tpu as pltpu
from jax.sharding import PartitionSpec as P

BF16 = jnp.bfloat16
F32 = jnp.float32
LANES = 128
VMEM = pl.BlockSpec(memory_space=pltpu.VMEM)
SMEM = pl.BlockSpec(memory_space=pltpu.SMEM)
HBM = pl.BlockSpec(memory_space=pltpu.HBM)
def split_host(table):
    high = table.astype(ml_dtypes.bfloat16)
    low = (table - high.astype(np.float64)).astype(ml_dtypes.bfloat16)
    return high, low


def half_tables(size):
    half = size // 2
    left, right = [], []
    for parity in range(2):
        product = (2 * np.arange(half)[:, None] + parity) * np.arange(half)[None, :] % size
        angle = 2.0 * np.pi * product / size
        cos, sin = np.cos(angle) / np.sqrt(size), np.sin(angle) / np.sqrt(size)
        base = np.block([[cos, sin], [-sin, cos]])
        for table in (base, base.T):
            high, low = split_host(table)
            left.append(np.concatenate([high, high, low], axis=1))
            right.append(np.concatenate([high, high, low], axis=0))
    return np.stack(left), np.stack(right)


def parity_tables(size):
    order = np.concatenate([np.arange(0, size, 2), np.arange(1, size, 2)])
    gather = np.eye(size)[order].astype(ml_dtypes.bfloat16)
    return np.concatenate([gather] * 3, axis=1), np.concatenate([gather.T] * 3, axis=0)


def matmul(left, right):
    return jnp.dot(left, right, preferred_element_type=F32)


def split(value):
    high = value.astype(BF16)
    return high, (value - high.astype(F32)).astype(BF16)


def put_rows(ref, start, columns, value):
    rows = value.shape[0]
    high, low = split(value)
    third = ref.shape[0] // 3
    ref[start : start + rows, columns] = high
    ref[third + start : third + start + rows, columns] = low
    ref[2 * third + start : 2 * third + start + rows, columns] = high


def put_columns(ref, rows, start, value):
    width = value.shape[1]
    high, low = split(value)
    third = ref.shape[1] // 3
    ref[rows, start : start + width] = high
    ref[rows, third + start : third + start + width] = low
    ref[rows, 2 * third + start : 2 * third + start + width] = high


def place(row, col, last):
    tile = jnp.minimum(lax.shift_right_logical(col, 7), last)
    return row, tile, col - tile * LANES


def add_window(accumulate, row, tile, offset, first, second):
    rows = first.shape[0]
    turn = jnp.bitwise_and(offset, LANES - 1)
    kept = lax.broadcasted_iota(jnp.int32, first.shape, 1) >= offset
    first = pltpu.roll(first, turn, 1)
    second = pltpu.roll(second, turn, 1)
    where = pl.ds(row, rows)
    accumulate[tile, where, :] += jnp.where(kept, first, 0.0)
    accumulate[tile + 1, where, :] += jnp.where(kept, second, first)
    accumulate[tile + 2, where, :] += jnp.where(kept, 0.0, second)


def fold_kernel(count, measured, gather_left, gather_right, folded, parts):
    size = measured.shape[1]

    def three(value):
        high = value.astype(BF16)
        rest = value - high.astype(F32)
        middle = rest.astype(BF16)
        return high, middle, (rest - middle.astype(F32)).astype(BF16)

    def step(slot, carry):
        for index, part in enumerate(three(measured[slot])):
            parts[:, index * size : (index + 1) * size] = part
        value = matmul(parts[...], gather_right[...])
        folded[slot] = matmul(gather_left[...], jnp.concatenate(three(value), axis=0))
        return carry

    lax.fori_loop(0, count[0], step, 0)


def own_notes(position, count):
    row = lax.broadcasted_iota(jnp.int32, (8, LANES), 0)
    lane = lax.broadcasted_iota(jnp.int32, (8, LANES), 1)
    notes = jnp.where(row == 2, count[0], 0)
    for slot in range(position.shape[1]):
        for axis in range(2):
            notes = jnp.where((row == axis) & (lane == slot), position[axis, slot], notes)
    return notes.astype(F32)


def edge_kernel(odd, position, count, tile_ref, x_first, x_second, y_first, y_second):
    half = LANES
    side = tile_ref.shape[1]
    odd_y, odd_x = odd[0] == 1, odd[1] == 1
    notes = own_notes(position, count)
    low, high = tile_ref[:, :, :half], tile_ref[:, :, side - half :]
    x_first[:, :side, :] = jnp.where(odd_x, high, low)
    x_second[:, :side, :] = jnp.where(odd_x, low, high)
    for out in (x_first, x_second):
        for plane in range(2):
            out[plane, side:, :] = notes
    low, high = tile_ref[:, :half, :], tile_ref[:, side - half :, :]
    y_first[...] = jnp.where(odd_y, high, low)
    y_second[...] = jnp.where(odd_y, low, high)


def corner_kernel(odd, position, count, x_first, x_second, after, first, second):
    half = LANES
    side = x_first.shape[1] - 8
    far = side - half
    odd_x = odd[1] == 1
    notes = own_notes(position, count)
    for out, odd_start in ((first, far), (second, 0)):
        rows = pl.ds(pl.multiple_of(jnp.where(odd[0] == 1, odd_start, far - odd_start), LANES), half)
        for index, (even_ref, odd_ref) in enumerate(((x_first, x_second), (x_second, x_first))):
            out[:, index, :half, :] = jnp.where(odd_x, odd_ref[:, rows, :], even_ref[:, rows, :])
            out[:, index, half : half + 8, :] = jnp.where(odd_x, odd_ref[:, side:, :], even_ref[:, side:, :])
            for plane in range(2):
                out[plane, index, half + 8 :, :] = notes


def slot_stages(row, tile, offset, live, probe, measured, left, right, canvas, grad, probe_sum, patch, rhs, lhs):
    size = probe.shape[1]
    half = size // 2
    near, far = slice(0, half), slice(half, size)
    turn = jnp.bitwise_and(LANES - offset, LANES - 1)
    kept = lax.broadcasted_iota(jnp.int32, (size, LANES), 1) < LANES - offset
    for plane in range(2):
        raw = [pltpu.roll(canvas[plane, tile + index, pl.ds(row, size), :], turn, 1) for index in range(3)]
        patch[plane, 0] = jnp.where(kept, raw[0], raw[1])
        patch[plane, 1] = jnp.where(kept, raw[1], raw[2])
    for index, columns in enumerate((near, far)):
        probe_re, probe_im = probe[0, :, columns], probe[1, :, columns]
        patch_re, patch_im = patch[0, index], patch[1, index]
        exit_re = probe_re * patch_re - probe_im * patch_im
        exit_im = probe_re * patch_im + probe_im * patch_re
        probe_sum[2, index] += (patch_re * patch_re + patch_im * patch_im) * live
        put_rows(rhs.at[0], 0, columns, exit_re[:half] + exit_re[half:])
        put_rows(rhs.at[0], half, columns, exit_im[:half] + exit_im[half:])
        put_rows(rhs.at[1], 0, columns, exit_re[:half] - exit_re[half:])
        put_rows(rhs.at[1], half, columns, exit_im[:half] - exit_im[half:])
    yield
    for parity in range(2):
        value = matmul(left[2 * parity], rhs[parity])
        rows = slice(parity * half, (parity + 1) * half)
        put_columns(lhs.at[0], rows, 0, value[:half, near] + value[:half, far])
        put_columns(lhs.at[0], rows, half, value[half:, near] + value[half:, far])
        put_columns(lhs.at[1], rows, 0, value[:half, near] - value[:half, far])
        put_columns(lhs.at[1], rows, half, value[half:, near] - value[half:, far])
        yield
    everything = slice(0, size)
    for parity in range(2):
        value = matmul(lhs[parity], right[2 * parity + 1])
        wave_re, wave_im = value[:, near], value[:, far]
        columns = slice(parity * half, (parity + 1) * half)
        excess = (wave_re * wave_re + wave_im * wave_im - measured[:, columns]) * live
        put_columns(lhs.at[parity], everything, 0, excess * wave_re)
        put_columns(lhs.at[parity], everything, half, excess * wave_im)
        yield
    back = []
    for parity in range(2):
        back.append(matmul(lhs[parity], right[2 * parity]))
    for parity in range(2):
        rows = slice(parity * half, (parity + 1) * half)
        put_rows(rhs.at[parity], 0, near, back[0][rows, near] + back[1][rows, near])
        put_rows(rhs.at[parity], half, near, back[0][rows, far] + back[1][rows, far])
        put_rows(rhs.at[parity], 0, far, back[0][rows, near] - back[1][rows, near])
        put_rows(rhs.at[parity], half, far, back[0][rows, far] - back[1][rows, far])
    yield
    even = matmul(left[1], rhs[0])
    odd = matmul(left[3], rhs[1])
    pieces = []
    for index, columns in enumerate((near, far)):
        chi_re, chi_im = (
            jnp.concatenate([even[rows, columns] + odd[rows, columns], even[rows, columns] - odd[rows, columns]], axis=0)
            for rows in (near, far)
        )
        probe_re, probe_im = probe[0, :, columns], probe[1, :, columns]
        patch_re, patch_im = patch[0, index], patch[1, index]
        probe_sum[0, index] += patch_re * chi_re + patch_im * chi_im
        probe_sum[1, index] += patch_re * chi_im - patch_im * chi_re
        pieces.append((probe_re * chi_re + probe_im * chi_im, probe_re * chi_im - probe_im * chi_re))
    for plane in range(2):
        add_window(grad.at[plane], row, tile, offset, pieces[0][plane], pieces[1][plane])
    yield


def run_slots(wanted, position, count, probe, folded, left, right, canvas, grad, probe_sum, order, patch, rhs, lhs):
    size = probe.shape[1]
    half = size // 2
    tiles = canvas.shape[1] - 2
    reach = tiles * LANES - size

    def pick(slot, found):
        row, col = position[0, slot], position[1, slot]
        take = wanted((row >= 0) & (row <= reach), (col >= 0) & (col <= reach))

        @pl.when(take)
        def keep():
            order[found] = slot

        return found + jnp.where(take, 1, 0)

    total = lax.fori_loop(0, count[0], pick, 0)
    lanes = patch.shape[0]

    def step(group, carry):
        stages = []
        for lane in range(lanes):
            index = lanes * group + lane
            live = jnp.where(index < total, 1.0, 0.0)
            slot = order[jnp.minimum(index, total - 1)]
            row, tile, offset = place(position[0, slot] + half, position[1, slot] + half, tiles - 1)
            stages.append(slot_stages(
                row, tile, offset, live, probe, folded.at[slot], left, right, canvas, grad, probe_sum,
                patch.at[lane], rhs.at[lane], lhs.at[lane],
            ))
        for _ in zip(*stages):
            pass
        return carry

    lax.fori_loop(0, lax.div(total + (lanes - 1), lanes), step, 0)


def core_kernel(odd, position, count, probe, folded, left, right, tile_ref, canvas, grad, probe_sum, token, *scratch):
    side = tile_ref.shape[1]
    half = LANES
    tiles = side // LANES
    canvas[...] = jnp.zeros_like(canvas)
    for index in range(tiles):
        canvas[:, 1 + index, half : half + side, :] = tile_ref[:, :, index * LANES : (index + 1) * LANES]
    grad[...] = jnp.zeros_like(grad)
    probe_sum[...] = jnp.zeros_like(probe_sum)
    token[...] = jnp.zeros_like(token)
    run_slots(lambda row, col: row & col, position, count, probe, folded, left, right, canvas, grad, probe_sum, *scratch)


def column_slots_kernel(
    odd, position, count, probe, folded, left, right, x_first, x_second, canvas_in, grad_in, sum_in,
    canvas, grad, probe_sum, *scratch,
):
    side = x_first.shape[1] - 8
    half = LANES
    last = canvas.shape[1] - 1
    inner = slice(half, half + side)
    odd_x = odd[1] == 1
    canvas[:, 0, inner, :] = jnp.where(odd_x, x_second[:, :side, :], x_first[:, :side, :])
    canvas[:, last, inner, :] = jnp.where(odd_x, x_first[:, :side, :], x_second[:, :side, :])
    run_slots(
        lambda row, col: row & jnp.logical_not(col),
        position, count, probe, folded, left, right, canvas, grad, probe_sum, *scratch,
    )


def row_kernel(
    odd, position, count, probe, folded, left, right, y_first, y_second, canvas_in, grad_in, sum_in,
    canvas, grad, probe_sum, *scratch,
):
    half = LANES
    side = y_first.shape[2]
    odd_y = odd[0] == 1
    for index in range(side // LANES):
        columns = slice(index * LANES, (index + 1) * LANES)
        canvas[:, 1 + index, :half, :] = jnp.where(odd_y, y_second[:, :, columns], y_first[:, :, columns])
        canvas[:, 1 + index, half + side :, :] = jnp.where(odd_y, y_first[:, :, columns], y_second[:, :, columns])
    run_slots(
        lambda row, col: jnp.logical_not(row) & col,
        position, count, probe, folded, left, right, canvas, grad, probe_sum, *scratch,
    )


def outer_kernel(
    odd, position, count, probe, folded, left, right, x_first, x_second, corner_first, corner_second,
    canvas_in, grad_in, sum_in,
    margin_first, margin_second, side_low, side_high, middle, sums, places, canvas, grad, probe_sum, sems, *scratch,
):
    size = probe.shape[1]
    half = size // 2
    side = x_first.shape[1] - 8
    tiles = side // LANES
    inner = slice(half, half + side)
    odd_y, odd_x = odd[0] == 1, odd[1] == 1
    for index, tile in enumerate((0, 1 + tiles)):
        above, below = corner_first[:, index, :half, :], corner_second[:, index, :half, :]
        canvas[:, tile, :half, :] = jnp.where(odd_y, below, above)
        canvas[:, tile, half + side :, :] = jnp.where(odd_y, above, below)
    run_slots(
        lambda row, col: jnp.logical_not(row | col),
        position, count, probe, folded, left, right, canvas, grad, probe_sum, *scratch,
    )
    copies = []

    def send(source, target):
        copy = pltpu.make_async_copy(source, target, sems.at[len(copies)])
        copy.start()
        copies.append(copy)

    for out, odd_start in ((margin_first, half + side), (margin_second, 0)):
        rows = pl.ds(pl.multiple_of(jnp.where(odd_y, odd_start, half + side - odd_start), LANES), half)
        send(grad.at[:, :, rows, :], out)
    send(grad.at[:, 0, inner, :], side_low)
    send(grad.at[:, 1 + tiles, inner, :], side_high)
    send(grad.at[:, 1 : 1 + tiles, inner, :], middle)
    for plane in range(3):
        for index in range(2):
            sums[:, 2 * plane + index] = probe_sum[plane, index].reshape(size // 8, 8, LANES)
    beside, own = slice(half, half + 8), slice(half + 8, half + 16)
    for start, (even_ref, odd_ref) in ((0, (corner_first, corner_second)), (6, (corner_second, corner_first))):
        for index, (tile, rows) in enumerate(((0, beside), (0, own), (1, beside))):
            places[start + index] = jnp.where(odd_y, odd_ref[0, tile, rows, :], even_ref[0, tile, rows, :])
    places[3] = jnp.where(odd_x, x_second[0, side:, :], x_first[0, side:, :])
    places[4] = own_notes(position, count)
    places[5] = jnp.where(odd_x, x_first[0, side:, :], x_second[0, side:, :])
    for copy in copies:
        copy.wait()


def sides_kernel(odd, own_low, own_high, low_first, low_second, high_first, high_second, after, first, second, token):
    half = LANES
    side = own_low.shape[1]
    odd_y, odd_x = odd[0] == 1, odd[1] == 1
    for start in range(0, side, half):
        rows = slice(start, start + half)
        values = []
        for own, y_first, y_second in ((own_low, low_first, low_second), (own_high, high_first, high_second)):
            value = own[:, rows, :]
            if start == 0:
                value = value + jnp.where(odd_y, y_second[:, 0], y_first[:, 0])
            if start + half == side:
                value = value + jnp.where(odd_y, y_first[:, 0], y_second[:, 0])
            values.append(value)
        first[:, rows, :] = jnp.where(odd_x, values[1], values[0])
        second[:, rows, :] = jnp.where(odd_x, values[0], values[1])
    token[...] = jnp.zeros_like(token)


def weight_kernel(numbers, probe, scale, power, weight):
    half = LANES
    side = scale.shape[1]
    tiles = side // LANES
    weight[...] = jnp.zeros_like(weight)
    for index in range(2):
        columns = slice(index * LANES, (index + 1) * LANES)
        power[index] = probe[0, :, columns] * probe[0, :, columns] + probe[1, :, columns] * probe[1, :, columns]
    for index in range(9):
        down, across = index // 3 - 1, index % 3 - 1

        def step(slot, carry):
            row = numbers[index, 0, slot].astype(jnp.int32) + (2 * half + down * side)
            col = numbers[index, 1, slot].astype(jnp.int32) + (2 * half + across * side)
            reach = side + 2 * half

            @pl.when((row > 0) & (row < reach) & (col > 0) & (col < reach))
            def add():
                at, tile, offset = place(row, col, tiles + 1)
                add_window(weight, at, tile, offset, power[0], power[1])

            return carry

        lax.fori_loop(0, numbers[index, 2, 0].astype(jnp.int32), step, 0)
    for index in range(tiles):
        scale[index] = 1.0 / (weight[2 + index, 2 * half : 2 * half + side, :] + 1.0)


def update_kernel(odd, tile_ref, grad, y_first, y_second, scale, out):
    half = LANES
    side = tile_ref.shape[1]
    odd_y = odd[0] == 1
    for plane in range(2):
        for start in range(0, side, half):
            rows = slice(start, start + half)
            value = grad[plane, 0, rows, :]
            if start == 0:
                value = value + jnp.where(odd_y, y_second[plane, 0], y_first[plane, 0])
            if start + half == side:
                value = value + jnp.where(odd_y, y_first[plane, 0], y_second[plane, 0])
            out[plane, rows, :] = tile_ref[plane, rows, :] - value * scale[0, rows, :]


def column_kernel(odd, before, x_first, x_second, scale, out):
    use_first = odd[1] == pl.program_id(0)
    for plane in range(2):
        out[plane] = before[plane] - jnp.where(use_first, x_first[plane], x_second[plane]) * scale[0]


def plane_kernel(parts, after, later, out):
    out[...] = jnp.broadcast_to(jnp.sum(parts[...], axis=0)[None], out.shape)


def probe_kernel(index, parts, probe, after, out):
    total = jnp.sum(parts[...], axis=0)
    rows = pl.ds(pl.multiple_of(index[0] * 8, 8), 8)
    for tile in range(2):
        root = jnp.sqrt(total[4 + tile] + 1.0)
        for plane in range(2):
            new = probe[plane, rows, tile * LANES : (tile + 1) * LANES] - total[2 * plane + tile] / root
            out[:, 2 * plane + tile] = jnp.broadcast_to(new[None], (out.shape[0], 8, LANES))


def join_kernel(pieces, out):
    for plane in range(2):
        for tile in range(2):
            value = pieces[:, 2 * plane + tile]
            out[plane, :, tile * LANES : (tile + 1) * LANES] = value.reshape(out.shape[1], LANES)


def swap(first, second, axis):
    count = lax.axis_size(axis)
    across = [pair for low in range(1, count - 1, 2) for pair in ((low, low + 1), (low + 1, low))]
    return lax.ppermute(first, axis, across), lax.ppermute(second, axis, [(index, index ^ 1) for index in range(count)])


def keep(value):
    return pltpu.with_memory_space_constraint(value, pltpu.HBM)


def params(mib):
    return pltpu.CompilerParams(vmem_limit_bytes=mib * 2**20)


def cost(mib):
    return pl.CostEstimate(flops=0, bytes_accessed=mib * 2**20, transcendentals=0)


def solution(mesh):
    rows, cols = mesh.shape["ty"], mesh.shape["tx"]
    near_y, near_z = 8, 4
    planes = [
        [(8 * high + row) * cols + near_z * x + low for row in range(near_y) for x in range(cols // near_z)]
        for high in range(rows // near_y)
        for low in range(near_z)
    ]
    lines = [list(line) for line in zip(*planes)]

    def trade(pieces, groups):
        return lax.all_to_all(pieces, ("ty", "tx"), 0, 0, axis_index_groups=groups, tiled=True)

    def per_device(object_field, probe, intensity, positions, counts):
        side = object_field.shape[1]
        size = probe.shape[1]
        half = size // 2
        slots = intensity.shape[2]
        tiles = side // LANES
        position = positions[:, 0, 0, :]
        count = counts[0]
        row, col = lax.axis_index("ty"), lax.axis_index("tx")
        piece = jnp.bitwise_and(row, near_y - 1) * (cols // near_z) + lax.shift_right_logical(col, 2)
        piece = piece.reshape(1).astype(jnp.int32)
        left, right = (jnp.asarray(table) for table in half_tables(size))
        gather_left, gather_right = (jnp.asarray(table) for table in parity_tables(size))

        odd = jnp.bitwise_and(jnp.stack([row, col]), 1).astype(jnp.int32)

        strip = jax.ShapeDtypeStruct((2, side + 8, LANES), F32)
        edge = jax.ShapeDtypeStruct((2, half, side), F32)
        x_first, x_second, y_first, y_second = pl.pallas_call(
            edge_kernel,
            out_shape=(strip, strip, edge, edge),
            in_specs=[SMEM] * 3 + [VMEM],
            out_specs=(VMEM,) * 4,
            compiler_params=params(6),
            cost_estimate=cost(4),
            name="edges",
        )(odd, position, count, object_field)
        x_first, x_second = swap(x_first, x_second, "tx")
        y_first, y_second = swap(y_first, y_second, "ty")
        folded = pl.pallas_call(
            fold_kernel,
            out_shape=jax.ShapeDtypeStruct((slots, size, size), F32),
            in_specs=[SMEM, VMEM, VMEM, VMEM],
            out_specs=VMEM,
            scratch_shapes=[pltpu.VMEM((size, 3 * size), BF16)],
            compiler_params=params(8),
            cost_estimate=cost(6),
            name="fold",
        )(count, intensity[0, 0], gather_left, gather_right)
        members = len(planes[0])
        lanes = 2
        scratch = [
            pltpu.SMEM((slots,), jnp.int32),
            pltpu.VMEM((lanes, 2, 2, size, LANES), F32),
            pltpu.VMEM((lanes, 2, 3 * size, size), BF16),
            pltpu.VMEM((lanes, 2, size, 3 * size), BF16),
        ]
        state = (
            pltpu.VMEM((2, tiles + 2, side + size, LANES), F32),
            pltpu.VMEM((2, tiles + 2, side + size, LANES), F32),
            pltpu.VMEM((3, 2, size, LANES), F32),
        )
        given = (odd, position, count, probe, folded, left, right)
        canvas, grad, probe_sum, token = pl.pallas_call(
            core_kernel,
            out_shape=state + (jax.ShapeDtypeStruct((8, LANES), F32),),
            in_specs=[SMEM] * 3 + [VMEM] * 5,
            out_specs=(VMEM,) * 4,
            scratch_shapes=scratch,
            compiler_params=params(26),
            cost_estimate=cost(16),
            name="core_slots",
        )(*given, object_field)
        corner = jax.ShapeDtypeStruct((2, 2, half + 16, LANES), F32)
        corners = pl.pallas_call(
            corner_kernel,
            out_shape=(corner, corner),
            in_specs=[SMEM] * 3 + [VMEM] * 2 + [HBM],
            out_specs=(VMEM, VMEM),
            compiler_params=params(4),
            cost_estimate=cost(4),
            name="corners",
        )(odd, position, count, x_first, x_second, token)
        corners = swap(*corners, "ty")

        canvas, grad, probe_sum = pl.pallas_call(
            column_slots_kernel,
            out_shape=state,
            in_specs=[SMEM] * 3 + [VMEM] * 9,
            out_specs=(VMEM,) * 3,
            scratch_shapes=scratch,
            input_output_aliases={9: 0, 10: 1, 11: 2},
            compiler_params=params(26),
            cost_estimate=cost(16),
            name="column_slots",
        )(*given, x_first, x_second, canvas, grad, probe_sum)
        canvas, grad, probe_sum = pl.pallas_call(
            row_kernel,
            out_shape=state,
            in_specs=[SMEM] * 3 + [VMEM] * 9,
            out_specs=(VMEM,) * 3,
            scratch_shapes=scratch,
            input_output_aliases={9: 0, 10: 1, 11: 2},
            compiler_params=params(26),
            cost_estimate=cost(8),
            name="row_slots",
        )(*given, y_first, y_second, canvas, grad, probe_sum)
        margin = pltpu.HBM((2, tiles + 2, half, LANES), F32)
        column = pltpu.HBM((2, side, LANES), F32)
        margin_first, margin_second, side_low, side_high, middle, sums, places, *_ = pl.pallas_call(
            outer_kernel,
            out_shape=(
                margin, margin, column, column,
                pltpu.HBM((2, tiles, side, LANES), F32),
                pltpu.HBM((members, 6, 8, LANES), F32),
                jax.ShapeDtypeStruct((9, 8, LANES), F32),
            ) + state,
            in_specs=[SMEM] * 3 + [VMEM] * 11,
            out_specs=(HBM,) * 5 + (VMEM,) * 5,
            scratch_shapes=[pltpu.SemaphoreType.DMA((5,))] + scratch,
            input_output_aliases={11: 7, 12: 8, 13: 9},
            compiler_params=params(26),
            cost_estimate=cost(16),
            name="outer_slots",
        )(*given, x_first, x_second, *corners, canvas, grad, probe_sum)

        margin_first, margin_second = swap(margin_first, margin_second, "ty")
        scale = pl.pallas_call(
            weight_kernel,
            out_shape=jax.ShapeDtypeStruct((tiles, side, LANES), F32),
            in_specs=[SMEM, VMEM],
            out_specs=VMEM,
            scratch_shapes=[
                pltpu.VMEM((2, size, LANES), F32),
                pltpu.VMEM((tiles + 4, side + 2 * size, LANES), F32),
            ],
            compiler_params=params(8),
            cost_estimate=cost(8),
            name="weights",
        )(places, keep(probe))
        parts = trade(sums, planes)
        parts = pl.pallas_call(
            plane_kernel,
            out_shape=pltpu.HBM((len(lines[0]), 6, 8, LANES), F32),
            in_specs=[VMEM, HBM, HBM],
            out_specs=VMEM,
            compiler_params=params(6),
            cost_estimate=cost(2),
            name="plane_sum",
        )(parts, scale, margin_first)
        parts = trade(parts, lines)
        strip = pltpu.HBM((2, side, LANES), F32)
        whole = pl.BlockSpec((2, side, LANES), lambda index: (0, 0, 0))
        first_tile = pl.BlockSpec((2, 1, half, LANES), lambda index: (0, 0, 0, 0))
        last_tile = pl.BlockSpec((2, 1, half, LANES), lambda index: (0, tiles + 1, 0, 0))
        *margins, token = pl.pallas_call(
            sides_kernel,
            out_shape=(strip, strip, jax.ShapeDtypeStruct((8, LANES), F32)),
            grid=(1,),
            in_specs=[SMEM, whole, whole, first_tile, first_tile, last_tile, last_tile, HBM],
            out_specs=(whole, whole, pl.BlockSpec((8, LANES), lambda index: (0, 0))),
            compiler_params=params(8),
            cost_estimate=cost(16),
            name="sides",
        )(odd, keep(side_low), keep(side_high), margin_first, margin_second, margin_first, margin_second, parts)
        x_first, x_second = swap(*margins, "tx")

        pieces = pl.pallas_call(
            probe_kernel,
            out_shape=pltpu.HBM((members, 4, 8, LANES), F32),
            in_specs=[SMEM, VMEM, VMEM, HBM],
            out_specs=VMEM,
            compiler_params=params(6),
            cost_estimate=cost(2),
            name="probe_rows",
        )(piece, parts, keep(probe), token)
        probe_new = pl.pallas_call(
            join_kernel,
            out_shape=jax.ShapeDtypeStruct(probe.shape, F32),
            in_specs=[VMEM],
            out_specs=VMEM,
            compiler_params=params(6),
            cost_estimate=cost(2),
            name="join",
        )(trade(pieces, planes))

        column = pl.BlockSpec((2, side, LANES), lambda index: (0, 0, index))
        flat = pl.BlockSpec((2, 1, half, LANES), lambda index: (0, index + 1, 0, 0))
        object_new = pl.pallas_call(
            update_kernel,
            out_shape=jax.ShapeDtypeStruct(object_field.shape, F32),
            grid=(tiles,),
            in_specs=[
                SMEM, column, pl.BlockSpec((2, 1, side, LANES), lambda index: (0, index, 0, 0)), flat, flat,
                pl.BlockSpec((1, side, LANES), lambda index: (index, 0, 0)),
            ],
            out_specs=column,
            compiler_params=params(8),
            cost_estimate=cost(8),
            name="update",
        )(odd, keep(object_field), keep(middle), margin_first, margin_second, scale)
        ends = pl.BlockSpec((2, side, LANES), lambda index: (0, 0, index * (tiles - 1)))
        object_new = pl.pallas_call(
            column_kernel,
            out_shape=jax.ShapeDtypeStruct(object_field.shape, F32),
            grid=(2,),
            in_specs=[SMEM, ends, whole, whole, pl.BlockSpec((1, side, LANES), lambda index: (index * (tiles - 1), 0, 0))],
            out_specs=ends,
            input_output_aliases={1: 0},
            compiler_params=params(8),
            name="columns",
        )(odd, object_new, x_first, x_second, scale)
        return (object_new, probe_new)

    in_specs = (
        P(None, "ty", "tx"),
        P(),
        P("ty", "tx", None, None, None),
        P(None, "ty", "tx", None),
        P("ty", "tx"),
    )
    out_specs = (P(None, "ty", "tx"), P())
    return jax.shard_map(per_device, mesh=mesh, in_specs=in_specs, out_specs=out_specs, check_vma=False)
```

```python
import numpy as np
import ml_dtypes
import jax
import jax.numpy as jnp
from jax import lax
from jax.experimental import pallas as pl
from jax.experimental.pallas import tpu as pltpu
from jax.sharding import PartitionSpec as P

BF16 = jnp.bfloat16
F32 = jnp.float32
LANES = 128
VMEM = pl.BlockSpec(memory_space=pltpu.VMEM)
SMEM = pl.BlockSpec(memory_space=pltpu.SMEM)
HBM = pl.BlockSpec(memory_space=pltpu.HBM)
def split_host(table):
    high = table.astype(ml_dtypes.bfloat16)
    low = (table - high.astype(np.float64)).astype(ml_dtypes.bfloat16)
    return high, low


def half_tables(size):
    half = size // 2
    left, right = [], []
    for parity in range(2):
        product = (2 * np.arange(half)[:, None] + parity) * np.arange(half)[None, :] % size
        angle = 2.0 * np.pi * product / size
        cos, sin = np.cos(angle) / np.sqrt(size), np.sin(angle) / np.sqrt(size)
        base = np.block([[cos, sin], [-sin, cos]])
        for table in (base, base.T):
            high, low = split_host(table)
            left.append(np.concatenate([high, high, low], axis=1))
            right.append(np.concatenate([high, high, low], axis=0))
    return np.stack(left), np.stack(right)


def parity_tables(size):
    order = np.concatenate([np.arange(0, size, 2), np.arange(1, size, 2)])
    gather = np.eye(size)[order].astype(ml_dtypes.bfloat16)
    return np.concatenate([gather] * 3, axis=1), np.concatenate([gather.T] * 3, axis=0)


def matmul(left, right):
    return jnp.dot(left, right, preferred_element_type=F32)


def split(value):
    high = value.astype(BF16)
    return high, (value - high.astype(F32)).astype(BF16)


def put_rows(ref, start, columns, value):
    rows = value.shape[0]
    high, low = split(value)
    third = ref.shape[0] // 3
    ref[start : start + rows, columns] = high
    ref[third + start : third + start + rows, columns] = low
    ref[2 * third + start : 2 * third + start + rows, columns] = high


def put_columns(ref, rows, start, value):
    width = value.shape[1]
    high, low = split(value)
    third = ref.shape[1] // 3
    ref[rows, start : start + width] = high
    ref[rows, third + start : third + start + width] = low
    ref[rows, 2 * third + start : 2 * third + start + width] = high


def place(row, col, last):
    tile = jnp.minimum(lax.shift_right_logical(col, 7), last)
    return row, tile, col - tile * LANES


def add_window(accumulate, row, tile, offset, first, second):
    rows = first.shape[0]
    turn = jnp.bitwise_and(offset, LANES - 1)
    kept = lax.broadcasted_iota(jnp.int32, first.shape, 1) >= offset
    first = pltpu.roll(first, turn, 1)
    second = pltpu.roll(second, turn, 1)
    where = pl.ds(row, rows)
    accumulate[tile, where, :] += jnp.where(kept, first, 0.0)
    accumulate[tile + 1, where, :] += jnp.where(kept, second, first)
    accumulate[tile + 2, where, :] += jnp.where(kept, 0.0, second)


def fold_kernel(count, measured, gather_left, gather_right, folded, parts):
    size = measured.shape[1]

    def three(value):
        high = value.astype(BF16)
        rest = value - high.astype(F32)
        middle = rest.astype(BF16)
        return high, middle, (rest - middle.astype(F32)).astype(BF16)

    def step(slot, carry):
        for index, part in enumerate(three(measured[slot])):
            parts[:, index * size : (index + 1) * size] = part
        value = matmul(parts[...], gather_right[...])
        folded[slot] = matmul(gather_left[...], jnp.concatenate(three(value), axis=0))
        return carry

    lax.fori_loop(0, count[0], step, 0)


def own_notes(position, count):
    row = lax.broadcasted_iota(jnp.int32, (8, LANES), 0)
    lane = lax.broadcasted_iota(jnp.int32, (8, LANES), 1)
    notes = jnp.where(row == 2, count[0], 0)
    for slot in range(position.shape[1]):
        for axis in range(2):
            notes = jnp.where((row == axis) & (lane == slot), position[axis, slot], notes)
    return notes.astype(F32)


def edge_kernel(odd, position, count, tile_ref, x_first, x_second, y_first, y_second):
    half = LANES
    side = tile_ref.shape[1]
    odd_y, odd_x = odd[0] == 1, odd[1] == 1
    notes = own_notes(position, count)
    low, high = tile_ref[:, :, :half], tile_ref[:, :, side - half :]
    x_first[:, :side, :] = jnp.where(odd_x, high, low)
    x_second[:, :side, :] = jnp.where(odd_x, low, high)
    for out in (x_first, x_second):
        for plane in range(2):
            out[plane, side:, :] = notes
    low, high = tile_ref[:, :half, :], tile_ref[:, side - half :, :]
    y_first[...] = jnp.where(odd_y, high, low)
    y_second[...] = jnp.where(odd_y, low, high)


def corner_kernel(odd, position, count, x_first, x_second, after, first, second):
    half = LANES
    side = x_first.shape[1] - 8
    far = side - half
    odd_x = odd[1] == 1
    notes = own_notes(position, count)
    for out, odd_start in ((first, far), (second, 0)):
        rows = pl.ds(pl.multiple_of(jnp.where(odd[0] == 1, odd_start, far - odd_start), LANES), half)
        for index, (even_ref, odd_ref) in enumerate(((x_first, x_second), (x_second, x_first))):
            out[:, index, :half, :] = jnp.where(odd_x, odd_ref[:, rows, :], even_ref[:, rows, :])
            out[:, index, half : half + 8, :] = jnp.where(odd_x, odd_ref[:, side:, :], even_ref[:, side:, :])
            for plane in range(2):
                out[plane, index, half + 8 :, :] = notes


def slot_stages(row, tile, offset, live, probe, measured, left, right, canvas, grad, probe_sum, patch, rhs, lhs):
    size = probe.shape[1]
    half = size // 2
    near, far = slice(0, half), slice(half, size)
    turn = jnp.bitwise_and(LANES - offset, LANES - 1)
    kept = lax.broadcasted_iota(jnp.int32, (size, LANES), 1) < LANES - offset
    for plane in range(2):
        raw = [pltpu.roll(canvas[plane, tile + index, pl.ds(row, size), :], turn, 1) for index in range(3)]
        patch[plane, 0] = jnp.where(kept, raw[0], raw[1])
        patch[plane, 1] = jnp.where(kept, raw[1], raw[2])
    for index, columns in enumerate((near, far)):
        probe_re, probe_im = probe[0, :, columns], probe[1, :, columns]
        patch_re, patch_im = patch[0, index], patch[1, index]
        exit_re = probe_re * patch_re - probe_im * patch_im
        exit_im = probe_re * patch_im + probe_im * patch_re
        probe_sum[2, index] += (patch_re * patch_re + patch_im * patch_im) * live
        put_rows(rhs.at[0], 0, columns, exit_re[:half] + exit_re[half:])
        put_rows(rhs.at[0], half, columns, exit_im[:half] + exit_im[half:])
        put_rows(rhs.at[1], 0, columns, exit_re[:half] - exit_re[half:])
        put_rows(rhs.at[1], half, columns, exit_im[:half] - exit_im[half:])
    yield
    for parity in range(2):
        value = matmul(left[2 * parity], rhs[parity])
        rows = slice(parity * half, (parity + 1) * half)
        put_columns(lhs.at[0], rows, 0, value[:half, near] + value[:half, far])
        put_columns(lhs.at[0], rows, half, value[half:, near] + value[half:, far])
        put_columns(lhs.at[1], rows, 0, value[:half, near] - value[:half, far])
        put_columns(lhs.at[1], rows, half, value[half:, near] - value[half:, far])
        yield
    everything = slice(0, size)
    for parity in range(2):
        value = matmul(lhs[parity], right[2 * parity + 1])
        wave_re, wave_im = value[:, near], value[:, far]
        columns = slice(parity * half, (parity + 1) * half)
        excess = (wave_re * wave_re + wave_im * wave_im - measured[:, columns]) * live
        put_columns(lhs.at[parity], everything, 0, excess * wave_re)
        put_columns(lhs.at[parity], everything, half, excess * wave_im)
        yield
    back = []
    for parity in range(2):
        back.append(matmul(lhs[parity], right[2 * parity]))
    for parity in range(2):
        rows = slice(parity * half, (parity + 1) * half)
        put_rows(rhs.at[parity], 0, near, back[0][rows, near] + back[1][rows, near])
        put_rows(rhs.at[parity], half, near, back[0][rows, far] + back[1][rows, far])
        put_rows(rhs.at[parity], 0, far, back[0][rows, near] - back[1][rows, near])
        put_rows(rhs.at[parity], half, far, back[0][rows, far] - back[1][rows, far])
    yield
    even = matmul(left[1], rhs[0])
    odd = matmul(left[3], rhs[1])
    pieces = []
    for index, columns in enumerate((near, far)):
        chi_re, chi_im = (
            jnp.concatenate([even[rows, columns] + odd[rows, columns], even[rows, columns] - odd[rows, columns]], axis=0)
            for rows in (near, far)
        )
        probe_re, probe_im = probe[0, :, columns], probe[1, :, columns]
        patch_re, patch_im = patch[0, index], patch[1, index]
        probe_sum[0, index] += patch_re * chi_re + patch_im * chi_im
        probe_sum[1, index] += patch_re * chi_im - patch_im * chi_re
        pieces.append((probe_re * chi_re + probe_im * chi_im, probe_re * chi_im - probe_im * chi_re))
    for plane in range(2):
        add_window(grad.at[plane], row, tile, offset, pieces[0][plane], pieces[1][plane])
    yield


def run_slots(wanted, position, count, probe, folded, left, right, canvas, grad, probe_sum, order, patch, rhs, lhs):
    size = probe.shape[1]
    half = size // 2
    tiles = canvas.shape[1] - 2
    reach = tiles * LANES - size

    def pick(slot, found):
        row, col = position[0, slot], position[1, slot]
        take = wanted((row >= 0) & (row <= reach), (col >= 0) & (col <= reach))

        @pl.when(take)
        def keep():
            order[found] = slot

        return found + jnp.where(take, 1, 0)

    total = lax.fori_loop(0, count[0], pick, 0)
    lanes = patch.shape[0]

    def step(group, carry):
        stages = []
        for lane in range(lanes):
            index = lanes * group + lane
            live = jnp.where(index < total, 1.0, 0.0)
            slot = order[jnp.minimum(index, total - 1)]
            row, tile, offset = place(position[0, slot] + half, position[1, slot] + half, tiles - 1)
            stages.append(slot_stages(
                row, tile, offset, live, probe, folded.at[slot], left, right, canvas, grad, probe_sum,
                patch.at[lane], rhs.at[lane], lhs.at[lane],
            ))
        for _ in zip(*stages):
            pass
        return carry

    lax.fori_loop(0, lax.div(total + (lanes - 1), lanes), step, 0)


def core_kernel(odd, position, count, probe, folded, left, right, tile_ref, canvas, grad, probe_sum, token, *scratch):
    side = tile_ref.shape[1]
    half = LANES
    tiles = side // LANES
    canvas[...] = jnp.zeros_like(canvas)
    for index in range(tiles):
        canvas[:, 1 + index, half : half + side, :] = tile_ref[:, :, index * LANES : (index + 1) * LANES]
    grad[...] = jnp.zeros_like(grad)
    probe_sum[...] = jnp.zeros_like(probe_sum)
    token[...] = jnp.zeros_like(token)
    run_slots(lambda row, col: row & col, position, count, probe, folded, left, right, canvas, grad, probe_sum, *scratch)


def column_slots_kernel(
    odd, position, count, probe, folded, left, right, x_first, x_second, canvas_in, grad_in, sum_in,
    canvas, grad, probe_sum, *scratch,
):
    side = x_first.shape[1] - 8
    half = LANES
    last = canvas.shape[1] - 1
    inner = slice(half, half + side)
    odd_x = odd[1] == 1
    canvas[:, 0, inner, :] = jnp.where(odd_x, x_second[:, :side, :], x_first[:, :side, :])
    canvas[:, last, inner, :] = jnp.where(odd_x, x_first[:, :side, :], x_second[:, :side, :])
    run_slots(
        lambda row, col: row & jnp.logical_not(col),
        position, count, probe, folded, left, right, canvas, grad, probe_sum, *scratch,
    )


def row_kernel(
    odd, position, count, probe, folded, left, right, y_first, y_second, canvas_in, grad_in, sum_in,
    canvas, grad, probe_sum, *scratch,
):
    half = LANES
    side = y_first.shape[2]
    odd_y = odd[0] == 1
    for index in range(side // LANES):
        columns = slice(index * LANES, (index + 1) * LANES)
        canvas[:, 1 + index, :half, :] = jnp.where(odd_y, y_second[:, :, columns], y_first[:, :, columns])
        canvas[:, 1 + index, half + side :, :] = jnp.where(odd_y, y_first[:, :, columns], y_second[:, :, columns])
    run_slots(
        lambda row, col: jnp.logical_not(row) & col,
        position, count, probe, folded, left, right, canvas, grad, probe_sum, *scratch,
    )


def outer_kernel(
    odd, position, count, probe, folded, left, right, x_first, x_second, corner_first, corner_second,
    canvas_in, grad_in, sum_in,
    margin_first, margin_second, side_low, side_high, middle, sums, places, canvas, grad, probe_sum, sems, *scratch,
):
    size = probe.shape[1]
    half = size // 2
    side = x_first.shape[1] - 8
    tiles = side // LANES
    inner = slice(half, half + side)
    odd_y, odd_x = odd[0] == 1, odd[1] == 1
    for index, tile in enumerate((0, 1 + tiles)):
        above, below = corner_first[:, index, :half, :], corner_second[:, index, :half, :]
        canvas[:, tile, :half, :] = jnp.where(odd_y, below, above)
        canvas[:, tile, half + side :, :] = jnp.where(odd_y, above, below)
    run_slots(
        lambda row, col: jnp.logical_not(row | col),
        position, count, probe, folded, left, right, canvas, grad, probe_sum, *scratch,
    )
    copies = []

    def send(source, target):
        copy = pltpu.make_async_copy(source, target, sems.at[len(copies)])
        copy.start()
        copies.append(copy)

    for out, odd_start in ((margin_first, half + side), (margin_second, 0)):
        rows = pl.ds(pl.multiple_of(jnp.where(odd_y, odd_start, half + side - odd_start), LANES), half)
        send(grad.at[:, :, rows, :], out)
    send(grad.at[:, 0, inner, :], side_low)
    send(grad.at[:, 1 + tiles, inner, :], side_high)
    send(grad.at[:, 1 : 1 + tiles, inner, :], middle)
    for plane in range(3):
        for index in range(2):
            sums[:, 2 * plane + index] = probe_sum[plane, index].reshape(size // 8, 8, LANES)
    beside, own = slice(half, half + 8), slice(half + 8, half + 16)
    for start, (even_ref, odd_ref) in ((0, (corner_first, corner_second)), (6, (corner_second, corner_first))):
        for index, (tile, rows) in enumerate(((0, beside), (0, own), (1, beside))):
            places[start + index] = jnp.where(odd_y, odd_ref[0, tile, rows, :], even_ref[0, tile, rows, :])
    places[3] = jnp.where(odd_x, x_second[0, side:, :], x_first[0, side:, :])
    places[4] = own_notes(position, count)
    places[5] = jnp.where(odd_x, x_first[0, side:, :], x_second[0, side:, :])
    for copy in copies:
        copy.wait()


def sides_kernel(odd, own_low, own_high, low_first, low_second, high_first, high_second, after, first, second):
    half = LANES
    side = own_low.shape[1]
    odd_y, odd_x = odd[0] == 1, odd[1] == 1
    for start in range(0, side, half):
        rows = slice(start, start + half)
        values = []
        for own, y_first, y_second in ((own_low, low_first, low_second), (own_high, high_first, high_second)):
            value = own[:, rows, :]
            if start == 0:
                value = value + jnp.where(odd_y, y_second[:, 0], y_first[:, 0])
            if start + half == side:
                value = value + jnp.where(odd_y, y_first[:, 0], y_second[:, 0])
            values.append(value)
        first[:, rows, :] = jnp.where(odd_x, values[1], values[0])
        second[:, rows, :] = jnp.where(odd_x, values[0], values[1])


def weight_kernel(numbers, probe, scale, power, weight):
    half = LANES
    side = scale.shape[1]
    tiles = side // LANES
    weight[...] = jnp.zeros_like(weight)
    for index in range(2):
        columns = slice(index * LANES, (index + 1) * LANES)
        power[index] = probe[0, :, columns] * probe[0, :, columns] + probe[1, :, columns] * probe[1, :, columns]
    for index in range(9):
        down, across = index // 3 - 1, index % 3 - 1

        def step(slot, carry):
            row = numbers[index, 0, slot].astype(jnp.int32) + (2 * half + down * side)
            col = numbers[index, 1, slot].astype(jnp.int32) + (2 * half + across * side)
            reach = side + 2 * half

            @pl.when((row > 0) & (row < reach) & (col > 0) & (col < reach))
            def add():
                at, tile, offset = place(row, col, tiles + 1)
                add_window(weight, at, tile, offset, power[0], power[1])

            return carry

        lax.fori_loop(0, numbers[index, 2, 0].astype(jnp.int32), step, 0)
    for index in range(tiles):
        scale[index] = 1.0 / (weight[2 + index, 2 * half : 2 * half + side, :] + 1.0)


def update_kernel(odd, tile_ref, grad, y_first, y_second, scale, out):
    half = LANES
    side = tile_ref.shape[1]
    odd_y = odd[0] == 1
    for plane in range(2):
        for start in range(0, side, half):
            rows = slice(start, start + half)
            value = grad[plane, 0, rows, :]
            if start == 0:
                value = value + jnp.where(odd_y, y_second[plane, 0], y_first[plane, 0])
            if start + half == side:
                value = value + jnp.where(odd_y, y_first[plane, 0], y_second[plane, 0])
            out[plane, rows, :] = tile_ref[plane, rows, :] - value * scale[0, rows, :]


def column_kernel(odd, x_first, x_second, scale, whole, out, columns, sems):
    half = LANES
    far = out.shape[2] - half
    odd_x = odd[1] == 1
    places = [out.at[:, :, start : start + half] for start in (0, far)]
    loads = [pltpu.make_async_copy(place, columns.at[index], sems.at[index]) for index, place in enumerate(places)]
    stores = [pltpu.make_async_copy(columns.at[index], place, sems.at[2 + index]) for index, place in enumerate(places)]
    for load in loads:
        load.start()
    for index, (tile, even_ref, odd_ref) in enumerate(((0, x_first, x_second), (scale.shape[0] - 1, x_second, x_first))):
        loads[index].wait()
        for plane in range(2):
            strip = jnp.where(odd_x, odd_ref[plane], even_ref[plane])
            columns[index, plane] = columns[index, plane] - strip * scale[tile]
        stores[index].start()
    for store in stores:
        store.wait()


def plane_kernel(parts, after, out):
    out[...] = jnp.broadcast_to(jnp.sum(parts[...], axis=0)[None], out.shape)


def probe_kernel(index, parts, probe, out):
    total = jnp.sum(parts[...], axis=0)
    rows = pl.ds(pl.multiple_of(index[0] * 8, 8), 8)
    for tile in range(2):
        root = jnp.sqrt(total[4 + tile] + 1.0)
        for plane in range(2):
            new = probe[plane, rows, tile * LANES : (tile + 1) * LANES] - total[2 * plane + tile] / root
            out[:, 2 * plane + tile] = jnp.broadcast_to(new[None], (out.shape[0], 8, LANES))


def join_kernel(pieces, out):
    for plane in range(2):
        for tile in range(2):
            value = pieces[:, 2 * plane + tile]
            out[plane, :, tile * LANES : (tile + 1) * LANES] = value.reshape(out.shape[1], LANES)


def swap(first, second, axis):
    count = lax.axis_size(axis)
    across = [pair for low in range(1, count - 1, 2) for pair in ((low, low + 1), (low + 1, low))]
    return lax.ppermute(first, axis, across), lax.ppermute(second, axis, [(index, index ^ 1) for index in range(count)])


def keep(value):
    return pltpu.with_memory_space_constraint(value, pltpu.HBM)


def params(mib):
    return pltpu.CompilerParams(vmem_limit_bytes=mib * 2**20)


def cost(mib):
    return pl.CostEstimate(flops=0, bytes_accessed=mib * 2**20, transcendentals=0)


def solution(mesh):
    rows, cols = mesh.shape["ty"], mesh.shape["tx"]
    near_y, near_z = 8, 4
    planes = [
        [(8 * high + row) * cols + near_z * x + low for row in range(near_y) for x in range(cols // near_z)]
        for high in range(rows // near_y)
        for low in range(near_z)
    ]
    lines = [list(line) for line in zip(*planes)]

    def trade(pieces, groups):
        return lax.all_to_all(pieces, ("ty", "tx"), 0, 0, axis_index_groups=groups, tiled=True)

    def per_device(object_field, probe, intensity, positions, counts):
        side = object_field.shape[1]
        size = probe.shape[1]
        half = size // 2
        slots = intensity.shape[2]
        tiles = side // LANES
        position = positions[:, 0, 0, :]
        count = counts[0]
        row, col = lax.axis_index("ty"), lax.axis_index("tx")
        piece = jnp.bitwise_and(row, near_y - 1) * (cols // near_z) + lax.shift_right_logical(col, 2)
        piece = piece.reshape(1).astype(jnp.int32)
        left, right = (jnp.asarray(table) for table in half_tables(size))
        gather_left, gather_right = (jnp.asarray(table) for table in parity_tables(size))

        odd = jnp.bitwise_and(jnp.stack([row, col]), 1).astype(jnp.int32)

        strip = jax.ShapeDtypeStruct((2, side + 8, LANES), F32)
        edge = jax.ShapeDtypeStruct((2, half, side), F32)
        x_first, x_second, y_first, y_second = pl.pallas_call(
            edge_kernel,
            out_shape=(strip, strip, edge, edge),
            in_specs=[SMEM] * 3 + [VMEM],
            out_specs=(VMEM,) * 4,
            compiler_params=params(6),
            cost_estimate=cost(4),
            name="edges",
        )(odd, position, count, object_field)
        x_first, x_second = swap(x_first, x_second, "tx")
        y_first, y_second = swap(y_first, y_second, "ty")
        folded = pl.pallas_call(
            fold_kernel,
            out_shape=jax.ShapeDtypeStruct((slots, size, size), F32),
            in_specs=[SMEM, VMEM, VMEM, VMEM],
            out_specs=VMEM,
            scratch_shapes=[pltpu.VMEM((size, 3 * size), BF16)],
            compiler_params=params(8),
            cost_estimate=cost(6),
            name="fold",
        )(count, intensity[0, 0], gather_left, gather_right)
        members = len(planes[0])
        lanes = 2
        scratch = [
            pltpu.SMEM((slots,), jnp.int32),
            pltpu.VMEM((lanes, 2, 2, size, LANES), F32),
            pltpu.VMEM((lanes, 2, 3 * size, size), BF16),
            pltpu.VMEM((lanes, 2, size, 3 * size), BF16),
        ]
        state = (
            pltpu.VMEM((2, tiles + 2, side + size, LANES), F32),
            pltpu.VMEM((2, tiles + 2, side + size, LANES), F32),
            pltpu.VMEM((3, 2, size, LANES), F32),
        )
        given = (odd, position, count, probe, folded, left, right)
        canvas, grad, probe_sum, token = pl.pallas_call(
            core_kernel,
            out_shape=state + (jax.ShapeDtypeStruct((8, LANES), F32),),
            in_specs=[SMEM] * 3 + [VMEM] * 5,
            out_specs=(VMEM,) * 4,
            scratch_shapes=scratch,
            compiler_params=params(26),
            cost_estimate=cost(16),
            name="core_slots",
        )(*given, object_field)
        corner = jax.ShapeDtypeStruct((2, 2, half + 16, LANES), F32)
        corners = pl.pallas_call(
            corner_kernel,
            out_shape=(corner, corner),
            in_specs=[SMEM] * 3 + [VMEM] * 2 + [HBM],
            out_specs=(VMEM, VMEM),
            compiler_params=params(4),
            cost_estimate=cost(4),
            name="corners",
        )(odd, position, count, x_first, x_second, token)
        corners = swap(*corners, "ty")

        canvas, grad, probe_sum = pl.pallas_call(
            column_slots_kernel,
            out_shape=state,
            in_specs=[SMEM] * 3 + [VMEM] * 9,
            out_specs=(VMEM,) * 3,
            scratch_shapes=scratch,
            input_output_aliases={9: 0, 10: 1, 11: 2},
            compiler_params=params(26),
            cost_estimate=cost(16),
            name="column_slots",
        )(*given, x_first, x_second, canvas, grad, probe_sum)
        canvas, grad, probe_sum = pl.pallas_call(
            row_kernel,
            out_shape=state,
            in_specs=[SMEM] * 3 + [VMEM] * 9,
            out_specs=(VMEM,) * 3,
            scratch_shapes=scratch,
            input_output_aliases={9: 0, 10: 1, 11: 2},
            compiler_params=params(26),
            cost_estimate=cost(8),
            name="row_slots",
        )(*given, y_first, y_second, canvas, grad, probe_sum)
        margin = pltpu.HBM((2, tiles + 2, half, LANES), F32)
        column = pltpu.HBM((2, side, LANES), F32)
        margin_first, margin_second, side_low, side_high, middle, sums, places, *_ = pl.pallas_call(
            outer_kernel,
            out_shape=(
                margin, margin, column, column,
                pltpu.HBM((2, tiles, side, LANES), F32),
                pltpu.HBM((members, 6, 8, LANES), F32),
                jax.ShapeDtypeStruct((9, 8, LANES), F32),
            ) + state,
            in_specs=[SMEM] * 3 + [VMEM] * 11,
            out_specs=(HBM,) * 5 + (VMEM,) * 5,
            scratch_shapes=[pltpu.SemaphoreType.DMA((5,))] + scratch,
            input_output_aliases={11: 7, 12: 8, 13: 9},
            compiler_params=params(26),
            cost_estimate=cost(16),
            name="outer_slots",
        )(*given, x_first, x_second, *corners, canvas, grad, probe_sum)

        margin_first, margin_second = swap(margin_first, margin_second, "ty")
        scale = pl.pallas_call(
            weight_kernel,
            out_shape=jax.ShapeDtypeStruct((tiles, side, LANES), F32),
            in_specs=[SMEM, VMEM],
            out_specs=VMEM,
            scratch_shapes=[
                pltpu.VMEM((2, size, LANES), F32),
                pltpu.VMEM((tiles + 4, side + 2 * size, LANES), F32),
            ],
            compiler_params=params(8),
            cost_estimate=cost(8),
            name="weights",
        )(places, keep(probe))
        parts = trade(sums, planes)
        parts = pl.pallas_call(
            plane_kernel,
            out_shape=pltpu.HBM((len(lines[0]), 6, 8, LANES), F32),
            in_specs=[VMEM, HBM],
            out_specs=VMEM,
            compiler_params=params(6),
            cost_estimate=cost(2),
            name="plane_sum",
        )(parts, scale)
        parts = trade(parts, lines)
        strip = pltpu.HBM((2, side, LANES), F32)
        whole = pl.BlockSpec((2, side, LANES), lambda index: (0, 0, 0))
        first_tile = pl.BlockSpec((2, 1, half, LANES), lambda index: (0, 0, 0, 0))
        last_tile = pl.BlockSpec((2, 1, half, LANES), lambda index: (0, tiles + 1, 0, 0))
        margins = pl.pallas_call(
            sides_kernel,
            out_shape=(strip, strip),
            grid=(1,),
            in_specs=[SMEM, whole, whole, first_tile, first_tile, last_tile, last_tile, HBM],
            out_specs=(whole, whole),
            compiler_params=params(8),
            cost_estimate=cost(16),
            name="sides",
        )(odd, keep(side_low), keep(side_high), margin_first, margin_second, margin_first, margin_second, parts)
        x_first, x_second = swap(*margins, "tx")

        pieces = pl.pallas_call(
            probe_kernel,
            out_shape=pltpu.HBM((members, 4, 8, LANES), F32),
            in_specs=[SMEM, VMEM, VMEM],
            out_specs=VMEM,
            compiler_params=params(6),
            cost_estimate=cost(2),
            name="probe_rows",
        )(piece, parts, keep(probe))
        probe_new = pl.pallas_call(
            join_kernel,
            out_shape=jax.ShapeDtypeStruct(probe.shape, F32),
            in_specs=[VMEM],
            out_specs=VMEM,
            compiler_params=params(6),
            cost_estimate=cost(2),
            name="join",
        )(trade(pieces, planes))

        column = pl.BlockSpec((2, side, LANES), lambda index: (0, 0, index))
        flat = pl.BlockSpec((2, 1, half, LANES), lambda index: (0, index + 1, 0, 0))
        object_new = pl.pallas_call(
            update_kernel,
            out_shape=pltpu.HBM(object_field.shape, F32),
            grid=(tiles,),
            in_specs=[
                SMEM, column, pl.BlockSpec((2, 1, side, LANES), lambda index: (0, index, 0, 0)), flat, flat,
                pl.BlockSpec((1, side, LANES), lambda index: (index, 0, 0)),
            ],
            out_specs=column,
            compiler_params=params(8),
            cost_estimate=cost(8),
            name="update",
        )(odd, keep(object_field), keep(middle), margin_first, margin_second, scale)
        object_new = pl.pallas_call(
            column_kernel,
            out_shape=pltpu.HBM(object_field.shape, F32),
            in_specs=[SMEM] + [VMEM] * 3 + [HBM],
            out_specs=HBM,
            scratch_shapes=[pltpu.VMEM((2, 2, side, LANES), F32), pltpu.SemaphoreType.DMA((4,))],
            input_output_aliases={4: 0},
            compiler_params=params(8),
            name="columns",
        )(odd, x_first, x_second, scale, object_new)
        return (object_new, probe_new)

    in_specs = (
        P(None, "ty", "tx"),
        P(),
        P("ty", "tx", None, None, None),
        P(None, "ty", "tx", None),
        P("ty", "tx"),
    )
    out_specs = (P(None, "ty", "tx"), P())
    return jax.shard_map(per_device, mesh=mesh, in_specs=in_specs, out_specs=out_specs, check_vma=False)
```

```python
import numpy as np
import ml_dtypes
import jax
import jax.numpy as jnp
from jax import lax
from jax.experimental import pallas as pl
from jax.experimental.pallas import tpu as pltpu
from jax.sharding import PartitionSpec as P

BF16 = jnp.bfloat16
F32 = jnp.float32
LANES = 128
VMEM = pl.BlockSpec(memory_space=pltpu.VMEM)
SMEM = pl.BlockSpec(memory_space=pltpu.SMEM)
HBM = pl.BlockSpec(memory_space=pltpu.HBM)
def split_host(table):
    high = table.astype(ml_dtypes.bfloat16)
    low = (table - high.astype(np.float64)).astype(ml_dtypes.bfloat16)
    return high, low


def half_tables(size):
    half = size // 2
    left, right = [], []
    for parity in range(2):
        product = (2 * np.arange(half)[:, None] + parity) * np.arange(half)[None, :] % size
        angle = 2.0 * np.pi * product / size
        cos, sin = np.cos(angle) / np.sqrt(size), np.sin(angle) / np.sqrt(size)
        base = np.block([[cos, sin], [-sin, cos]])
        for table in (base, base.T):
            high, low = split_host(table)
            left.append(np.concatenate([high, high, low], axis=1))
            right.append(np.concatenate([high, high, low], axis=0))
    return np.stack(left), np.stack(right)


def parity_tables(size):
    order = np.concatenate([np.arange(0, size, 2), np.arange(1, size, 2)])
    gather = np.eye(size)[order].astype(ml_dtypes.bfloat16)
    return np.concatenate([gather] * 3, axis=1), np.concatenate([gather.T] * 3, axis=0)


def matmul(left, right):
    return jnp.dot(left, right, preferred_element_type=F32)


def split(value):
    high = value.astype(BF16)
    return high, (value - high.astype(F32)).astype(BF16)


def put_rows(ref, start, columns, value):
    rows = value.shape[0]
    high, low = split(value)
    third = ref.shape[0] // 3
    ref[start : start + rows, columns] = high
    ref[third + start : third + start + rows, columns] = low
    ref[2 * third + start : 2 * third + start + rows, columns] = high


def put_columns(ref, rows, start, value):
    width = value.shape[1]
    high, low = split(value)
    third = ref.shape[1] // 3
    ref[rows, start : start + width] = high
    ref[rows, third + start : third + start + width] = low
    ref[rows, 2 * third + start : 2 * third + start + width] = high


def place(row, col, last):
    tile = jnp.minimum(lax.shift_right_logical(col, 7), last)
    return row, tile, col - tile * LANES


def add_window(accumulate, row, tile, offset, first, second):
    rows = first.shape[0]
    turn = jnp.bitwise_and(offset, LANES - 1)
    kept = lax.broadcasted_iota(jnp.int32, first.shape, 1) >= offset
    first = pltpu.roll(first, turn, 1)
    second = pltpu.roll(second, turn, 1)
    where = pl.ds(row, rows)
    accumulate[tile, where, :] += jnp.where(kept, first, 0.0)
    accumulate[tile + 1, where, :] += jnp.where(kept, second, first)
    accumulate[tile + 2, where, :] += jnp.where(kept, 0.0, second)


def fold_kernel(count, measured, gather_left, gather_right, folded, parts):
    size = measured.shape[1]

    def three(value):
        high = value.astype(BF16)
        rest = value - high.astype(F32)
        middle = rest.astype(BF16)
        return high, middle, (rest - middle.astype(F32)).astype(BF16)

    def step(slot, carry):
        for index, part in enumerate(three(measured[slot])):
            parts[:, index * size : (index + 1) * size] = part
        value = matmul(parts[...], gather_right[...])
        folded[slot] = matmul(gather_left[...], jnp.concatenate(three(value), axis=0))
        return carry

    lax.fori_loop(0, count[0], step, 0)


def own_notes(position, count):
    row = lax.broadcasted_iota(jnp.int32, (8, LANES), 0)
    lane = lax.broadcasted_iota(jnp.int32, (8, LANES), 1)
    notes = jnp.where(row == 2, count[0], 0)
    for slot in range(position.shape[1]):
        for axis in range(2):
            notes = jnp.where((row == axis) & (lane == slot), position[axis, slot], notes)
    return notes.astype(F32)


def edge_kernel(odd, position, count, tile_ref, x_first, x_second, y_first, y_second):
    half = LANES
    side = tile_ref.shape[1]
    odd_y, odd_x = odd[0] == 1, odd[1] == 1
    notes = own_notes(position, count)
    low, high = tile_ref[:, :, :half], tile_ref[:, :, side - half :]
    x_first[:, :side, :] = jnp.where(odd_x, high, low)
    x_second[:, :side, :] = jnp.where(odd_x, low, high)
    for out in (x_first, x_second):
        for plane in range(2):
            out[plane, side:, :] = notes
    low, high = tile_ref[:, :half, :], tile_ref[:, side - half :, :]
    y_first[...] = jnp.where(odd_y, high, low)
    y_second[...] = jnp.where(odd_y, low, high)


def corner_kernel(odd, position, count, x_first, x_second, after, first, second):
    half = LANES
    side = x_first.shape[1] - 8
    far = side - half
    odd_x = odd[1] == 1
    notes = own_notes(position, count)
    for out, odd_start in ((first, far), (second, 0)):
        rows = pl.ds(pl.multiple_of(jnp.where(odd[0] == 1, odd_start, far - odd_start), LANES), half)
        for index, (even_ref, odd_ref) in enumerate(((x_first, x_second), (x_second, x_first))):
            out[:, index, :half, :] = jnp.where(odd_x, odd_ref[:, rows, :], even_ref[:, rows, :])
            out[:, index, half : half + 8, :] = jnp.where(odd_x, odd_ref[:, side:, :], even_ref[:, side:, :])
            for plane in range(2):
                out[plane, index, half + 8 :, :] = notes


def slot_stages(row, tile, offset, live, probe, measured, left, right, canvas, grad, probe_sum, patch, rhs, lhs):
    size = probe.shape[1]
    half = size // 2
    near, far = slice(0, half), slice(half, size)
    turn = jnp.bitwise_and(LANES - offset, LANES - 1)
    kept = lax.broadcasted_iota(jnp.int32, (size, LANES), 1) < LANES - offset
    for plane in range(2):
        raw = [pltpu.roll(canvas[plane, tile + index, pl.ds(row, size), :], turn, 1) for index in range(3)]
        patch[plane, 0] = jnp.where(kept, raw[0], raw[1])
        patch[plane, 1] = jnp.where(kept, raw[1], raw[2])
    for index, columns in enumerate((near, far)):
        probe_re, probe_im = probe[0, :, columns], probe[1, :, columns]
        patch_re, patch_im = patch[0, index], patch[1, index]
        exit_re = probe_re * patch_re - probe_im * patch_im
        exit_im = probe_re * patch_im + probe_im * patch_re
        probe_sum[2, index] += (patch_re * patch_re + patch_im * patch_im) * live
        put_rows(rhs.at[0], 0, columns, exit_re[:half] + exit_re[half:])
        put_rows(rhs.at[0], half, columns, exit_im[:half] + exit_im[half:])
        put_rows(rhs.at[1], 0, columns, exit_re[:half] - exit_re[half:])
        put_rows(rhs.at[1], half, columns, exit_im[:half] - exit_im[half:])
    yield
    for parity in range(2):
        value = matmul(left[2 * parity], rhs[parity])
        rows = slice(parity * half, (parity + 1) * half)
        put_columns(lhs.at[0], rows, 0, value[:half, near] + value[:half, far])
        put_columns(lhs.at[0], rows, half, value[half:, near] + value[half:, far])
        put_columns(lhs.at[1], rows, 0, value[:half, near] - value[:half, far])
        put_columns(lhs.at[1], rows, half, value[half:, near] - value[half:, far])
        yield
    everything = slice(0, size)
    for parity in range(2):
        value = matmul(lhs[parity], right[2 * parity + 1])
        wave_re, wave_im = value[:, near], value[:, far]
        columns = slice(parity * half, (parity + 1) * half)
        excess = (wave_re * wave_re + wave_im * wave_im - measured[:, columns]) * live
        put_columns(lhs.at[parity], everything, 0, excess * wave_re)
        put_columns(lhs.at[parity], everything, half, excess * wave_im)
        yield
    back = []
    for parity in range(2):
        back.append(matmul(lhs[parity], right[2 * parity]))
    for parity in range(2):
        rows = slice(parity * half, (parity + 1) * half)
        put_rows(rhs.at[parity], 0, near, back[0][rows, near] + back[1][rows, near])
        put_rows(rhs.at[parity], half, near, back[0][rows, far] + back[1][rows, far])
        put_rows(rhs.at[parity], 0, far, back[0][rows, near] - back[1][rows, near])
        put_rows(rhs.at[parity], half, far, back[0][rows, far] - back[1][rows, far])
    yield
    even = matmul(left[1], rhs[0])
    odd = matmul(left[3], rhs[1])
    pieces = []
    for index, columns in enumerate((near, far)):
        chi_re, chi_im = (
            jnp.concatenate([even[rows, columns] + odd[rows, columns], even[rows, columns] - odd[rows, columns]], axis=0)
            for rows in (near, far)
        )
        probe_re, probe_im = probe[0, :, columns], probe[1, :, columns]
        patch_re, patch_im = patch[0, index], patch[1, index]
        probe_sum[0, index] += patch_re * chi_re + patch_im * chi_im
        probe_sum[1, index] += patch_re * chi_im - patch_im * chi_re
        pieces.append((probe_re * chi_re + probe_im * chi_im, probe_re * chi_im - probe_im * chi_re))
    for plane in range(2):
        add_window(grad.at[plane], row, tile, offset, pieces[0][plane], pieces[1][plane])
    yield


def run_slots(wanted, position, count, probe, folded, left, right, canvas, grad, probe_sum, order, patch, rhs, lhs):
    size = probe.shape[1]
    half = size // 2
    tiles = canvas.shape[1] - 2
    reach = tiles * LANES - size

    def pick(slot, found):
        row, col = position[0, slot], position[1, slot]
        take = wanted((row >= 0) & (row <= reach), (col >= 0) & (col <= reach))

        @pl.when(take)
        def keep():
            order[found] = slot

        return found + jnp.where(take, 1, 0)

    total = lax.fori_loop(0, count[0], pick, 0)
    lanes = patch.shape[0]

    def step(group, carry):
        stages = []
        for lane in range(lanes):
            index = lanes * group + lane
            live = jnp.where(index < total, 1.0, 0.0)
            slot = order[jnp.minimum(index, total - 1)]
            row, tile, offset = place(position[0, slot] + half, position[1, slot] + half, tiles - 1)
            stages.append(slot_stages(
                row, tile, offset, live, probe, folded.at[slot], left, right, canvas, grad, probe_sum,
                patch.at[lane], rhs.at[lane], lhs.at[lane],
            ))
        for _ in zip(*stages):
            pass
        return carry

    lax.fori_loop(0, lax.div(total + (lanes - 1), lanes), step, 0)


def core_kernel(odd, position, count, probe, folded, left, right, tile_ref, canvas, grad, probe_sum, token, *scratch):
    side = tile_ref.shape[1]
    half = LANES
    tiles = side // LANES
    canvas[...] = jnp.zeros_like(canvas)
    for index in range(tiles):
        canvas[:, 1 + index, half : half + side, :] = tile_ref[:, :, index * LANES : (index + 1) * LANES]
    grad[...] = jnp.zeros_like(grad)
    probe_sum[...] = jnp.zeros_like(probe_sum)
    token[...] = jnp.zeros_like(token)
    run_slots(lambda row, col: row & col, position, count, probe, folded, left, right, canvas, grad, probe_sum, *scratch)


def column_slots_kernel(
    odd, position, count, probe, folded, left, right, x_first, x_second, canvas_in, grad_in, sum_in,
    canvas, grad, probe_sum, *scratch,
):
    side = x_first.shape[1] - 8
    half = LANES
    last = canvas.shape[1] - 1
    inner = slice(half, half + side)
    odd_x = odd[1] == 1
    canvas[:, 0, inner, :] = jnp.where(odd_x, x_second[:, :side, :], x_first[:, :side, :])
    canvas[:, last, inner, :] = jnp.where(odd_x, x_first[:, :side, :], x_second[:, :side, :])
    run_slots(
        lambda row, col: row & jnp.logical_not(col),
        position, count, probe, folded, left, right, canvas, grad, probe_sum, *scratch,
    )


def row_kernel(
    odd, position, count, probe, folded, left, right, y_first, y_second, canvas_in, grad_in, sum_in,
    canvas, grad, probe_sum, *scratch,
):
    half = LANES
    side = y_first.shape[2]
    odd_y = odd[0] == 1
    for index in range(side // LANES):
        columns = slice(index * LANES, (index + 1) * LANES)
        canvas[:, 1 + index, :half, :] = jnp.where(odd_y, y_second[:, :, columns], y_first[:, :, columns])
        canvas[:, 1 + index, half + side :, :] = jnp.where(odd_y, y_first[:, :, columns], y_second[:, :, columns])
    run_slots(
        lambda row, col: jnp.logical_not(row) & col,
        position, count, probe, folded, left, right, canvas, grad, probe_sum, *scratch,
    )


def outer_kernel(
    odd, position, count, probe, folded, left, right, x_first, x_second, corner_first, corner_second,
    canvas_in, grad_in, sum_in,
    margin_first, margin_second, side_low, side_high, middle, sums, places, canvas, grad, probe_sum, sems, *scratch,
):
    size = probe.shape[1]
    half = size // 2
    side = x_first.shape[1] - 8
    tiles = side // LANES
    inner = slice(half, half + side)
    odd_y, odd_x = odd[0] == 1, odd[1] == 1
    for index, tile in enumerate((0, 1 + tiles)):
        above, below = corner_first[:, index, :half, :], corner_second[:, index, :half, :]
        canvas[:, tile, :half, :] = jnp.where(odd_y, below, above)
        canvas[:, tile, half + side :, :] = jnp.where(odd_y, above, below)
    run_slots(
        lambda row, col: jnp.logical_not(row | col),
        position, count, probe, folded, left, right, canvas, grad, probe_sum, *scratch,
    )
    copies = []

    def send(source, target):
        copy = pltpu.make_async_copy(source, target, sems.at[len(copies)])
        copy.start()
        copies.append(copy)

    for out, odd_start in ((margin_first, half + side), (margin_second, 0)):
        rows = pl.ds(pl.multiple_of(jnp.where(odd_y, odd_start, half + side - odd_start), LANES), half)
        send(grad.at[:, :, rows, :], out)
    send(grad.at[:, 0, inner, :], side_low)
    send(grad.at[:, 1 + tiles, inner, :], side_high)
    send(grad.at[:, 1 : 1 + tiles, inner, :], middle)
    for plane in range(3):
        for index in range(2):
            sums[:, 2 * plane + index] = probe_sum[plane, index].reshape(size // 8, 8, LANES)
    beside, own = slice(half, half + 8), slice(half + 8, half + 16)
    for start, (even_ref, odd_ref) in ((0, (corner_first, corner_second)), (6, (corner_second, corner_first))):
        for index, (tile, rows) in enumerate(((0, beside), (0, own), (1, beside))):
            places[start + index] = jnp.where(odd_y, odd_ref[0, tile, rows, :], even_ref[0, tile, rows, :])
    places[3] = jnp.where(odd_x, x_second[0, side:, :], x_first[0, side:, :])
    places[4] = own_notes(position, count)
    places[5] = jnp.where(odd_x, x_first[0, side:, :], x_second[0, side:, :])
    for copy in copies:
        copy.wait()


def sides_kernel(odd, own_low, own_high, low_first, low_second, high_first, high_second, first, second):
    half = LANES
    side = own_low.shape[1]
    odd_y, odd_x = odd[0] == 1, odd[1] == 1
    for start in range(0, side, half):
        rows = slice(start, start + half)
        values = []
        for own, y_first, y_second in ((own_low, low_first, low_second), (own_high, high_first, high_second)):
            value = own[:, rows, :]
            if start == 0:
                value = value + jnp.where(odd_y, y_second[:, 0], y_first[:, 0])
            if start + half == side:
                value = value + jnp.where(odd_y, y_first[:, 0], y_second[:, 0])
            values.append(value)
        first[:, rows, :] = jnp.where(odd_x, values[1], values[0])
        second[:, rows, :] = jnp.where(odd_x, values[0], values[1])


def weight_kernel(numbers, probe, scale, power, weight):
    half = LANES
    side = scale.shape[1]
    tiles = side // LANES
    weight[...] = jnp.zeros_like(weight)
    for index in range(2):
        columns = slice(index * LANES, (index + 1) * LANES)
        power[index] = probe[0, :, columns] * probe[0, :, columns] + probe[1, :, columns] * probe[1, :, columns]
    for index in range(9):
        down, across = index // 3 - 1, index % 3 - 1

        def step(slot, carry):
            row = numbers[index, 0, slot].astype(jnp.int32) + (2 * half + down * side)
            col = numbers[index, 1, slot].astype(jnp.int32) + (2 * half + across * side)
            reach = side + 2 * half

            @pl.when((row > 0) & (row < reach) & (col > 0) & (col < reach))
            def add():
                at, tile, offset = place(row, col, tiles + 1)
                add_window(weight, at, tile, offset, power[0], power[1])

            return carry

        lax.fori_loop(0, numbers[index, 2, 0].astype(jnp.int32), step, 0)
    for index in range(tiles):
        scale[index] = 1.0 / (weight[2 + index, 2 * half : 2 * half + side, :] + 1.0)


def update_kernel(odd, tile_ref, grad, y_first, y_second, scale, out):
    half = LANES
    side = tile_ref.shape[1]
    odd_y = odd[0] == 1
    for plane in range(2):
        for start in range(0, side, half):
            rows = slice(start, start + half)
            value = grad[plane, 0, rows, :]
            if start == 0:
                value = value + jnp.where(odd_y, y_second[plane, 0], y_first[plane, 0])
            if start + half == side:
                value = value + jnp.where(odd_y, y_first[plane, 0], y_second[plane, 0])
            out[plane, rows, :] = tile_ref[plane, rows, :] - value * scale[0, rows, :]


def column_kernel(odd, before, x_first, x_second, scale, out):
    use_first = odd[1] == pl.program_id(0)
    for plane in range(2):
        out[plane] = before[plane] - jnp.where(use_first, x_first[plane], x_second[plane]) * scale[0]


def plane_kernel(parts, after, out):
    out[...] = jnp.broadcast_to(jnp.sum(parts[...], axis=0)[None], out.shape)


def probe_kernel(index, parts, probe, out):
    total = jnp.sum(parts[...], axis=0)
    rows = pl.ds(pl.multiple_of(index[0] * 8, 8), 8)
    for tile in range(2):
        root = jnp.sqrt(total[4 + tile] + 1.0)
        for plane in range(2):
            new = probe[plane, rows, tile * LANES : (tile + 1) * LANES] - total[2 * plane + tile] / root
            out[:, 2 * plane + tile] = jnp.broadcast_to(new[None], (out.shape[0], 8, LANES))


def join_kernel(pieces, out):
    for plane in range(2):
        for tile in range(2):
            value = pieces[:, 2 * plane + tile]
            out[plane, :, tile * LANES : (tile + 1) * LANES] = value.reshape(out.shape[1], LANES)


def swap(first, second, axis):
    count = lax.axis_size(axis)
    across = [pair for low in range(1, count - 1, 2) for pair in ((low, low + 1), (low + 1, low))]
    return lax.ppermute(first, axis, across), lax.ppermute(second, axis, [(index, index ^ 1) for index in range(count)])


def keep(value):
    return pltpu.with_memory_space_constraint(value, pltpu.HBM)


def params(mib):
    return pltpu.CompilerParams(vmem_limit_bytes=mib * 2**20)


def cost(mib):
    return pl.CostEstimate(flops=0, bytes_accessed=mib * 2**20, transcendentals=0)


def solution(mesh):
    rows, cols = mesh.shape["ty"], mesh.shape["tx"]
    near_y, near_z = 8, 4
    planes = [
        [(8 * high + row) * cols + near_z * x + low for row in range(near_y) for x in range(cols // near_z)]
        for high in range(rows // near_y)
        for low in range(near_z)
    ]
    lines = [list(line) for line in zip(*planes)]

    def trade(pieces, groups):
        return lax.all_to_all(pieces, ("ty", "tx"), 0, 0, axis_index_groups=groups, tiled=True)

    def per_device(object_field, probe, intensity, positions, counts):
        side = object_field.shape[1]
        size = probe.shape[1]
        half = size // 2
        slots = intensity.shape[2]
        tiles = side // LANES
        position = positions[:, 0, 0, :]
        count = counts[0]
        row, col = lax.axis_index("ty"), lax.axis_index("tx")
        piece = jnp.bitwise_and(row, near_y - 1) * (cols // near_z) + lax.shift_right_logical(col, 2)
        piece = piece.reshape(1).astype(jnp.int32)
        left, right = (jnp.asarray(table) for table in half_tables(size))
        gather_left, gather_right = (jnp.asarray(table) for table in parity_tables(size))

        odd = jnp.bitwise_and(jnp.stack([row, col]), 1).astype(jnp.int32)

        strip = jax.ShapeDtypeStruct((2, side + 8, LANES), F32)
        edge = jax.ShapeDtypeStruct((2, half, side), F32)
        x_first, x_second, y_first, y_second = pl.pallas_call(
            edge_kernel,
            out_shape=(strip, strip, edge, edge),
            in_specs=[SMEM] * 3 + [VMEM],
            out_specs=(VMEM,) * 4,
            compiler_params=params(6),
            cost_estimate=cost(4),
            name="edges",
        )(odd, position, count, object_field)
        x_first, x_second = swap(x_first, x_second, "tx")
        y_first, y_second = swap(y_first, y_second, "ty")
        folded = pl.pallas_call(
            fold_kernel,
            out_shape=jax.ShapeDtypeStruct((slots, size, size), F32),
            in_specs=[SMEM, VMEM, VMEM, VMEM],
            out_specs=VMEM,
            scratch_shapes=[pltpu.VMEM((size, 3 * size), BF16)],
            compiler_params=params(8),
            cost_estimate=cost(6),
            name="fold",
        )(count, intensity[0, 0], gather_left, gather_right)
        members = len(planes[0])
        lanes = 2
        scratch = [
            pltpu.SMEM((slots,), jnp.int32),
            pltpu.VMEM((lanes, 2, 2, size, LANES), F32),
            pltpu.VMEM((lanes, 2, 3 * size, size), BF16),
            pltpu.VMEM((lanes, 2, size, 3 * size), BF16),
        ]
        state = (
            pltpu.VMEM((2, tiles + 2, side + size, LANES), F32),
            pltpu.VMEM((2, tiles + 2, side + size, LANES), F32),
            pltpu.VMEM((3, 2, size, LANES), F32),
        )
        given = (odd, position, count, probe, folded, left, right)
        canvas, grad, probe_sum, token = pl.pallas_call(
            core_kernel,
            out_shape=state + (jax.ShapeDtypeStruct((8, LANES), F32),),
            in_specs=[SMEM] * 3 + [VMEM] * 5,
            out_specs=(VMEM,) * 4,
            scratch_shapes=scratch,
            compiler_params=params(26),
            cost_estimate=cost(16),
            name="core_slots",
        )(*given, object_field)
        corner = jax.ShapeDtypeStruct((2, 2, half + 16, LANES), F32)
        corners = pl.pallas_call(
            corner_kernel,
            out_shape=(corner, corner),
            in_specs=[SMEM] * 3 + [VMEM] * 2 + [HBM],
            out_specs=(VMEM, VMEM),
            compiler_params=params(4),
            cost_estimate=cost(4),
            name="corners",
        )(odd, position, count, x_first, x_second, token)
        corners = swap(*corners, "ty")

        canvas, grad, probe_sum = pl.pallas_call(
            column_slots_kernel,
            out_shape=state,
            in_specs=[SMEM] * 3 + [VMEM] * 9,
            out_specs=(VMEM,) * 3,
            scratch_shapes=scratch,
            input_output_aliases={9: 0, 10: 1, 11: 2},
            compiler_params=params(26),
            cost_estimate=cost(16),
            name="column_slots",
        )(*given, x_first, x_second, canvas, grad, probe_sum)
        canvas, grad, probe_sum = pl.pallas_call(
            row_kernel,
            out_shape=state,
            in_specs=[SMEM] * 3 + [VMEM] * 9,
            out_specs=(VMEM,) * 3,
            scratch_shapes=scratch,
            input_output_aliases={9: 0, 10: 1, 11: 2},
            compiler_params=params(26),
            cost_estimate=cost(8),
            name="row_slots",
        )(*given, y_first, y_second, canvas, grad, probe_sum)
        margin = pltpu.HBM((2, tiles + 2, half, LANES), F32)
        column = pltpu.HBM((2, side, LANES), F32)
        margin_first, margin_second, side_low, side_high, middle, sums, places, *_ = pl.pallas_call(
            outer_kernel,
            out_shape=(
                margin, margin, column, column,
                pltpu.HBM((2, tiles, side, LANES), F32),
                pltpu.HBM((members, 6, 8, LANES), F32),
                jax.ShapeDtypeStruct((9, 8, LANES), F32),
            ) + state,
            in_specs=[SMEM] * 3 + [VMEM] * 11,
            out_specs=(HBM,) * 5 + (VMEM,) * 5,
            scratch_shapes=[pltpu.SemaphoreType.DMA((5,))] + scratch,
            input_output_aliases={11: 7, 12: 8, 13: 9},
            compiler_params=params(26),
            cost_estimate=cost(16),
            name="outer_slots",
        )(*given, x_first, x_second, *corners, canvas, grad, probe_sum)

        margin_first, margin_second = swap(margin_first, margin_second, "ty")
        scale = pl.pallas_call(
            weight_kernel,
            out_shape=jax.ShapeDtypeStruct((tiles, side, LANES), F32),
            in_specs=[SMEM, VMEM],
            out_specs=VMEM,
            scratch_shapes=[
                pltpu.VMEM((2, size, LANES), F32),
                pltpu.VMEM((tiles + 4, side + 2 * size, LANES), F32),
            ],
            compiler_params=params(8),
            cost_estimate=cost(8),
            name="weights",
        )(places, keep(probe))
        parts = trade(sums, planes)
        strip = pltpu.HBM((2, side, LANES), F32)
        whole = pl.BlockSpec((2, side, LANES), lambda index: (0, 0, 0))
        first_tile = pl.BlockSpec((2, 1, half, LANES), lambda index: (0, 0, 0, 0))
        last_tile = pl.BlockSpec((2, 1, half, LANES), lambda index: (0, tiles + 1, 0, 0))
        margins = pl.pallas_call(
            sides_kernel,
            out_shape=(strip, strip),
            grid=(1,),
            in_specs=[SMEM, whole, whole, first_tile, first_tile, last_tile, last_tile],
            out_specs=(whole, whole),
            compiler_params=params(8),
            cost_estimate=cost(16),
            name="sides",
        )(odd, keep(side_low), keep(side_high), margin_first, margin_second, margin_first, margin_second)
        x_first, x_second = swap(*margins, "tx")

        parts = pl.pallas_call(
            plane_kernel,
            out_shape=pltpu.HBM((len(lines[0]), 6, 8, LANES), F32),
            in_specs=[VMEM, HBM],
            out_specs=VMEM,
            compiler_params=params(6),
            cost_estimate=cost(2),
            name="plane_sum",
        )(parts, scale)
        parts = trade(parts, lines)
        pieces = pl.pallas_call(
            probe_kernel,
            out_shape=pltpu.HBM((members, 4, 8, LANES), F32),
            in_specs=[SMEM, VMEM, VMEM],
            out_specs=VMEM,
            compiler_params=params(6),
            cost_estimate=cost(2),
            name="probe_rows",
        )(piece, parts, keep(probe))
        probe_new = pl.pallas_call(
            join_kernel,
            out_shape=jax.ShapeDtypeStruct(probe.shape, F32),
            in_specs=[VMEM],
            out_specs=VMEM,
            compiler_params=params(6),
            cost_estimate=cost(2),
            name="join",
        )(trade(pieces, planes))

        column = pl.BlockSpec((2, side, LANES), lambda index: (0, 0, index))
        flat = pl.BlockSpec((2, 1, half, LANES), lambda index: (0, index + 1, 0, 0))
        object_new = pl.pallas_call(
            update_kernel,
            out_shape=jax.ShapeDtypeStruct(object_field.shape, F32),
            grid=(tiles,),
            in_specs=[
                SMEM, column, pl.BlockSpec((2, 1, side, LANES), lambda index: (0, index, 0, 0)), flat, flat,
                pl.BlockSpec((1, side, LANES), lambda index: (index, 0, 0)),
            ],
            out_specs=column,
            compiler_params=params(8),
            cost_estimate=cost(8),
            name="update",
        )(odd, keep(object_field), keep(middle), margin_first, margin_second, scale)
        ends = pl.BlockSpec((2, side, LANES), lambda index: (0, 0, index * (tiles - 1)))
        object_new = pl.pallas_call(
            column_kernel,
            out_shape=jax.ShapeDtypeStruct(object_field.shape, F32),
            grid=(2,),
            in_specs=[SMEM, ends, whole, whole, pl.BlockSpec((1, side, LANES), lambda index: (index * (tiles - 1), 0, 0))],
            out_specs=ends,
            input_output_aliases={1: 0},
            compiler_params=params(8),
            name="columns",
        )(odd, object_new, x_first, x_second, scale)
        return (object_new, probe_new)

    in_specs = (
        P(None, "ty", "tx"),
        P(),
        P("ty", "tx", None, None, None),
        P(None, "ty", "tx", None),
        P("ty", "tx"),
    )
    out_specs = (P(None, "ty", "tx"), P())
    return jax.shard_map(per_device, mesh=mesh, in_specs=in_specs, out_specs=out_specs, check_vma=False)
```

```python
import numpy as np
import ml_dtypes
import jax
import jax.numpy as jnp
from jax import lax
from jax.experimental import pallas as pl
from jax.experimental.pallas import tpu as pltpu
from jax.sharding import PartitionSpec as P

BF16 = jnp.bfloat16
F32 = jnp.float32
LANES = 128
VMEM = pl.BlockSpec(memory_space=pltpu.VMEM)
SMEM = pl.BlockSpec(memory_space=pltpu.SMEM)
HBM = pl.BlockSpec(memory_space=pltpu.HBM)
def split_host(table):
    high = table.astype(ml_dtypes.bfloat16)
    low = (table - high.astype(np.float64)).astype(ml_dtypes.bfloat16)
    return high, low


def half_tables(size):
    half = size // 2
    left, right = [], []
    for parity in range(2):
        product = (2 * np.arange(half)[:, None] + parity) * np.arange(half)[None, :] % size
        angle = 2.0 * np.pi * product / size
        cos, sin = np.cos(angle) / np.sqrt(size), np.sin(angle) / np.sqrt(size)
        base = np.block([[cos, sin], [-sin, cos]])
        for table in (base, base.T):
            high, low = split_host(table)
            left.append(np.concatenate([high, high, low], axis=1))
            right.append(np.concatenate([high, high, low], axis=0))
    return np.stack(left), np.stack(right)


def parity_tables(size):
    order = np.concatenate([np.arange(0, size, 2), np.arange(1, size, 2)])
    gather = np.eye(size)[order].astype(ml_dtypes.bfloat16)
    return np.concatenate([gather] * 3, axis=1), np.concatenate([gather.T] * 3, axis=0)


def matmul(left, right):
    return jnp.dot(left, right, preferred_element_type=F32)


def split(value):
    high = value.astype(BF16)
    return high, (value - high.astype(F32)).astype(BF16)


def put_rows(ref, start, columns, value):
    rows = value.shape[0]
    high, low = split(value)
    third = ref.shape[0] // 3
    ref[start : start + rows, columns] = high
    ref[third + start : third + start + rows, columns] = low
    ref[2 * third + start : 2 * third + start + rows, columns] = high


def put_columns(ref, rows, start, value):
    width = value.shape[1]
    high, low = split(value)
    third = ref.shape[1] // 3
    ref[rows, start : start + width] = high
    ref[rows, third + start : third + start + width] = low
    ref[rows, 2 * third + start : 2 * third + start + width] = high


def place(row, col, last):
    tile = jnp.minimum(lax.shift_right_logical(col, 7), last)
    return row, tile, col - tile * LANES


def add_window(accumulate, row, tile, offset, first, second):
    rows = first.shape[0]
    turn = jnp.bitwise_and(offset, LANES - 1)
    kept = lax.broadcasted_iota(jnp.int32, first.shape, 1) >= offset
    first = pltpu.roll(first, turn, 1)
    second = pltpu.roll(second, turn, 1)
    where = pl.ds(row, rows)
    accumulate[tile, where, :] += jnp.where(kept, first, 0.0)
    accumulate[tile + 1, where, :] += jnp.where(kept, second, first)
    accumulate[tile + 2, where, :] += jnp.where(kept, 0.0, second)


def fold_kernel(count, measured, gather_left, gather_right, folded, parts):
    size = measured.shape[1]

    def three(value):
        high = value.astype(BF16)
        rest = value - high.astype(F32)
        middle = rest.astype(BF16)
        return high, middle, (rest - middle.astype(F32)).astype(BF16)

    def step(slot, carry):
        for index, part in enumerate(three(measured[slot])):
            parts[:, index * size : (index + 1) * size] = part
        value = matmul(parts[...], gather_right[...])
        folded[slot] = matmul(gather_left[...], jnp.concatenate(three(value), axis=0))
        return carry

    lax.fori_loop(0, count[0], step, 0)


def own_notes(position, count):
    row = lax.broadcasted_iota(jnp.int32, (8, LANES), 0)
    lane = lax.broadcasted_iota(jnp.int32, (8, LANES), 1)
    notes = jnp.where(row == 2, count[0], 0)
    for slot in range(position.shape[1]):
        for axis in range(2):
            notes = jnp.where((row == axis) & (lane == slot), position[axis, slot], notes)
    return notes.astype(F32)


def edge_kernel(odd, position, count, tile_ref, x_first, x_second, y_first, y_second):
    half = LANES
    side = tile_ref.shape[1]
    odd_y, odd_x = odd[0] == 1, odd[1] == 1
    notes = own_notes(position, count)
    low, high = tile_ref[:, :, :half], tile_ref[:, :, side - half :]
    x_first[:, :side, :] = jnp.where(odd_x, high, low)
    x_second[:, :side, :] = jnp.where(odd_x, low, high)
    for out in (x_first, x_second):
        for plane in range(2):
            out[plane, side:, :] = notes
    low, high = tile_ref[:, :half, :], tile_ref[:, side - half :, :]
    y_first[...] = jnp.where(odd_y, high, low)
    y_second[...] = jnp.where(odd_y, low, high)


def corner_kernel(odd, position, count, x_first, x_second, after, first, second):
    half = LANES
    side = x_first.shape[1] - 8
    far = side - half
    odd_x = odd[1] == 1
    notes = own_notes(position, count)
    for out, odd_start in ((first, far), (second, 0)):
        rows = pl.ds(pl.multiple_of(jnp.where(odd[0] == 1, odd_start, far - odd_start), LANES), half)
        for index, (even_ref, odd_ref) in enumerate(((x_first, x_second), (x_second, x_first))):
            out[:, index, :half, :] = jnp.where(odd_x, odd_ref[:, rows, :], even_ref[:, rows, :])
            out[:, index, half : half + 8, :] = jnp.where(odd_x, odd_ref[:, side:, :], even_ref[:, side:, :])
            for plane in range(2):
                out[plane, index, half + 8 :, :] = notes


def slot_stages(row, tile, offset, live, probe, measured, left, right, canvas, grad, probe_sum, patch, rhs, lhs):
    size = probe.shape[1]
    half = size // 2
    near, far = slice(0, half), slice(half, size)
    turn = jnp.bitwise_and(LANES - offset, LANES - 1)
    kept = lax.broadcasted_iota(jnp.int32, (size, LANES), 1) < LANES - offset
    for plane in range(2):
        raw = [pltpu.roll(canvas[plane, tile + index, pl.ds(row, size), :], turn, 1) for index in range(3)]
        patch[plane, 0] = jnp.where(kept, raw[0], raw[1])
        patch[plane, 1] = jnp.where(kept, raw[1], raw[2])
    for index, columns in enumerate((near, far)):
        probe_re, probe_im = probe[0, :, columns], probe[1, :, columns]
        patch_re, patch_im = patch[0, index], patch[1, index]
        exit_re = probe_re * patch_re - probe_im * patch_im
        exit_im = probe_re * patch_im + probe_im * patch_re
        probe_sum[2, index] += (patch_re * patch_re + patch_im * patch_im) * live
        put_rows(rhs.at[0], 0, columns, exit_re[:half] + exit_re[half:])
        put_rows(rhs.at[0], half, columns, exit_im[:half] + exit_im[half:])
        put_rows(rhs.at[1], 0, columns, exit_re[:half] - exit_re[half:])
        put_rows(rhs.at[1], half, columns, exit_im[:half] - exit_im[half:])
    yield
    for parity in range(2):
        value = matmul(left[2 * parity], rhs[parity])
        rows = slice(parity * half, (parity + 1) * half)
        put_columns(lhs.at[0], rows, 0, value[:half, near] + value[:half, far])
        put_columns(lhs.at[0], rows, half, value[half:, near] + value[half:, far])
        put_columns(lhs.at[1], rows, 0, value[:half, near] - value[:half, far])
        put_columns(lhs.at[1], rows, half, value[half:, near] - value[half:, far])
        yield
    everything = slice(0, size)
    for parity in range(2):
        value = matmul(lhs[parity], right[2 * parity + 1])
        wave_re, wave_im = value[:, near], value[:, far]
        columns = slice(parity * half, (parity + 1) * half)
        excess = (wave_re * wave_re + wave_im * wave_im - measured[:, columns]) * live
        put_columns(lhs.at[parity], everything, 0, excess * wave_re)
        put_columns(lhs.at[parity], everything, half, excess * wave_im)
        yield
    back = []
    for parity in range(2):
        back.append(matmul(lhs[parity], right[2 * parity]))
    for parity in range(2):
        rows = slice(parity * half, (parity + 1) * half)
        put_rows(rhs.at[parity], 0, near, back[0][rows, near] + back[1][rows, near])
        put_rows(rhs.at[parity], half, near, back[0][rows, far] + back[1][rows, far])
        put_rows(rhs.at[parity], 0, far, back[0][rows, near] - back[1][rows, near])
        put_rows(rhs.at[parity], half, far, back[0][rows, far] - back[1][rows, far])
    yield
    even = matmul(left[1], rhs[0])
    odd = matmul(left[3], rhs[1])
    pieces = []
    for index, columns in enumerate((near, far)):
        chi_re, chi_im = (
            jnp.concatenate([even[rows, columns] + odd[rows, columns], even[rows, columns] - odd[rows, columns]], axis=0)
            for rows in (near, far)
        )
        probe_re, probe_im = probe[0, :, columns], probe[1, :, columns]
        patch_re, patch_im = patch[0, index], patch[1, index]
        probe_sum[0, index] += patch_re * chi_re + patch_im * chi_im
        probe_sum[1, index] += patch_re * chi_im - patch_im * chi_re
        pieces.append((probe_re * chi_re + probe_im * chi_im, probe_re * chi_im - probe_im * chi_re))
    for plane in range(2):
        add_window(grad.at[plane], row, tile, offset, pieces[0][plane], pieces[1][plane])
    yield


def run_slots(wanted, position, count, probe, folded, left, right, canvas, grad, probe_sum, order, patch, rhs, lhs):
    size = probe.shape[1]
    half = size // 2
    tiles = canvas.shape[1] - 2
    reach = tiles * LANES - size

    def pick(slot, found):
        row, col = position[0, slot], position[1, slot]
        take = wanted((row >= 0) & (row <= reach), (col >= 0) & (col <= reach))

        @pl.when(take)
        def keep():
            order[found] = slot

        return found + jnp.where(take, 1, 0)

    total = lax.fori_loop(0, count[0], pick, 0)
    lanes = patch.shape[0]

    def step(group, carry):
        stages = []
        for lane in range(lanes):
            index = lanes * group + lane
            live = jnp.where(index < total, 1.0, 0.0)
            slot = order[jnp.minimum(index, total - 1)]
            row, tile, offset = place(position[0, slot] + half, position[1, slot] + half, tiles - 1)
            stages.append(slot_stages(
                row, tile, offset, live, probe, folded.at[slot], left, right, canvas, grad, probe_sum,
                patch.at[lane], rhs.at[lane], lhs.at[lane],
            ))
        for _ in zip(*stages):
            pass
        return carry

    lax.fori_loop(0, lax.div(total + (lanes - 1), lanes), step, 0)


def core_kernel(odd, position, count, probe, folded, left, right, tile_ref, canvas, grad, probe_sum, token, *scratch):
    side = tile_ref.shape[1]
    half = LANES
    tiles = side // LANES
    canvas[...] = jnp.zeros_like(canvas)
    for index in range(tiles):
        canvas[:, 1 + index, half : half + side, :] = tile_ref[:, :, index * LANES : (index + 1) * LANES]
    grad[...] = jnp.zeros_like(grad)
    probe_sum[...] = jnp.zeros_like(probe_sum)
    token[...] = jnp.zeros_like(token)
    run_slots(lambda row, col: row & col, position, count, probe, folded, left, right, canvas, grad, probe_sum, *scratch)


def column_slots_kernel(
    odd, position, count, probe, folded, left, right, x_first, x_second, canvas_in, grad_in, sum_in,
    canvas, grad, probe_sum, *scratch,
):
    side = x_first.shape[1] - 8
    half = LANES
    last = canvas.shape[1] - 1
    inner = slice(half, half + side)
    odd_x = odd[1] == 1
    canvas[:, 0, inner, :] = jnp.where(odd_x, x_second[:, :side, :], x_first[:, :side, :])
    canvas[:, last, inner, :] = jnp.where(odd_x, x_first[:, :side, :], x_second[:, :side, :])
    run_slots(
        lambda row, col: row & jnp.logical_not(col),
        position, count, probe, folded, left, right, canvas, grad, probe_sum, *scratch,
    )


def row_kernel(
    odd, position, count, probe, folded, left, right, y_first, y_second, canvas_in, grad_in, sum_in,
    canvas, grad, probe_sum, *scratch,
):
    half = LANES
    side = y_first.shape[2]
    odd_y = odd[0] == 1
    for index in range(side // LANES):
        columns = slice(index * LANES, (index + 1) * LANES)
        canvas[:, 1 + index, :half, :] = jnp.where(odd_y, y_second[:, :, columns], y_first[:, :, columns])
        canvas[:, 1 + index, half + side :, :] = jnp.where(odd_y, y_first[:, :, columns], y_second[:, :, columns])
    run_slots(
        lambda row, col: jnp.logical_not(row) & col,
        position, count, probe, folded, left, right, canvas, grad, probe_sum, *scratch,
    )


def outer_kernel(
    odd, position, count, probe, folded, left, right, x_first, x_second, corner_first, corner_second,
    canvas_in, grad_in, sum_in,
    margin_first, margin_second, side_low, side_high, middle, sums, places, canvas, grad, probe_sum, packed, sems, *scratch,
):
    size = probe.shape[1]
    half = size // 2
    side = x_first.shape[1] - 8
    tiles = side // LANES
    inner = slice(half, half + side)
    odd_y, odd_x = odd[0] == 1, odd[1] == 1
    for index, tile in enumerate((0, 1 + tiles)):
        above, below = corner_first[:, index, :half, :], corner_second[:, index, :half, :]
        canvas[:, tile, :half, :] = jnp.where(odd_y, below, above)
        canvas[:, tile, half + side :, :] = jnp.where(odd_y, above, below)
    run_slots(
        lambda row, col: jnp.logical_not(row | col),
        position, count, probe, folded, left, right, canvas, grad, probe_sum, *scratch,
    )
    copies = []

    def send(source, target):
        copy = pltpu.make_async_copy(source, target, sems.at[len(copies)])
        copy.start()
        copies.append(copy)

    for plane in range(3):
        for index in range(2):
            packed[:, 2 * plane + index] = probe_sum[plane, index].reshape(size // 8, 8, LANES)
    send(packed, sums)
    for out, odd_start in ((margin_first, half + side), (margin_second, 0)):
        rows = pl.ds(pl.multiple_of(jnp.where(odd_y, odd_start, half + side - odd_start), LANES), half)
        send(grad.at[:, :, rows, :], out)
    send(grad.at[:, 0, inner, :], side_low)
    send(grad.at[:, 1 + tiles, inner, :], side_high)
    send(grad.at[:, 1 : 1 + tiles, inner, :], middle)
    beside, own = slice(half, half + 8), slice(half + 8, half + 16)
    for start, (even_ref, odd_ref) in ((0, (corner_first, corner_second)), (6, (corner_second, corner_first))):
        for index, (tile, rows) in enumerate(((0, beside), (0, own), (1, beside))):
            places[start + index] = jnp.where(odd_y, odd_ref[0, tile, rows, :], even_ref[0, tile, rows, :])
    places[3] = jnp.where(odd_x, x_second[0, side:, :], x_first[0, side:, :])
    places[4] = own_notes(position, count)
    places[5] = jnp.where(odd_x, x_first[0, side:, :], x_second[0, side:, :])
    for copy in copies:
        copy.wait()


def sides_kernel(odd, own_low, own_high, low_first, low_second, high_first, high_second, first, second):
    half = LANES
    side = own_low.shape[1]
    odd_y, odd_x = odd[0] == 1, odd[1] == 1
    for start in range(0, side, half):
        rows = slice(start, start + half)
        values = []
        for own, y_first, y_second in ((own_low, low_first, low_second), (own_high, high_first, high_second)):
            value = own[:, rows, :]
            if start == 0:
                value = value + jnp.where(odd_y, y_second[:, 0], y_first[:, 0])
            if start + half == side:
                value = value + jnp.where(odd_y, y_first[:, 0], y_second[:, 0])
            values.append(value)
        first[:, rows, :] = jnp.where(odd_x, values[1], values[0])
        second[:, rows, :] = jnp.where(odd_x, values[0], values[1])


def weight_kernel(numbers, probe, scale, power, weight):
    half = LANES
    side = scale.shape[1]
    tiles = side // LANES
    weight[...] = jnp.zeros_like(weight)
    for index in range(2):
        columns = slice(index * LANES, (index + 1) * LANES)
        power[index] = probe[0, :, columns] * probe[0, :, columns] + probe[1, :, columns] * probe[1, :, columns]
    for index in range(9):
        down, across = index // 3 - 1, index % 3 - 1

        def step(slot, carry):
            row = numbers[index, 0, slot].astype(jnp.int32) + (2 * half + down * side)
            col = numbers[index, 1, slot].astype(jnp.int32) + (2 * half + across * side)
            reach = side + 2 * half

            @pl.when((row > 0) & (row < reach) & (col > 0) & (col < reach))
            def add():
                at, tile, offset = place(row, col, tiles + 1)
                add_window(weight, at, tile, offset, power[0], power[1])

            return carry

        lax.fori_loop(0, numbers[index, 2, 0].astype(jnp.int32), step, 0)
    for index in range(tiles):
        scale[index] = 1.0 / (weight[2 + index, 2 * half : 2 * half + side, :] + 1.0)


def update_kernel(odd, tile_ref, grad, y_first, y_second, scale, out):
    half = LANES
    side = tile_ref.shape[1]
    odd_y = odd[0] == 1
    for plane in range(2):
        for start in range(0, side, half):
            rows = slice(start, start + half)
            value = grad[plane, 0, rows, :]
            if start == 0:
                value = value + jnp.where(odd_y, y_second[plane, 0], y_first[plane, 0])
            if start + half == side:
                value = value + jnp.where(odd_y, y_first[plane, 0], y_second[plane, 0])
            out[plane, rows, :] = tile_ref[plane, rows, :] - value * scale[0, rows, :]


def column_kernel(odd, before, x_first, x_second, scale, out):
    use_first = odd[1] == pl.program_id(0)
    for plane in range(2):
        out[plane] = before[plane] - jnp.where(use_first, x_first[plane], x_second[plane]) * scale[0]


def plane_kernel(parts, after, out):
    out[...] = jnp.broadcast_to(jnp.sum(parts[...], axis=0)[None], out.shape)


def probe_kernel(index, parts, probe, out):
    total = jnp.sum(parts[...], axis=0)
    rows = pl.ds(pl.multiple_of(index[0] * 8, 8), 8)
    for tile in range(2):
        root = jnp.sqrt(total[4 + tile] + 1.0)
        for plane in range(2):
            new = probe[plane, rows, tile * LANES : (tile + 1) * LANES] - total[2 * plane + tile] / root
            out[:, 2 * plane + tile] = jnp.broadcast_to(new[None], (out.shape[0], 8, LANES))


def join_kernel(pieces, out):
    for plane in range(2):
        for tile in range(2):
            value = pieces[:, 2 * plane + tile]
            out[plane, :, tile * LANES : (tile + 1) * LANES] = value.reshape(out.shape[1], LANES)


def swap(first, second, axis):
    count = lax.axis_size(axis)
    across = [pair for low in range(1, count - 1, 2) for pair in ((low, low + 1), (low + 1, low))]
    return lax.ppermute(first, axis, across), lax.ppermute(second, axis, [(index, index ^ 1) for index in range(count)])


def keep(value):
    return pltpu.with_memory_space_constraint(value, pltpu.HBM)


def params(mib):
    return pltpu.CompilerParams(vmem_limit_bytes=mib * 2**20)


def cost(mib):
    return pl.CostEstimate(flops=0, bytes_accessed=mib * 2**20, transcendentals=0)


def solution(mesh):
    rows, cols = mesh.shape["ty"], mesh.shape["tx"]
    near_y, near_z = 8, 4
    planes = [
        [(8 * high + row) * cols + near_z * x + low for row in range(near_y) for x in range(cols // near_z)]
        for high in range(rows // near_y)
        for low in range(near_z)
    ]
    lines = [list(line) for line in zip(*planes)]

    def trade(pieces, groups):
        return lax.all_to_all(pieces, ("ty", "tx"), 0, 0, axis_index_groups=groups, tiled=True)

    def per_device(object_field, probe, intensity, positions, counts):
        side = object_field.shape[1]
        size = probe.shape[1]
        half = size // 2
        slots = intensity.shape[2]
        tiles = side // LANES
        position = positions[:, 0, 0, :]
        count = counts[0]
        row, col = lax.axis_index("ty"), lax.axis_index("tx")
        piece = jnp.bitwise_and(row, near_y - 1) * (cols // near_z) + lax.shift_right_logical(col, 2)
        piece = piece.reshape(1).astype(jnp.int32)
        left, right = (jnp.asarray(table) for table in half_tables(size))
        gather_left, gather_right = (jnp.asarray(table) for table in parity_tables(size))

        odd = jnp.bitwise_and(jnp.stack([row, col]), 1).astype(jnp.int32)

        strip = jax.ShapeDtypeStruct((2, side + 8, LANES), F32)
        edge = jax.ShapeDtypeStruct((2, half, side), F32)
        x_first, x_second, y_first, y_second = pl.pallas_call(
            edge_kernel,
            out_shape=(strip, strip, edge, edge),
            in_specs=[SMEM] * 3 + [VMEM],
            out_specs=(VMEM,) * 4,
            compiler_params=params(6),
            cost_estimate=cost(4),
            name="edges",
        )(odd, position, count, object_field)
        x_first, x_second = swap(x_first, x_second, "tx")
        y_first, y_second = swap(y_first, y_second, "ty")
        folded = pl.pallas_call(
            fold_kernel,
            out_shape=jax.ShapeDtypeStruct((slots, size, size), F32),
            in_specs=[SMEM, VMEM, VMEM, VMEM],
            out_specs=VMEM,
            scratch_shapes=[pltpu.VMEM((size, 3 * size), BF16)],
            compiler_params=params(8),
            cost_estimate=cost(6),
            name="fold",
        )(count, intensity[0, 0], gather_left, gather_right)
        members = len(planes[0])
        lanes = 2
        scratch = [
            pltpu.SMEM((slots,), jnp.int32),
            pltpu.VMEM((lanes, 2, 2, size, LANES), F32),
            pltpu.VMEM((lanes, 2, 3 * size, size), BF16),
            pltpu.VMEM((lanes, 2, size, 3 * size), BF16),
        ]
        state = (
            pltpu.VMEM((2, tiles + 2, side + size, LANES), F32),
            pltpu.VMEM((2, tiles + 2, side + size, LANES), F32),
            pltpu.VMEM((3, 2, size, LANES), F32),
        )
        given = (odd, position, count, probe, folded, left, right)
        canvas, grad, probe_sum, token = pl.pallas_call(
            core_kernel,
            out_shape=state + (jax.ShapeDtypeStruct((8, LANES), F32),),
            in_specs=[SMEM] * 3 + [VMEM] * 5,
            out_specs=(VMEM,) * 4,
            scratch_shapes=scratch,
            compiler_params=params(26),
            cost_estimate=cost(16),
            name="core_slots",
        )(*given, object_field)
        corner = jax.ShapeDtypeStruct((2, 2, half + 16, LANES), F32)
        corners = pl.pallas_call(
            corner_kernel,
            out_shape=(corner, corner),
            in_specs=[SMEM] * 3 + [VMEM] * 2 + [HBM],
            out_specs=(VMEM, VMEM),
            compiler_params=params(4),
            cost_estimate=cost(4),
            name="corners",
        )(odd, position, count, x_first, x_second, token)
        corners = swap(*corners, "ty")

        canvas, grad, probe_sum = pl.pallas_call(
            column_slots_kernel,
            out_shape=state,
            in_specs=[SMEM] * 3 + [VMEM] * 9,
            out_specs=(VMEM,) * 3,
            scratch_shapes=scratch,
            input_output_aliases={9: 0, 10: 1, 11: 2},
            compiler_params=params(26),
            cost_estimate=cost(16),
            name="column_slots",
        )(*given, x_first, x_second, canvas, grad, probe_sum)
        canvas, grad, probe_sum = pl.pallas_call(
            row_kernel,
            out_shape=state,
            in_specs=[SMEM] * 3 + [VMEM] * 9,
            out_specs=(VMEM,) * 3,
            scratch_shapes=scratch,
            input_output_aliases={9: 0, 10: 1, 11: 2},
            compiler_params=params(26),
            cost_estimate=cost(8),
            name="row_slots",
        )(*given, y_first, y_second, canvas, grad, probe_sum)
        margin = pltpu.HBM((2, tiles + 2, half, LANES), F32)
        column = pltpu.HBM((2, side, LANES), F32)
        margin_first, margin_second, side_low, side_high, middle, sums, places, *_ = pl.pallas_call(
            outer_kernel,
            out_shape=(
                margin, margin, column, column,
                pltpu.HBM((2, tiles, side, LANES), F32),
                pltpu.HBM((members, 6, 8, LANES), F32),
                jax.ShapeDtypeStruct((9, 8, LANES), F32),
            ) + state,
            in_specs=[SMEM] * 3 + [VMEM] * 11,
            out_specs=(HBM,) * 6 + (VMEM,) * 4,
            scratch_shapes=[pltpu.VMEM((members, 6, 8, LANES), F32), pltpu.SemaphoreType.DMA((6,))] + scratch,
            input_output_aliases={11: 7, 12: 8, 13: 9},
            compiler_params=params(26),
            cost_estimate=cost(16),
            name="outer_slots",
        )(*given, x_first, x_second, *corners, canvas, grad, probe_sum)

        margin_first, margin_second = swap(margin_first, margin_second, "ty")
        scale = pl.pallas_call(
            weight_kernel,
            out_shape=jax.ShapeDtypeStruct((tiles, side, LANES), F32),
            in_specs=[SMEM, VMEM],
            out_specs=VMEM,
            scratch_shapes=[
                pltpu.VMEM((2, size, LANES), F32),
                pltpu.VMEM((tiles + 4, side + 2 * size, LANES), F32),
            ],
            compiler_params=params(8),
            cost_estimate=cost(8),
            name="weights",
        )(places, keep(probe))
        parts = trade(sums, planes)
        strip = pltpu.HBM((2, side, LANES), F32)
        whole = pl.BlockSpec((2, side, LANES), lambda index: (0, 0, 0))
        first_tile = pl.BlockSpec((2, 1, half, LANES), lambda index: (0, 0, 0, 0))
        last_tile = pl.BlockSpec((2, 1, half, LANES), lambda index: (0, tiles + 1, 0, 0))
        margins = pl.pallas_call(
            sides_kernel,
            out_shape=(strip, strip),
            grid=(1,),
            in_specs=[SMEM, whole, whole, first_tile, first_tile, last_tile, last_tile],
            out_specs=(whole, whole),
            compiler_params=params(8),
            cost_estimate=cost(16),
            name="sides",
        )(odd, keep(side_low), keep(side_high), margin_first, margin_second, margin_first, margin_second)
        x_first, x_second = swap(*margins, "tx")

        parts = pl.pallas_call(
            plane_kernel,
            out_shape=pltpu.HBM((len(lines[0]), 6, 8, LANES), F32),
            in_specs=[VMEM, HBM],
            out_specs=VMEM,
            compiler_params=params(6),
            cost_estimate=cost(2),
            name="plane_sum",
        )(parts, scale)
        parts = trade(parts, lines)
        pieces = pl.pallas_call(
            probe_kernel,
            out_shape=pltpu.HBM((members, 4, 8, LANES), F32),
            in_specs=[SMEM, VMEM, VMEM],
            out_specs=VMEM,
            compiler_params=params(6),
            cost_estimate=cost(2),
            name="probe_rows",
        )(piece, parts, keep(probe))
        probe_new = pl.pallas_call(
            join_kernel,
            out_shape=jax.ShapeDtypeStruct(probe.shape, F32),
            in_specs=[VMEM],
            out_specs=VMEM,
            compiler_params=params(6),
            cost_estimate=cost(2),
            name="join",
        )(trade(pieces, planes))

        column = pl.BlockSpec((2, side, LANES), lambda index: (0, 0, index))
        flat = pl.BlockSpec((2, 1, half, LANES), lambda index: (0, index + 1, 0, 0))
        object_new = pl.pallas_call(
            update_kernel,
            out_shape=jax.ShapeDtypeStruct(object_field.shape, F32),
            grid=(tiles,),
            in_specs=[
                SMEM, column, pl.BlockSpec((2, 1, side, LANES), lambda index: (0, index, 0, 0)), flat, flat,
                pl.BlockSpec((1, side, LANES), lambda index: (index, 0, 0)),
            ],
            out_specs=column,
            compiler_params=params(8),
            cost_estimate=cost(8),
            name="update",
        )(odd, keep(object_field), keep(middle), margin_first, margin_second, scale)
        ends = pl.BlockSpec((2, side, LANES), lambda index: (0, 0, index * (tiles - 1)))
        object_new = pl.pallas_call(
            column_kernel,
            out_shape=jax.ShapeDtypeStruct(object_field.shape, F32),
            grid=(2,),
            in_specs=[SMEM, ends, whole, whole, pl.BlockSpec((1, side, LANES), lambda index: (index * (tiles - 1), 0, 0))],
            out_specs=ends,
            input_output_aliases={1: 0},
            compiler_params=params(8),
            name="columns",
        )(odd, object_new, x_first, x_second, scale)
        return (object_new, probe_new)

    in_specs = (
        P(None, "ty", "tx"),
        P(),
        P("ty", "tx", None, None, None),
        P(None, "ty", "tx", None),
        P("ty", "tx"),
    )
    out_specs = (P(None, "ty", "tx"), P())
    return jax.shard_map(per_device, mesh=mesh, in_specs=in_specs, out_specs=out_specs, check_vma=False)
```
